32 devices in a mesh: ctx: 16 (over z, y, core), tp: 2 (over x).
Axes of the slice: x: 2, y: 2, z: 4, core: 2. Of those that a mesh axis runs over, the one named last changes fastest.
Arguments:
- hidden_in: bfloat16 [2048, 1024], P('ctx'), may hold values from -6 to 6
- cotangent: bfloat16 [2048, 1024], P('ctx'), may hold values from -6 to 6
- gain_attn: float32 [1024], replicated, may hold values from 0.5 to 1.5
- gain_mlp: float32 [1024], replicated, may hold values from 0.5 to 1.5
- w_qkv: bfloat16 [1024, 3, 1024], P(None, None, 'tp'), may hold values from -0.25 to 0.25
- w_attn_out: bfloat16 [1024, 1024], P('tp'), may hold values from -1 to 1
- w_in: bfloat16 [1024, 2, 2624], P(None, None, 'tp'), may hold values from -0.1875 to 0.1875
- w_mlp_out: bfloat16 [2624, 1024], P('tp'), may hold values from -0.125 to 0.125
Outputs:
- output: bfloat16 [2048, 1024], P('ctx')
- grad_input: float32 [2048, 1024], P('ctx')
- grad_gain_attn: float32 [1024], P('ctx')
- grad_gain_mlp: float32 [1024], P('ctx')
- grad_w_qkv: float32 [1024, 3, 1024], P('ctx', None, 'tp')
- grad_w_attn_out: float32 [1024, 1024], P('tp', 'ctx')
- grad_w_in: float32 [1024, 2, 2624], P('ctx', None, 'tp')
- grad_w_mlp_out: float32 [2624, 1024], P('tp', 'ctx')
The draws below stay inside these ranges and needn't reach their ends.
All inputs are finite; a program needn't handle non-finite values.
Results may differ from the reference program's by a relative error of at most 0.023.
The reference program's roundings to bfloat16 on the way count: a program that leaves them out, or rounds other values in their place, can miss the bound.
Values may be sent and summed in bfloat16 or wider, within the bound.
No kernel may reach another device: no remote copies, remote signals or barrier semaphores. Data moves between devices by JAX's collectives and lax.ppermute only.
A program may use at most 192 MiB of HBM per device.

```python
import math
import jax
import jax.numpy as jnp
from jax import lax

D = 1024
H = 16
HD = 64
FF = 2624
TOKENS = 2048


def spiked(entries, own_key, source, target, shards_of, factor):
    def block_of(axis_at):
        return (jnp.arange(entries.shape[axis_at]) // (entries.shape[axis_at] // shards_of)).reshape((-1,) + (1,) * (entries.ndim - 1 - axis_at))

    first = jax.random.permutation(own_key, shards_of)[block_of(target)]
    far = (block_of(target) + shards_of // 2) % shards_of
    return jnp.where((block_of(source) == first) | (block_of(source) == far), factor * entries, entries)


def steps_of(stream_key, shape, shards, low, high):
    def one(axis_at, blocks):
        steps = jax.random.uniform(jax.random.fold_in(jax.random.fold_in(stream_key, 6), axis_at), (blocks,), jnp.float32, low / len(shards), high / len(shards))
        return jnp.repeat(jnp.exp(steps), shape[axis_at] // blocks).reshape((-1,) + (1,) * (len(shape) - axis_at - 1))

    loudness = one(*shards[0])
    for cut in shards[1:]:
        loudness = loudness * one(*cut)
    return loudness


def normal_values(key, extent, scale, limit, shards=(), kind=jnp.bfloat16):
    factor_of = steps_of(key, extent, shards, -0.22, 0.18) if shards else 1.0
    values = jax.random.normal(key, extent, jnp.float32) * scale * factor_of
    return jnp.minimum(jnp.maximum(values, -limit), limit).astype(kind)


def heavy_noise(own_key, extent, scale, bound, split, heavy, kind=jnp.bfloat16):
    drawn = scale * jax.random.normal(own_key, extent, jnp.float32)
    if split:
        drawn = drawn * steps_of(own_key, extent, split, -0.22, 0.18)
    return jnp.clip(spiked(drawn, jax.random.fold_in(own_key, 3), *heavy), -bound, bound).astype(kind)


def setup_inputs(seed: int = 0) -> dict:
    arg_keys = jax.random.split(jax.random.key(seed), 9)
    hidden_in = normal_values(arg_keys[0], (TOKENS, D), 1.0, 6.0, ((0, 16),))
    cotangent = heavy_noise(arg_keys[1], (TOKENS, D), 1.0, 6.0, ((0, 16),), (0, 1, 16, 2.0))
    gain_attn = jnp.clip(1.0 + 0.1 * jax.random.normal(arg_keys[2], (D,), jnp.float32), 0.5, 1.5)
    gain_mlp = jnp.clip(1.0 + 0.1 * jax.random.normal(arg_keys[3], (D,), jnp.float32), 0.5, 1.5)
    w_qkv = normal_values(arg_keys[4], (D, 3, H * HD), (D // 2) ** -0.5, 0.25, ((2, 2),))
    w_attn_out = normal_values(arg_keys[5], (H * HD, D), (H * HD // 32) ** -0.5, 1.0, ((0, 2),))
    w_in = normal_values(arg_keys[6], (D, 2, FF), D ** -0.5, 0.1875, ((2, 2),))
    w_mlp_out = normal_values(arg_keys[7], (FF, D), FF ** -0.5, 0.125, ((0, 2),))
    return dict(hidden_in=hidden_in, cotangent=cotangent, gain_attn=gain_attn, gain_mlp=gain_mlp, w_qkv=w_qkv, w_attn_out=w_attn_out, w_in=w_in, w_mlp_out=w_mlp_out)


ROPE_BASE = 160000.0
NORM_EPS = 1e-05

@jax.custom_vjp
def low(v):
    return lax.optimization_barrier(v.astype(jnp.bfloat16)).astype(jnp.float32)

@jax.custom_vjp
def low_back(v):
    return v

def low_keep(v):
    return (low(v), None)

def low_pass(kept, grad):
    return (grad,)

def back_keep(v):
    return (v, None)

def back_low(kept, grad):
    return (low(grad),)
low.defvjp(low_keep, low_pass)
low_back.defvjp(back_keep, back_low)

def layer_norm(values, norm_gain):
    centred = values - lax.optimization_barrier(jnp.mean(values, axis=-1, keepdims=True))
    spread = lax.optimization_barrier(jnp.mean(centred * centred, axis=-1, keepdims=True))
    return centred * lax.rsqrt(spread + NORM_EPS) * norm_gain

def rope_tables(positions, head_width):
    inverse = ROPE_BASE ** (-(jnp.arange(head_width // 2).astype(jnp.float32) * 2.0) / head_width)
    angles = positions[:, None] * inverse[None, :]
    angles = jnp.concatenate([angles, angles], axis=-1)[:, None, :]
    return (jnp.cos(angles), jnp.sin(angles))

def rotate(values, cosine, sine_table):
    half_width = values.shape[-1] // 2
    turned = jnp.concatenate([-values[..., half_width:], values[..., :half_width]], axis=-1)
    return values * cosine + turned * sine_table

def gated_gelu(projected):
    return jax.nn.gelu(projected[:, 0], approximate=False) * projected[:, 1]

def attend(queries, key_rows, value_rows):
    highest = lax.Precision.HIGHEST
    block_size = math.gcd(TOKENS, 512)
    score_scale = HD ** (-0.5)

    def one_block(query_block):
        scores = low_back(jnp.einsum('qhe,khe->qhk', query_block, key_rows, precision=highest) * score_scale)
        shifted = scores - lax.optimization_barrier(jnp.max(scores, axis=-1, keepdims=True))
        exponent = jnp.exp(shifted)
        probabilities = exponent / lax.optimization_barrier(jnp.sum(exponent, axis=-1, keepdims=True))
        return jnp.einsum('qhk,khe->qhe', low(probabilities), value_rows, precision=highest)
    blocks = queries.reshape(TOKENS // block_size, block_size, H, HD)
    return lax.map(jax.checkpoint(one_block), blocks).reshape(TOKENS, H, HD)

def block_forward(residual_in, gain_attn, gain_mlp, w_qkv, w_attn_out, w_in, w_mlp_out):
    highest = lax.Precision.HIGHEST
    normed_one = low(layer_norm(residual_in, gain_attn))
    projected = low_back(jnp.einsum('td,dcf->tcf', normed_one, w_qkv, precision=highest))
    positions = jnp.arange(TOKENS).astype(jnp.float32)
    cosine, sine_table = rope_tables(positions, HD)
    shaped = projected.reshape(TOKENS, 3, H, HD)
    queries = low(rotate(shaped[:, 0], cosine, sine_table))
    key_rows = low(rotate(shaped[:, 1], cosine, sine_table))
    value_rows = low(shaped[:, 2])
    attended = attend(queries, key_rows, value_rows)
    attn_flat = low(low_back(attended.reshape(TOKENS, H * HD)))
    middle = residual_in + low_back(jnp.dot(attn_flat, w_attn_out, precision=highest))
    normed_two = low(layer_norm(middle, gain_mlp))
    gate_up = low_back(jnp.einsum('td,dcf->tcf', normed_two, w_in, precision=highest))
    activated = low(gated_gelu(gate_up))
    return middle + jnp.dot(activated, w_mlp_out, precision=highest)

def reference(hidden_in, cotangent, gain_attn, gain_mlp, w_qkv, w_attn_out, w_in, w_mlp_out):
    output, pullback = jax.vjp(block_forward, hidden_in.astype(jnp.float32), gain_attn.astype(jnp.float32), gain_mlp.astype(jnp.float32), w_qkv.astype(jnp.float32), w_attn_out.astype(jnp.float32), w_in.astype(jnp.float32), w_mlp_out.astype(jnp.float32))
    gradient = pullback(cotangent.astype(jnp.float32))
    return (output.astype(jnp.bfloat16), gradient[0], gradient[1], gradient[2], gradient[3], gradient[4], gradient[5], gradient[6])
```

```python
import functools

import jax
import jax.numpy as jnp
from jax import lax
from jax.experimental import pallas as pl
from jax.experimental.pallas import tpu as pltpu
from jax.sharding import PartitionSpec as P

HD = 64
HALF = HD // 2
ROPE_BASE = 160000.0
NORM_EPS = 1e-05
BF = jnp.bfloat16
F32 = jnp.float32
VMEM_LIMIT = 60 * 1024 * 1024


def dot(a, b, dims):
    return lax.dot_general(a, b, (dims, ((), ())), preferred_element_type=F32)


def nn(a, b):
    return dot(a, b, ((1,), (0,)))


def nt(a, b):
    return dot(a, b, ((1,), (1,)))


def key_loop(count, body):
    if count <= 2:
        for j in range(count):
            body(j)
    else:
        pl.loop(0, count)(body)


def load_rows(parts, row, out_ref):
    for j, (ref, first) in enumerate(parts):
        blocks, width = ref.shape[0], ref.shape[2]
        for b in range(blocks):
            out_ref[j, b * width : (b + 1) * width, :] = ref[b, first + row : first + row + HD, :].T


def load_columns(parts, row, out_ref):
    for j, (ref, first) in enumerate(parts):
        blocks, width = ref.shape[0], ref.shape[2]
        for b in range(blocks):
            out_ref[j, :, b * width : (b + 1) * width] = ref[b, first + row : first + row + HD, :]


def attend_kernel(part_count, own_ref, *refs):
    others = refs[: part_count - 1]
    out_ref, low_ref, lse_ref, k_scr, vt_scr, s_scr = refs[part_count - 1 :]
    blocks, width = own_ref.shape[0], own_ref.shape[2]
    parts = [(own_ref, HD)] + [(r, 0) for r in others]
    load_rows(parts, 0, k_scr)
    load_columns(parts, HD, vt_scr)
    pair = s_scr.shape[2] // width

    @pl.loop(0, blocks // pair)
    def query_block(i):
        qt = jnp.concatenate([own_ref[pair * i + b, :HD, :] for b in range(pair)], axis=1)

        def score(j, top):
            s = nn(k_scr[j], qt)
            s_scr[j] = s
            return jnp.maximum(top, jnp.max(s, axis=0, keepdims=True))

        top = jnp.full((1, pair * width), -jnp.inf, F32)
        top = lax.fori_loop(0, part_count, score, top, unroll=part_count <= 2)

        def weigh(j, carry):
            total, acc = carry
            p = jnp.exp(s_scr[j] - top)
            return total + jnp.sum(p, axis=0, keepdims=True), acc + nn(vt_scr[j], p.astype(BF))

        start = (jnp.zeros((1, pair * width), F32), jnp.zeros((HD, pair * width), F32))
        total, acc = lax.fori_loop(0, part_count, weigh, start, unroll=part_count <= 2)
        attended = acc / total
        lse = top + jnp.log(total)
        for b in range(pair):
            cut = slice(b * width, (b + 1) * width)
            out_ref[pair * i + b] = attended[:, cut]
            low_ref[pair * i + b] = attended[:, cut].astype(BF)
            lse_ref[pair * i + b] = lse[:, cut]


def attend(own, others):
    blocks, unused, width = own.shape
    part_count = 1 + len(others)
    keys = blocks * width
    pair = 2 if blocks % 2 == 0 else 1
    flops = 4 * keys * keys * part_count * HD
    return pl.pallas_call(
        functools.partial(attend_kernel, part_count),
        out_shape=(
            jax.ShapeDtypeStruct((blocks, HD, width), F32),
            jax.ShapeDtypeStruct((blocks, HD, width), BF),
            jax.ShapeDtypeStruct((blocks, 1, width), F32),
        ),
        scratch_shapes=[
            pltpu.VMEM((part_count, keys, HD), BF),
            pltpu.VMEM((part_count, HD, keys), BF),
            pltpu.VMEM((part_count, keys, pair * width), F32),
        ],
        compiler_params=pltpu.CompilerParams(vmem_limit_bytes=VMEM_LIMIT),
        cost_estimate=pl.CostEstimate(
            flops=flops, bytes_accessed=4 * own.size, transcendentals=keys * keys * part_count
        ),
        name="attend",
    )(own, *others)


def attend_back_kernel(part_count, own_ref, *refs):
    others = refs[: part_count - 1]
    (
        grad_ref,
        out_ref,
        lse_ref,
        dq_ref,
        dkv_ref,
        k_scr,
        v_scr,
        kt_scr,
        dk_scr,
        dv_scr,
    ) = refs[part_count - 1 :]
    blocks, width = own_ref.shape[0], own_ref.shape[2]
    parts = [(own_ref, HD)] + [(r, 0) for r in others]
    load_rows(parts, 0, k_scr)
    load_rows(parts, HD, v_scr)
    load_columns(parts, 0, kt_scr)
    dk_scr[...] = jnp.zeros_like(dk_scr)
    dv_scr[...] = jnp.zeros_like(dv_scr)
    pair = 2 if blocks % 2 == 0 else 1

    @pl.loop(0, blocks // pair)
    def query_block(i):
        span = range(pair)
        qt = jnp.concatenate([own_ref[pair * i + b, :HD, :] for b in span], axis=1)
        gt = jnp.concatenate([grad_ref[pair * i + b] for b in span], axis=1)
        ot = jnp.concatenate([out_ref[pair * i + b] for b in span], axis=1)
        lse = jnp.concatenate([lse_ref[pair * i + b] for b in span], axis=1)
        q, g = qt.T, gt.T
        delta = jnp.sum(gt.astype(F32) * ot, axis=0, keepdims=True)

        def one(j, dq):
            p = jnp.exp(nn(k_scr[j], qt) - lse)
            ds = (p * (nn(v_scr[j], gt) - delta)).astype(BF)
            dv_scr[j] += nn(p.astype(BF), g)
            dk_scr[j] += nn(ds, q)
            return dq + nn(kt_scr[j], ds)

        start = jnp.zeros((HD, pair * width), F32)
        dq = lax.fori_loop(0, part_count, one, start, unroll=part_count <= 2)
        for b in span:
            dq_ref[pair * i + b] = dq[:, b * width : (b + 1) * width] * (HD**-0.5)

    def finish(j):
        for b in range(blocks):
            rows = slice(b * width, (b + 1) * width)
            dkv_ref[j, b, :HD, :] = dk_scr[j, rows, :].T
            dkv_ref[j, b, HD:, :] = dv_scr[j, rows, :].T

    key_loop(part_count, finish)


def attend_back(own, others, grad, attended, lse):
    blocks, unused, width = own.shape
    part_count = 1 + len(others)
    keys = blocks * width
    flops = 10 * keys * keys * part_count * HD
    return pl.pallas_call(
        functools.partial(attend_back_kernel, part_count),
        out_shape=(
            jax.ShapeDtypeStruct((blocks, HD, width), F32),
            jax.ShapeDtypeStruct((part_count, blocks, 2 * HD, width), F32),
        ),
        scratch_shapes=[
            pltpu.VMEM((part_count, keys, HD), BF),
            pltpu.VMEM((part_count, keys, HD), BF),
            pltpu.VMEM((part_count, HD, keys), BF),
            pltpu.VMEM((part_count, keys, HD), F32),
            pltpu.VMEM((part_count, keys, HD), F32),
        ],
        compiler_params=pltpu.CompilerParams(vmem_limit_bytes=VMEM_LIMIT),
        cost_estimate=pl.CostEstimate(
            flops=flops, bytes_accessed=8 * own.size, transcendentals=keys * keys * part_count
        ),
        name="attend_back",
    )(own, *others, grad, attended, lse)


def head_weight_kernel(rows_ref, own_ref, other_ref, out_ref):
    blocks = rows_ref.shape[0]
    total = jnp.zeros((rows_ref.shape[2], own_ref.shape[1]), F32)
    for b in range(blocks):
        total += nt(rows_ref[b, 0], own_ref[b])
        total += nt(rows_ref[b, 1], other_ref[b])
    out_ref[...] = total.astype(BF)


def head_weight(rows, own, other):
    return pl.pallas_call(
        head_weight_kernel,
        out_shape=jax.ShapeDtypeStruct((rows.shape[2], own.shape[1]), BF),
        compiler_params=pltpu.CompilerParams(vmem_limit_bytes=VMEM_LIMIT),
        cost_estimate=pl.CostEstimate(
            flops=2 * rows.size * own.shape[1], bytes_accessed=2 * rows.size, transcendentals=0
        ),
        name="head_weight",
    )(rows, own, other)


def standardise(values):
    centred = values - jnp.mean(values, axis=-1, keepdims=True)
    spread = jnp.mean(centred * centred, axis=-1, keepdims=True)
    scale = lax.rsqrt(spread + NORM_EPS)
    return centred * scale, scale


def standardise_back(gradient, gain, normed, scale):
    y = gradient * gain
    along = jnp.mean(y * normed, axis=-1, keepdims=True)
    return scale * (y - jnp.mean(y, axis=-1, keepdims=True) - normed * along)


def gated_gelu(gate, up):
    return jax.nn.gelu(gate, approximate=False) * up


def layer(ctx_size, tp_size, hidden_in, cotangent, gain_attn, gain_mlp, w_qkv, w_attn_out, w_in, w_mlp_out):
    width = hidden_in.shape[0]
    model = hidden_in.shape[1]
    inner = w_qkv.shape[2]
    heads = inner // HD
    units = w_in.shape[2]
    chips = ctx_size // 2
    copies = chips // heads
    mine = model // ctx_size
    me = lax.axis_index("ctx")
    core = me % 2

    same_core = [[2 * p + k for p in range(chips)] for k in range(2)]
    head_groups = [
        [2 * (heads * g + p) + k for p in range(heads)] for g in range(copies) for k in range(2)
    ]

    def exchange(values):
        return lax.all_to_all(values, "ctx", 0, 0, axis_index_groups=head_groups)

    def swap_core(values):
        return lax.ppermute(values, "ctx", [(c, c ^ 1) for c in range(ctx_size)])

    def shift_keys(values, step):
        ring = 2 * copies
        pairs = []
        for c in range(ctx_size):
            g, p, k = c // (2 * heads), (c // 2) % heads, c % 2
            t = (2 * g + k + step) % ring
            pairs.append((c, 2 * (heads * (t // 2) + p) + t % 2))
        return lax.ppermute(values, "ctx", pairs)

    def add_tp(values):
        low = values.astype(BF)
        if tp_size == 2:
            other = lax.ppermute(low, "tp", [(0, 1), (1, 0)])
            return low.astype(F32) + other.astype(F32)
        return lax.psum(low, "tp").astype(F32)

    def sum_tp(values):
        if tp_size == 2:
            return values + lax.ppermute(values, "tp", [(0, 1), (1, 0)])
        return lax.psum(values, "tp")

    def choose(values_t):
        blocks = values_t.reshape(chips, 2, mine, width)
        keep = lax.dynamic_index_in_dim(blocks, core, 1, keepdims=False)
        give = lax.dynamic_index_in_dim(blocks, 1 - core, 1, keepdims=False)
        return keep.reshape(chips * mine, width), give.reshape(chips * mine, width)

    def scatter(values):
        return lax.psum_scatter(
            values, "ctx", scatter_dimension=0, tiled=True, axis_index_groups=same_core
        )

    residual_in = hidden_in.astype(F32)
    normed_one, scale_one = standardise(residual_in)
    attn_input = (normed_one * gain_attn).astype(BF)
    projected = jnp.einsum("dcf,td->cft", w_qkv, attn_input, preferred_element_type=F32)
    projected = projected.reshape(3, heads, HD, width)
    group_first = (me // (2 * heads)) * (2 * heads)
    block_ids = group_first + 2 * jnp.arange(heads) + core
    inverse = ROPE_BASE ** (-(jnp.arange(HALF).astype(F32) * 2.0) / HD)

    def tables(ids):
        positions = (ids[:, None] * width + jnp.arange(width)[None, :]).astype(F32)
        angles = positions[:, None, :] * inverse[None, :, None]
        return jnp.cos(angles), jnp.sin(angles)

    cos_one, sin_one = tables(me[None])
    cos_all, sin_all = tables(block_ids)

    def rotate(values, cosine, sine):
        first, second = values[:, :HALF], values[:, HALF:]
        return jnp.concatenate(
            [first * cosine - second * sine, second * cosine + first * sine], axis=1
        )

    def rotate_back(values, cosine, sine):
        first, second = values[:, :HALF], values[:, HALF:]
        return jnp.concatenate(
            [first * cosine + second * sine, second * cosine - first * sine], axis=1
        )

    score_scale = HD**-0.5
    queries = rotate(projected[0], cos_one, sin_one).astype(BF) * BF(score_scale)
    keys = rotate(projected[1], cos_one, sin_one).astype(BF)
    packed = jnp.concatenate([queries, keys, projected[2].astype(BF)], axis=1)
    own = exchange(packed)
    others = [shift_keys(own[:, HD:], step) for step in range(1, 2 * copies)]
    attended, attended_low, lse = attend(own, others)
    attn_flat_t = exchange(attended_low).reshape(inner, width)

    if copies == 1:
        keep_in, give_in = choose(attn_input.T)
        both_in = jnp.stack([keep_in, swap_core(give_in)])
        both_in, attn_flat_t = lax.optimization_barrier((both_in, attn_flat_t))
        rows_in = lax.all_gather(both_in, "ctx", axis=0, axis_index_groups=same_core)

    middle = residual_in + add_tp(dot(attn_flat_t, w_attn_out, ((0,), (0,))))
    normed_two, scale_two = standardise(middle)
    mlp_input = (normed_two * gain_mlp).astype(BF)
    gate_up = jnp.einsum("td,dcf->ctf", mlp_input, w_in, preferred_element_type=F32)
    activated, gelu_back = jax.vjp(gated_gelu, gate_up[0], gate_up[1])
    activated_low = activated.astype(BF)
    grad_activated = nt(cotangent, w_mlp_out)
    grad_gate, grad_up = gelu_back(grad_activated)
    grad_gate_up = jnp.stack([grad_gate, grad_up]).astype(BF)
    grad_normed_two = add_tp(
        jnp.einsum("ctf,dcf->td", grad_gate_up, w_in, preferred_element_type=F32)
    )
    output = (middle + add_tp(nn(activated_low, w_mlp_out))).astype(BF)

    keep_mlp, give_mlp = choose(mlp_input.T)
    rows_mlp = jnp.concatenate([keep_mlp, swap_core(give_mlp)], axis=1)
    columns_mlp = jnp.concatenate([grad_gate_up, swap_core(grad_gate_up)], axis=1)
    part_in = jnp.einsum("dt,ctf->dcf", rows_mlp, columns_mlp, preferred_element_type=F32)
    keep_cot, give_cot = choose(cotangent.T)
    rows_cot = jnp.concatenate([keep_cot, swap_core(give_cot)], axis=1)
    columns_cot = jnp.concatenate([activated_low, swap_core(activated_low)], axis=0)
    part_mlp = nn(rows_cot, columns_cot)
    grad_w_in = scatter(part_in.astype(BF).reshape(chips * mine, 2 * units)).astype(F32)
    grad_w_mlp_out = scatter(part_mlp.astype(BF)).astype(F32).T

    grad_middle = cotangent.astype(F32) + standardise_back(
        grad_normed_two, gain_mlp, normed_two, scale_two
    )
    grad_middle_low = grad_middle.astype(BF)
    grad_heads = nt(w_attn_out, grad_middle_low).astype(BF).reshape(heads, HD, width)
    grad_received = exchange(grad_heads)

    keep_out, give_out = choose(grad_middle_low.T)
    rows_out = jnp.concatenate([keep_out, swap_core(give_out)], axis=1)
    columns_out = jnp.concatenate([attn_flat_t, swap_core(attn_flat_t)], axis=1)
    part_out = nt(rows_out, columns_out)
    grad_w_attn_out = scatter(part_out.astype(BF)).astype(F32).T

    grad_q, grad_kv = attend_back(own, others, grad_received, attended, lse)
    total_kv = grad_kv[0]
    for step in range(1, 2 * copies):
        total_kv = total_kv + shift_keys(grad_kv[step], -step)
    grad_own = jnp.concatenate(
        [
            rotate_back(grad_q, cos_all, sin_all),
            rotate_back(total_kv[:, :HD], cos_all, sin_all),
            total_kv[:, HD:],
        ],
        axis=1,
    ).astype(BF)
    grad_back = exchange(grad_own).reshape(heads, 3, HD, width)
    grad_back = grad_back.transpose(1, 0, 2, 3).reshape(3, inner, width)
    grad_normed_one = add_tp(
        jnp.einsum("cft,dcf->td", grad_back, w_qkv, preferred_element_type=F32)
    )
    if copies == 1:
        part_qkv = head_weight(rows_in, grad_own, swap_core(grad_own))
        blocks_qkv = exchange(part_qkv.reshape(chips, mine, 3 * HD))
        blocks_qkv = blocks_qkv.reshape(heads, mine, 3, HD).astype(F32)
        grad_w_qkv = blocks_qkv.transpose(1, 2, 0, 3).reshape(mine, 3, inner)
    else:
        keep_in, give_in = choose(attn_input.T)
        rows_in = jnp.concatenate([keep_in, swap_core(give_in)], axis=1)
        columns_in = jnp.concatenate([grad_back, swap_core(grad_back)], axis=2)
        part_qkv = jnp.einsum("dt,cft->dcf", rows_in, columns_in, preferred_element_type=F32)
        grad_w_qkv = scatter(part_qkv.astype(BF).reshape(chips * mine, 3 * inner))
        grad_w_qkv = grad_w_qkv.astype(F32).reshape(mine, 3, inner)
    grad_input = grad_middle + standardise_back(grad_normed_one, gain_attn, normed_one, scale_one)

    first = me * mine
    rows_w_qkv = lax.dynamic_slice_in_dim(w_qkv, first, mine, 0).astype(F32)
    rows_w_in = lax.dynamic_slice_in_dim(w_in, first, mine, 0).astype(F32)
    grad_w_in = grad_w_in.reshape(mine, 2, units)
    grad_gains = sum_tp(
        jnp.stack(
            [
                jnp.sum(rows_w_qkv * grad_w_qkv, axis=(1, 2)),
                jnp.sum(rows_w_in * grad_w_in, axis=(1, 2)),
            ]
        )
    )
    grad_gain_attn = grad_gains[0] / lax.dynamic_slice_in_dim(gain_attn, first, mine, 0)
    grad_gain_mlp = grad_gains[1] / lax.dynamic_slice_in_dim(gain_mlp, first, mine, 0)
    return (
        output,
        grad_input,
        grad_gain_attn,
        grad_gain_mlp,
        grad_w_qkv,
        grad_w_attn_out,
        grad_w_in,
        grad_w_mlp_out,
    )


def solution(mesh):
    in_specs = (
        P("ctx", None),
        P("ctx", None),
        P(),
        P(),
        P(None, None, "tp"),
        P("tp", None),
        P(None, None, "tp"),
        P("tp", None),
    )
    out_specs = (
        P("ctx", None),
        P("ctx", None),
        P("ctx"),
        P("ctx"),
        P("ctx", None, "tp"),
        P("tp", "ctx"),
        P("ctx", None, "tp"),
        P("tp", "ctx"),
    )
    body = functools.partial(layer, mesh.shape["ctx"], mesh.shape["tp"])
    return jax.shard_map(body, mesh=mesh, in_specs=in_specs, out_specs=out_specs, check_vma=False)
```

```python
import functools
import math

import jax
import jax.numpy as jnp
from jax import lax
from jax.experimental import pallas as pl
from jax.experimental.pallas import tpu as pltpu
from jax.sharding import PartitionSpec as P

HD = 64
HALF = HD // 2
ROPE_BASE = 160000.0
NORM_EPS = 1e-05
BF = jnp.bfloat16
F32 = jnp.float32
VMEM_LIMIT = 60 * 1024 * 1024
MIDDLE_LIMIT = 32 * 1024 * 1024


def dot(a, b, dims):
    return lax.dot_general(a, b, (dims, ((), ())), preferred_element_type=F32)


def nn(a, b):
    return dot(a, b, ((1,), (0,)))


def nt(a, b):
    return dot(a, b, ((1,), (1,)))


def load_rows(parts, row, out_ref):
    for j, (ref, first) in enumerate(parts):
        blocks, width = ref.shape[0], ref.shape[2]
        for b in range(blocks):
            out_ref[j, b * width : (b + 1) * width, :] = ref[b, first + row : first + row + HD, :].T


def load_columns(parts, row, out_ref):
    for j, (ref, first) in enumerate(parts):
        blocks, width = ref.shape[0], ref.shape[2]
        for b in range(blocks):
            out_ref[j, :, b * width : (b + 1) * width] = ref[b, first + row : first + row + HD, :]


def attend_kernel(part_count, own_ref, *refs):
    others = refs[: part_count - 1]
    out_ref, low_ref, lse_ref, k_scr, vt_scr, s_scr = refs[part_count - 1 :]
    blocks, width = own_ref.shape[0], own_ref.shape[2]
    parts = [(r, HD) for r in (own_ref, *others)]
    load_rows(parts, 0, k_scr)
    load_columns(parts, HD, vt_scr)
    pair = s_scr.shape[2] // width

    @pl.loop(0, blocks // pair)
    def query_block(i):
        qt = jnp.concatenate([own_ref[pair * i + b, :HD, :] for b in range(pair)], axis=1)

        def score(j, top):
            s = nn(k_scr[j], qt)
            s_scr[j] = s
            return jnp.maximum(top, jnp.max(s, axis=0, keepdims=True))

        top = jnp.full((1, pair * width), -jnp.inf, F32)
        top = lax.fori_loop(0, part_count, score, top, unroll=part_count <= 2)

        def weigh(j, carry):
            total, acc = carry
            p = jnp.exp(s_scr[j] - top)
            return total + jnp.sum(p, axis=0, keepdims=True), acc + nn(vt_scr[j], p.astype(BF))

        start = (jnp.zeros((1, pair * width), F32), jnp.zeros((HD, pair * width), F32))
        total, acc = lax.fori_loop(0, part_count, weigh, start, unroll=part_count <= 2)
        attended = acc / total
        lse = top + jnp.log(total)
        for b in range(pair):
            cut = slice(b * width, (b + 1) * width)
            out_ref[pair * i + b] = attended[:, cut]
            low_ref[pair * i + b] = attended[:, cut].astype(BF)
            lse_ref[pair * i + b] = lse[:, cut]


def attend(own, others):
    blocks, unused, width = own.shape
    part_count = 1 + len(others)
    keys = blocks * width
    pair = 2 if blocks % 2 == 0 else 1
    flops = 4 * keys * keys * part_count * HD
    return pl.pallas_call(
        functools.partial(attend_kernel, part_count),
        out_shape=(
            jax.ShapeDtypeStruct((blocks, HD, width), F32),
            jax.ShapeDtypeStruct((blocks, HD, width), BF),
            jax.ShapeDtypeStruct((blocks, 1, width), F32),
        ),
        scratch_shapes=[
            pltpu.VMEM((part_count, keys, HD), BF),
            pltpu.VMEM((part_count, HD, keys), BF),
            pltpu.VMEM((part_count, keys, pair * width), F32),
        ],
        compiler_params=pltpu.CompilerParams(vmem_limit_bytes=VMEM_LIMIT),
        cost_estimate=pl.CostEstimate(
            flops=flops, bytes_accessed=4 * own.size, transcendentals=keys * keys * part_count
        ),
        name="attend",
    )(own, *others)


def turn_back(values, cosine, sine):
    first, second = values[:HALF], values[HALF:]
    return jnp.concatenate([first * cosine + second * sine, second * cosine - first * sine], axis=0)


def attend_back_kernel(part_count, own_ref, *refs):
    others = refs[: part_count - 1]
    refs = refs[part_count - 1 :]
    grad_ref, out_ref, lse_ref, cos_ref, sin_ref = refs[:5]
    dq_ref, dkv_ref = refs[5:7]
    dkv_others = refs[7 : 6 + part_count]
    k_scr, v_scr, kt_scr, dk_scr, dv_scr = refs[6 + part_count :]
    blocks, width = own_ref.shape[0], own_ref.shape[2]
    parts = [(r, HD) for r in (own_ref, *others)]
    load_rows(parts, 0, k_scr)
    load_rows(parts, HD, v_scr)
    load_columns(parts, 0, kt_scr)
    dk_scr[...] = jnp.zeros_like(dk_scr)
    dv_scr[...] = jnp.zeros_like(dv_scr)
    pair = 2 if blocks % 2 == 0 else 1

    @pl.loop(0, blocks // pair)
    def query_block(i):
        span = range(pair)
        qt = jnp.concatenate([own_ref[pair * i + b, :HD, :] for b in span], axis=1)
        gt = jnp.concatenate(
            [
                (grad_ref[0, pair * i + b].astype(F32) + grad_ref[1, pair * i + b].astype(F32)).astype(BF)
                for b in span
            ],
            axis=1,
        )
        ot = jnp.concatenate([out_ref[pair * i + b] for b in span], axis=1)
        lse = jnp.concatenate([lse_ref[pair * i + b] for b in span], axis=1)
        q, g = qt.T, gt.T
        delta = jnp.sum(gt.astype(F32) * ot, axis=0, keepdims=True)

        def one(j, dq):
            p = jnp.exp(nn(k_scr[j], qt) - lse)
            ds = (p * (nn(v_scr[j], gt) - delta)).astype(BF)
            dv_scr[j] += nn(p.astype(BF), g)
            dk_scr[j] += nn(ds, q)
            return dq + nn(kt_scr[j], ds)

        start = jnp.zeros((HD, pair * width), F32)
        dq = lax.fori_loop(0, part_count, one, start, unroll=part_count <= 2)
        for b in span:
            at = pair * i + b
            block = dq[:, b * width : (b + 1) * width] * (HD**-0.5)
            dq_ref[at] = turn_back(block, cos_ref[at], sin_ref[at]).astype(BF)

    for j, ref in enumerate((dkv_ref, *dkv_others)):
        for b in range(blocks):
            rows = slice(b * width, (b + 1) * width)
            ref[b, :HD, :] = dk_scr[j, rows, :].T
            ref[b, HD:, :] = dv_scr[j, rows, :].T


def attend_back(own, others, grad, attended, lse, cosine, sine):
    blocks, unused, width = own.shape
    part_count = 1 + len(others)
    keys = blocks * width
    flops = 10 * keys * keys * part_count * HD
    terms = jax.ShapeDtypeStruct((blocks, 2 * HD, width), F32)
    return pl.pallas_call(
        functools.partial(attend_back_kernel, part_count),
        out_shape=(jax.ShapeDtypeStruct((blocks, HD, width), BF), *[terms] * part_count),
        scratch_shapes=[
            pltpu.VMEM((part_count, keys, HD), BF),
            pltpu.VMEM((part_count, keys, HD), BF),
            pltpu.VMEM((part_count, HD, keys), BF),
            pltpu.VMEM((part_count, keys, HD), F32),
            pltpu.VMEM((part_count, keys, HD), F32),
        ],
        compiler_params=pltpu.CompilerParams(vmem_limit_bytes=VMEM_LIMIT),
        cost_estimate=pl.CostEstimate(
            flops=flops, bytes_accessed=8 * own.size, transcendentals=keys * keys * part_count
        ),
        name="attend_back",
    )(own, *others, grad, attended, lse, cosine, sine)


def combine_kernel(count, dq_ref, *refs):
    terms, (cos_ref, sin_ref, out_ref) = refs[:count], refs[count:]
    for b in range(dq_ref.shape[0]):
        total = terms[0][b]
        for ref in terms[1:]:
            total = total + ref[b]
        out_ref[b, :HD] = dq_ref[b]
        out_ref[b, HD : 2 * HD] = turn_back(total[:HD], cos_ref[b], sin_ref[b]).astype(BF)
        out_ref[b, 2 * HD :] = total[HD:].astype(BF)


def combine(dq, terms, cosine, sine):
    blocks, unused, width = dq.shape
    return pl.pallas_call(
        functools.partial(combine_kernel, len(terms)),
        out_shape=jax.ShapeDtypeStruct((blocks, 3 * HD, width), BF),
        compiler_params=pltpu.CompilerParams(vmem_limit_bytes=VMEM_LIMIT),
        name="combine",
    )(dq, *terms, cosine, sine)


def standardise(values):
    centred = values - jnp.mean(values, axis=-1, keepdims=True)
    spread = jnp.mean(centred * centred, axis=-1, keepdims=True)
    scale = lax.rsqrt(spread + NORM_EPS)
    return centred * scale, scale


def standardise_back(gradient, gain, normed, scale):
    y = gradient * gain
    along = jnp.mean(y * normed, axis=-1, keepdims=True)
    return scale * (y - jnp.mean(y, axis=-1, keepdims=True) - normed * along)


def project_kernel(hidden_ref, gain_ref, cos_ref, sin_ref, w_ref, packed_ref, input_ref):
    c = pl.program_id(0)
    heads = packed_ref.shape[0]

    @pl.when(c == 0)
    def norm():
        normed, unused = standardise(hidden_ref[...].astype(F32))
        input_ref[...] = (normed * gain_ref[...]).astype(BF)

    rows = nn(input_ref[...], w_ref[0]).T

    @pl.when(c == 2)
    def plain():
        for h in range(heads):
            packed_ref[h, 2 * HD :] = rows[h * HD : (h + 1) * HD].astype(BF)

    @pl.when(c < 2)
    def turned():
        cosine, sine = cos_ref[...], sin_ref[...]
        factor = jnp.where(c == 0, HD**-0.5, 1.0).astype(F32)
        at = pl.multiple_of(c * HD, HD)
        for h in range(heads):
            first, second = rows[h * HD : h * HD + HALF], rows[h * HD + HALF : (h + 1) * HD]
            both = jnp.concatenate(
                [first * cosine - second * sine, second * cosine + first * sine], axis=0
            )
            packed_ref[h, pl.ds(at, HD)] = (both * factor).astype(BF)


def project(hidden, gain, cosine, sine, weights):
    width, model = hidden.shape
    inner = weights.shape[2]
    heads = inner // HD

    def whole(*shape):
        return pl.BlockSpec(shape, lambda c: (0,) * len(shape))

    return pl.pallas_call(
        project_kernel,
        grid=(3,),
        in_specs=[
            whole(width, model),
            whole(1, model),
            whole(HALF, width),
            whole(HALF, width),
            pl.BlockSpec((1, model, inner), lambda c: (c, 0, 0)),
        ],
        out_specs=(whole(heads, 3 * HD, width), whole(width, model)),
        out_shape=(
            jax.ShapeDtypeStruct((heads, 3 * HD, width), BF),
            jax.ShapeDtypeStruct((width, model), BF),
        ),
        compiler_params=pltpu.CompilerParams(vmem_limit_bytes=VMEM_LIMIT),
        name="project",
    )(hidden, gain, cosine, sine, weights)


def middle_kernel(
    tp_ref,
    attn_ref,
    hidden_ref,
    cot_ref,
    gain_ref,
    own_ref,
    other_ref,
    w_in_ref,
    grad_act_ref,
    middle_ref,
    input_ref,
    act_ref,
    grad_ref,
    part_ref,
    heads_ref,
):
    tp = tp_ref[0]
    branch = nn(attn_ref[tp].T, own_ref[...]) + nn(attn_ref[1 - tp].T, other_ref[...])
    middle = hidden_ref[...].astype(F32) + branch
    middle_ref[...] = middle
    normed, scale = standardise(middle)
    gain = gain_ref[...]
    mlp_input = (normed * gain).astype(BF)
    input_ref[...] = mlp_input
    gate, up = nt(mlp_input, w_in_ref[0]), nt(mlp_input, w_in_ref[1])
    share = 0.5 * (1.0 + lax.erf(gate * (0.5**0.5)))
    slope = share + gate * jnp.exp(-0.5 * gate * gate) * ((2.0 * math.pi) ** -0.5)
    bent = gate * share
    grad_act = grad_act_ref[...]
    act_ref[...] = (bent * up).astype(BF)
    grad_gate = (slope * up * grad_act).astype(BF)
    grad_up = (bent * grad_act).astype(BF)
    grad_ref[0] = grad_gate
    grad_ref[1] = grad_up
    part = nn(grad_gate, w_in_ref[0]) + nn(grad_up, w_in_ref[1])
    part_ref[...] = part.astype(BF)
    grad = 0.5 * cot_ref[...].astype(F32) + standardise_back(part, gain, normed, scale)
    grad = grad.astype(BF)
    shape = heads_ref.shape[1:]
    heads_ref[tp] = nt(own_ref[...], grad).astype(BF).reshape(shape)
    heads_ref[1 - tp] = nt(other_ref[...], grad).astype(BF).reshape(shape)


def middle_part(tp, attn, hidden, cotangent, gain, own, other, w_in, grad_act):
    width, model = hidden.shape
    units = w_in.shape[1]
    inner = own.shape[0]
    vmem = pl.BlockSpec(memory_space=pltpu.VMEM)
    return pl.pallas_call(
        middle_kernel,
        in_specs=[pl.BlockSpec(memory_space=pltpu.SMEM)] + [vmem] * 8,
        out_shape=(
            jax.ShapeDtypeStruct((width, model), F32),
            jax.ShapeDtypeStruct((width, model), BF),
            jax.ShapeDtypeStruct((width, units), BF),
            jax.ShapeDtypeStruct((2, width, units), BF),
            jax.ShapeDtypeStruct((width, model), BF),
            jax.ShapeDtypeStruct((2, inner // HD, HD, width), BF),
        ),
        compiler_params=pltpu.CompilerParams(vmem_limit_bytes=MIDDLE_LIMIT),
        cost_estimate=pl.CostEstimate(
            flops=8 * width * model * (units + inner),
            bytes_accessed=2 * w_in.size + 4 * own.size,
            transcendentals=2 * width * units,
        ),
        name="middle_part",
    )(tp, attn, hidden, cotangent, gain, own, other, w_in, grad_act)


def project_back_kernel(grad_ref, w_ref, out_ref):
    heads = grad_ref.shape[0]
    total = jnp.zeros(out_ref.shape, F32)
    for c in range(3):
        rows = jnp.concatenate([grad_ref[h, c * HD : (c + 1) * HD, :] for h in range(heads)], axis=0)
        total += nt(rows.T, w_ref[c])
    out_ref[...] = total.astype(BF)


def project_back(grad, weights):
    width = grad.shape[2]
    return pl.pallas_call(
        project_back_kernel,
        out_shape=jax.ShapeDtypeStruct((width, weights.shape[1]), BF),
        compiler_params=pltpu.CompilerParams(vmem_limit_bytes=MIDDLE_LIMIT),
        cost_estimate=pl.CostEstimate(
            flops=2 * width * weights.size, bytes_accessed=2 * weights.size, transcendentals=0
        ),
        name="project_back",
    )(grad, weights)


def head_weight_kernel(count, ids_ref, own_ref, other_ref, *refs):
    out_ref = refs[count]
    width = own_ref.shape[2]
    total = jnp.zeros((refs[0].shape[0], own_ref.shape[1]), F32)
    whole = count if refs[count - 1].shape == refs[0].shape else count - 2
    for b in range(whole):
        at = ids_ref[b]
        total += nt(refs[b][:, :width], own_ref[at])
        total += nt(refs[b][:, width:], other_ref[at])
    if whole < count:
        at = ids_ref[whole]
        rows = jnp.concatenate([refs[whole][...], refs[whole + 1][...]], axis=0)
        total += nt(rows[:, :width], own_ref[at])
        total += nt(rows[:, width:], other_ref[at])
    out_ref[...] = total.astype(BF)


def head_weight(ids, own, other, rows):
    count = len(rows)
    vmem = pl.BlockSpec(memory_space=pltpu.VMEM)
    return pl.pallas_call(
        functools.partial(head_weight_kernel, count),
        in_specs=[pl.BlockSpec(memory_space=pltpu.SMEM)] + [vmem] * (2 + count),
        out_specs=vmem,
        out_shape=jax.ShapeDtypeStruct((rows[0].shape[0], own.shape[1]), BF),
        compiler_params=pltpu.CompilerParams(vmem_limit_bytes=VMEM_LIMIT),
        cost_estimate=pl.CostEstimate(
            flops=2 * count * rows[0].size * own.shape[1],
            bytes_accessed=2 * count * rows[0].size,
            transcendentals=0,
        ),
        name="head_weight",
    )(ids, own, other, *rows)


def mlp_weight_kernel(rows_in_ref, rows_out_ref, own_ref, other_ref, act_ref, act_other_ref, out_ref):
    chips, unused, mine, units = out_ref.shape
    for c in range(2):
        columns = jnp.concatenate([own_ref[c], other_ref[c]], axis=0)
        out_ref[:, c] = nn(rows_in_ref[...], columns).astype(BF).reshape(chips, mine, units)
    columns = jnp.concatenate([act_ref[...], act_other_ref[...]], axis=0)
    out_ref[:, 2] = nn(rows_out_ref[...], columns).astype(BF).reshape(chips, mine, units)


def mlp_weight(chips, rows_in, rows_out, own, other, act, act_other):
    mine = rows_in.shape[0] // chips
    units = act.shape[1]
    return pl.pallas_call(
        mlp_weight_kernel,
        out_shape=jax.ShapeDtypeStruct((chips, 3, mine, units), BF),
        compiler_params=pltpu.CompilerParams(vmem_limit_bytes=VMEM_LIMIT),
        cost_estimate=pl.CostEstimate(
            flops=6 * rows_in.size * units,
            bytes_accessed=6 * chips * mine * units + 12 * act.size,
            transcendentals=0,
        ),
        name="mlp_weight",
    )(rows_in, rows_out, own, other, act, act_other)


def layer(ctx_size, tp_size, hidden_in, cotangent, gain_attn, gain_mlp, w_qkv, w_attn_out, w_in, w_mlp_out):
    width = hidden_in.shape[0]
    model = hidden_in.shape[1]
    inner = w_qkv.shape[2]
    heads = inner // HD
    units = w_in.shape[2]
    chips = ctx_size // 2
    copies = chips // heads
    mine = model // ctx_size
    me = lax.axis_index("ctx")
    core = me % 2

    same_core = [[2 * p + k for p in range(chips)] for k in range(2)]
    head_groups = [
        [2 * (heads * g + p) + k for p in range(heads)] for g in range(copies) for k in range(2)
    ]

    wide_groups = [
        [(2 * (heads * g + p) + k) * tp_size + t for t in range(tp_size) for p in range(heads)]
        for g in range(copies)
        for k in range(2)
    ]

    def exchange_wide(values):
        return lax.all_to_all(values, ("ctx", "tp"), 0, 0, axis_index_groups=wide_groups)

    def exchange(values):
        return lax.all_to_all(values, "ctx", 0, 0, axis_index_groups=head_groups)

    def swap_core(values):
        return lax.ppermute(values, "ctx", [(c, c ^ 1) for c in range(ctx_size)])

    def shift_keys(values, step):
        ring = 2 * copies
        pairs = []
        for c in range(ctx_size):
            g, p, k = c // (2 * heads), (c // 2) % heads, c % 2
            t = (2 * g + k + step) % ring
            pairs.append((c, 2 * (heads * (t // 2) + p) + t % 2))
        return lax.ppermute(values, "ctx", pairs)

    def swap_tp(values):
        return lax.ppermute(values, "tp", [(0, 1), (1, 0)])

    def add_tp(low):
        return low.astype(F32) + swap_tp(low).astype(F32)

    def after(values, *earlier):
        return lax.optimization_barrier((values, earlier))[0]

    def ring_chip(position):
        position = position % chips
        up = 2 * position
        return jnp.where(position < chips // 2, up, 2 * chips - 1 - up)

    ring = [2 * q if q < chips // 2 else 2 * chips - 1 - 2 * q for q in range(chips)]
    place = {p: q for q, p in enumerate(ring)}

    def turn(values, step):
        pairs = [
            (2 * p + k, 2 * ring[(place[p] + step) % chips] + k)
            for p in range(chips)
            for k in range(2)
        ]
        return lax.ppermute(values, "ctx", pairs)

    chip = me // 2
    position = jnp.where(chip % 2 == 0, chip // 2, chips - 1 - chip // 2)
    ringed = copies == 1

    def picker(chip_ids):
        wanted = ((2 * chip_ids + core) * mine)[:, None] + jnp.arange(mine)[None, :]
        return (wanted.reshape(-1, 1) == jnp.arange(model)[None, :]).astype(BF)

    pick_plain = picker(jnp.arange(chips))
    pick_ring = picker(ring_chip(position + jnp.arange(chips))) if ringed else pick_plain

    def rows_of(pick, values):
        both = jnp.concatenate([values, swap_core(values)], axis=0)
        return nt(pick, both).astype(BF)

    class Sum:
        def __init__(self, parts):
            self.parts, self.right, self.left, self.step = parts, None, None, 0

        def advance(self, *earlier):
            self.step += 1
            half = chips // 2
            cut = self.parts.shape[-2] // 2
            right, left = self.parts[half + 1 - self.step], self.parts[half - 1 + self.step]
            if self.step == 1:
                right, left = right[..., :cut, :], left[..., cut:, :]
            elif self.step == 2:
                first = right[..., :cut, :].astype(F32) + self.right.astype(F32)
                right = jnp.concatenate([first.astype(BF), right[..., cut:, :]], axis=-2)
                last = left[..., cut:, :].astype(F32) + self.left.astype(F32)
                left = jnp.concatenate([left[..., :cut, :], last.astype(BF)], axis=-2)
            else:
                right = (right.astype(F32) + self.right.astype(F32)).astype(BF)
                left = (left.astype(F32) + self.left.astype(F32)).astype(BF)
            right, left = after((right, left), *earlier)
            self.right, self.left = turn(right, 1), turn(left, -1)

        def result(self):
            total = self.parts[0].astype(F32) + self.right.astype(F32)
            return total + self.left.astype(F32)

    def scatter(parts):
        flat = parts.reshape(parts.shape[0], -1)
        summed = lax.psum_scatter(
            flat, "ctx", scatter_dimension=0, tiled=True, axis_index_groups=same_core
        )
        return summed.reshape(parts.shape[1:]).astype(F32)

    group_first = (me // (2 * heads)) * (2 * heads)
    block_ids = group_first + 2 * jnp.arange(heads) + core
    inverse = ROPE_BASE ** (-(jnp.arange(HALF).astype(F32) * 2.0) / HD)

    def tables(ids):
        positions = (ids[:, None] * width + jnp.arange(width)[None, :]).astype(F32)
        angles = positions[:, None, :] * inverse[None, :, None]
        return jnp.cos(angles), jnp.sin(angles)

    tp = lax.axis_index("tp")
    tp_list = tp.astype(jnp.int32).reshape(1)
    cos_one, sin_one = tables(me[None])
    w_three = w_qkv.transpose(1, 0, 2)
    w_pair = w_in.transpose(1, 2, 0)

    packed, attn_input = project(hidden_in, gain_attn[None], cos_one[0], sin_one[0], w_three)
    own = exchange(packed)
    w_out_other = swap_tp(after(w_attn_out, packed))
    later_cot = after(cotangent, packed)
    cos_all, sin_all = tables(after(block_ids, packed))
    rows_in = rows_of(pick_plain, after(attn_input, packed))
    rows_cot = rows_of(pick_ring, later_cot)
    grad_activated = nt(later_cot, w_mlp_out)
    own = after(own, rows_in, rows_cot, grad_activated, cos_all, sin_all)
    others = [shift_keys(own, step) for step in range(1, 2 * copies)]

    gathered = [rows_in]
    right = left = rows_in

    def gather_step(step, *earlier):
        nonlocal right, left
        right, left = after((right, left), *earlier)
        if 2 * step == chips:
            cut = right.shape[0] // 2
            right, left = right[:cut], left[cut:]
        right, left = turn(right, 1), turn(left, -1)
        gathered.extend([right, left])

    if ringed:
        gather_step(1, own)
    attended, attended_low, lse = attend(own, others)
    twice = jnp.concatenate([attended_low] * tp_size, axis=0)
    if ringed:
        gather_step(2, twice)
    attn_all = exchange_wide(twice).reshape(tp_size, inner, width)
    if ringed:
        attn_all = after(attn_all, right, left)
        gather_step(3, attn_all)
    middle, mlp_input, activated_low, grad_gate_up, part_two, head_terms = middle_part(
        tp_list,
        attn_all,
        hidden_in,
        cotangent,
        gain_mlp[None],
        w_attn_out,
        w_out_other,
        w_pair,
        grad_activated,
    )
    if ringed:
        gather_step(4, head_terms)
    grad_received = exchange_wide(head_terms.reshape(tp_size * heads, HD, width))

    rows_mlp = rows_of(pick_ring, mlp_input)
    parts_mlp = mlp_weight(
        chips,
        rows_mlp,
        rows_cot,
        grad_gate_up,
        swap_core(grad_gate_up),
        activated_low,
        swap_core(activated_low),
    )
    grad_received = after(grad_received, parts_mlp)
    if ringed:
        sum_mlp = Sum(parts_mlp)
        sum_mlp.advance()
    grad_received = grad_received.reshape(tp_size, heads, HD, width)
    dq, *grad_kv = attend_back(own, others, grad_received, attended, lse, cos_all, sin_all)

    normed_two, scale_two = standardise(middle)
    grad_middle = cotangent.astype(F32) + standardise_back(
        add_tp(part_two), gain_mlp, normed_two, scale_two
    )
    grad_middle_low = grad_middle.astype(BF)
    output = (middle + add_tp(nn(activated_low, w_mlp_out).astype(BF))).astype(BF)
    attn_flat_t = lax.dynamic_index_in_dim(attn_all, tp, 0, keepdims=False)
    rows_out = rows_of(pick_ring, after(grad_middle_low, dq))
    columns_out = jnp.concatenate([attn_flat_t, swap_core(attn_flat_t)], axis=1)
    parts_out = nt(rows_out, columns_out).astype(BF).reshape(chips, mine, inner)

    terms = [grad_kv[0]]
    for step in range(1, 2 * copies):
        terms.append(shift_keys(grad_kv[step], -step))
    if ringed:
        sum_mlp.advance(dq)
    grad_own = combine(dq, terms, cos_all, sin_all)
    grad_back = exchange(grad_own)
    if ringed:
        sum_out = Sum(parts_out)
        sum_out.advance(grad_own)
        steps = [0]
        for step in range(1, chips // 2 + 1):
            steps.extend([-step, step])
        ids = ring_chip(position + jnp.array(steps[:chips])).astype(jnp.int32)
        part_qkv = head_weight(ids, grad_own, swap_core(grad_own), gathered)
        sum_mlp.advance(part_qkv)
        sum_out.advance(part_qkv)
        grad_back = after(grad_back, part_qkv)
    part_one = project_back(grad_back, w_three)
    grad_normed_one = add_tp(part_one)
    if ringed:
        blocks_qkv = exchange(after(part_qkv, part_one).reshape(chips, mine, 3 * HD))
        sum_mlp.advance(part_one)
        sum_out.advance(part_one)
        blocks_qkv = blocks_qkv.reshape(heads, mine, 3, HD).astype(F32)
        grad_w_qkv = blocks_qkv.transpose(1, 2, 0, 3).reshape(mine, 3, inner)
        sum_out.advance(grad_w_qkv)
        grad_mlp, grad_out = sum_mlp.result(), sum_out.result()
    else:
        grad_back = grad_back.reshape(heads, 3, HD, width)
        grad_back = grad_back.transpose(1, 0, 2, 3).reshape(3, inner, width)
        columns_in = jnp.concatenate([grad_back, swap_core(grad_back)], axis=2)
        part_qkv = jnp.einsum("dt,cft->dcf", rows_in, columns_in, preferred_element_type=F32)
        grad_w_qkv = scatter(part_qkv.astype(BF).reshape(chips, mine, 3, inner))
        grad_mlp = scatter(parts_mlp)
        grad_out = scatter(parts_out)
    normed_one, scale_one = standardise(hidden_in.astype(F32))
    grad_input = grad_middle + standardise_back(grad_normed_one, gain_attn, normed_one, scale_one)
    grad_w_in = jnp.stack([grad_mlp[0], grad_mlp[1]], axis=1)
    grad_w_mlp_out = grad_mlp[2].T
    grad_w_attn_out = grad_out.T

    first = me * mine
    rows_w_qkv = lax.dynamic_slice_in_dim(w_qkv, first, mine, 0).astype(F32)
    rows_w_in = lax.dynamic_slice_in_dim(w_in, first, mine, 0).astype(F32)
    gain_terms = jnp.stack(
        [
            jnp.sum(rows_w_qkv * grad_w_qkv, axis=(1, 2)),
            jnp.sum(rows_w_in * grad_w_in, axis=(1, 2)),
        ]
    )
    grad_gains = gain_terms + swap_tp(gain_terms)
    grad_gain_attn = grad_gains[0] / lax.dynamic_slice_in_dim(gain_attn, first, mine, 0)
    grad_gain_mlp = grad_gains[1] / lax.dynamic_slice_in_dim(gain_mlp, first, mine, 0)
    return (
        output,
        grad_input,
        grad_gain_attn,
        grad_gain_mlp,
        grad_w_qkv,
        grad_w_attn_out,
        grad_w_in,
        grad_w_mlp_out,
    )


def solution(mesh):
    in_specs = (
        P("ctx", None),
        P("ctx", None),
        P(),
        P(),
        P(None, None, "tp"),
        P("tp", None),
        P(None, None, "tp"),
        P("tp", None),
    )
    out_specs = (
        P("ctx", None),
        P("ctx", None),
        P("ctx"),
        P("ctx"),
        P("ctx", None, "tp"),
        P("tp", "ctx"),
        P("ctx", None, "tp"),
        P("tp", "ctx"),
    )
    body = functools.partial(layer, mesh.shape["ctx"], mesh.shape["tp"])
    return jax.shard_map(body, mesh=mesh, in_specs=in_specs, out_specs=out_specs, check_vma=False)
```

```python
import functools
import math

import jax
import jax.numpy as jnp
from jax import lax
from jax.experimental import pallas as pl
from jax.experimental.pallas import tpu as pltpu
from jax.sharding import PartitionSpec as P

HD = 64
HALF = HD // 2
ROPE_BASE = 160000.0
NORM_EPS = 1e-05
BF = jnp.bfloat16
F32 = jnp.float32
GRANT = 60 * 1024 * 1024


def dot(a, b, dims):
    return lax.dot_general(a, b, (dims, ((), ())), preferred_element_type=F32)


def nn(a, b):
    return dot(a, b, ((1,), (0,)))


def nt(a, b):
    return dot(a, b, ((1,), (1,)))


def staged(body, ins, outs, name, scratch=(), late=0, scalars=0, cost=None, far=0):
    arrays = ins[scalars:]
    count = len(arrays)

    def kernel(*refs):
        front, refs = refs[:scalars], refs[scalars:]
        given, refs = refs[:count], refs[count:]
        results, refs = refs[: len(outs)], refs[len(outs) :]
        held, sems, rest = refs[:count], refs[count], refs[count + 1 :]
        copies = [pltpu.make_async_copy(g, h, sems.at[i]) for i, (g, h) in enumerate(zip(given, held))]
        for copy in copies:
            copy.start()
        for copy in copies[: count - late]:
            copy.wait()
        body(*front, *held, *results, *rest, *[copy.wait for copy in copies[count - late :]])

    vmem, hbm = pl.BlockSpec(memory_space=pltpu.VMEM), pl.BlockSpec(memory_space=pltpu.HBM)
    specs = [vmem] * (len(outs) - far) + [hbm] * far
    return pl.pallas_call(
        kernel,
        in_specs=[pl.BlockSpec(memory_space=pltpu.SMEM)] * scalars + [hbm] * count,
        out_specs=specs,
        out_shape=outs,
        scratch_shapes=[
            *[pltpu.VMEM(v.shape, v.dtype) for v in arrays],
            pltpu.SemaphoreType.DMA((count,)),
            *scratch,
        ],
        compiler_params=pltpu.CompilerParams(vmem_limit_bytes=GRANT),
        cost_estimate=cost,
        name=name,
    )(*ins)


def work(flops, byte_count, transcendentals=0):
    return pl.CostEstimate(flops=flops, bytes_accessed=byte_count, transcendentals=transcendentals)


def shaped(shape, dtype):
    return jax.ShapeDtypeStruct(shape, dtype)


def load_rows(parts, row, out_ref):
    for j, (ref, first) in enumerate(parts):
        blocks, width = ref.shape[0], ref.shape[2]
        for b in range(blocks):
            out_ref[j, b * width : (b + 1) * width, :] = ref[b, first + row : first + row + HD, :].T


def load_columns(parts, row, out_ref):
    for j, (ref, first) in enumerate(parts):
        blocks, width = ref.shape[0], ref.shape[2]
        for b in range(blocks):
            out_ref[j, :, b * width : (b + 1) * width] = ref[b, first + row : first + row + HD, :]


def attend_kernel(part_count, own_ref, *refs):
    others = refs[: part_count - 1]
    out_ref, low_ref, lse_ref, k_scr, vt_scr, s_scr = refs[part_count - 1 :]
    blocks, width = own_ref.shape[0], own_ref.shape[2]
    parts = [(r, HD) for r in (own_ref, *others)]
    load_rows(parts, 0, k_scr)
    load_columns(parts, HD, vt_scr)
    pair = s_scr.shape[2] // width

    @pl.loop(0, blocks // pair)
    def query_block(i):
        qt = jnp.concatenate([own_ref[pair * i + b, :HD, :] for b in range(pair)], axis=1)

        def score(j, top):
            s = nn(k_scr[j], qt)
            s_scr[j] = s
            return jnp.maximum(top, jnp.max(s, axis=0, keepdims=True))

        top = jnp.full((1, pair * width), -jnp.inf, F32)
        top = lax.fori_loop(0, part_count, score, top, unroll=part_count <= 2)

        def weigh(j, carry):
            total, acc = carry
            p = jnp.exp(s_scr[j] - top)
            return total + jnp.sum(p, axis=0, keepdims=True), acc + nn(vt_scr[j], p.astype(BF))

        start = (jnp.zeros((1, pair * width), F32), jnp.zeros((HD, pair * width), F32))
        total, acc = lax.fori_loop(0, part_count, weigh, start, unroll=part_count <= 2)
        attended = acc / total
        lse = top + jnp.log(total)
        for b in range(pair):
            cut = slice(b * width, (b + 1) * width)
            out_ref[pair * i + b] = attended[:, cut]
            for t in range(low_ref.shape[0]):
                low_ref[t, pair * i + b] = attended[:, cut].astype(BF)
            lse_ref[pair * i + b] = lse[:, cut]


def attend(tp_size, own, others):
    blocks, unused, width = own.shape
    part_count = 1 + len(others)
    keys = blocks * width
    pair = 2 if blocks % 2 == 0 else 1
    flops = 4 * keys * keys * part_count * HD
    return staged(
        functools.partial(attend_kernel, part_count),
        [own, *others],
        [
            shaped((blocks, HD, width), F32),
            shaped((tp_size, blocks, HD, width), BF),
            shaped((blocks, 1, width), F32),
        ],
        "attend",
        [
            pltpu.VMEM((part_count, keys, HD), BF),
            pltpu.VMEM((part_count, HD, keys), BF),
            pltpu.VMEM((part_count, keys, pair * width), F32),
        ],
        cost=work(flops, 4 * own.size, keys * keys * part_count),
    )


def turn_back(values, cosine, sine):
    first, second = values[:HALF], values[HALF:]
    return jnp.concatenate([first * cosine + second * sine, second * cosine - first * sine], axis=0)


def attend_back_kernel(part_count, own_ref, *refs):
    others = refs[: part_count - 1]
    refs = refs[part_count - 1 :]
    grad_ref, out_ref, lse_ref, cos_ref, sin_ref = refs[:5]
    dq_ref, dkv_ref = refs[5:7]
    dkv_others = refs[7 : 6 + part_count]
    k_scr, v_scr, kt_scr, dk_scr, dv_scr = refs[6 + part_count :]
    blocks, width = own_ref.shape[0], own_ref.shape[2]
    parts = [(r, HD) for r in (own_ref, *others)]
    load_rows(parts, 0, k_scr)
    load_rows(parts, HD, v_scr)
    load_columns(parts, 0, kt_scr)
    dk_scr[...] = jnp.zeros_like(dk_scr)
    dv_scr[...] = jnp.zeros_like(dv_scr)
    pair = 2 if blocks % 2 == 0 else 1

    @pl.loop(0, blocks // pair)
    def query_block(i):
        span = range(pair)
        qt = jnp.concatenate([own_ref[pair * i + b, :HD, :] for b in span], axis=1)
        gt = jnp.concatenate(
            [
                (grad_ref[0, pair * i + b].astype(F32) + grad_ref[1, pair * i + b].astype(F32)).astype(BF)
                for b in span
            ],
            axis=1,
        )
        ot = jnp.concatenate([out_ref[pair * i + b] for b in span], axis=1)
        lse = jnp.concatenate([lse_ref[pair * i + b] for b in span], axis=1)
        q, g = qt.T, gt.T
        delta = jnp.sum(gt.astype(F32) * ot, axis=0, keepdims=True)

        def one(j, dq):
            p = jnp.exp(nn(k_scr[j], qt) - lse)
            ds = (p * (nn(v_scr[j], gt) - delta)).astype(BF)
            dv_scr[j] += nn(p.astype(BF), g)
            dk_scr[j] += nn(ds, q)
            return dq + nn(kt_scr[j], ds)

        start = jnp.zeros((HD, pair * width), F32)
        dq = lax.fori_loop(0, part_count, one, start, unroll=part_count <= 2)
        for b in span:
            at = pair * i + b
            block = dq[:, b * width : (b + 1) * width] * (HD**-0.5)
            dq_ref[at] = turn_back(block, cos_ref[at], sin_ref[at]).astype(BF)

    for j, ref in enumerate((dkv_ref, *dkv_others)):
        for b in range(blocks):
            rows = slice(b * width, (b + 1) * width)
            ref[b, :HD, :] = dk_scr[j, rows, :].T
            ref[b, HD:, :] = dv_scr[j, rows, :].T


def attend_back(own, others, grad, attended, lse, cosine, sine):
    blocks, unused, width = own.shape
    part_count = 1 + len(others)
    keys = blocks * width
    flops = 10 * keys * keys * part_count * HD
    return staged(
        functools.partial(attend_back_kernel, part_count),
        [own, *others, grad, attended, lse, cosine, sine],
        [shaped((blocks, HD, width), BF)] + [shaped((blocks, 2 * HD, width), F32)] * part_count,
        "attend_back",
        [
            pltpu.VMEM((part_count, keys, HD), BF),
            pltpu.VMEM((part_count, keys, HD), BF),
            pltpu.VMEM((part_count, HD, keys), BF),
            pltpu.VMEM((part_count, keys, HD), F32),
            pltpu.VMEM((part_count, keys, HD), F32),
        ],
        cost=work(flops, 8 * own.size, keys * keys * part_count),
    )


def combine_kernel(count, dq_ref, *refs):
    terms, (cos_ref, sin_ref, out_ref) = refs[:count], refs[count:]
    for b in range(dq_ref.shape[0]):
        total = terms[0][b]
        for ref in terms[1:]:
            total = total + ref[b]
        out_ref[b, :HD] = dq_ref[b]
        out_ref[b, HD : 2 * HD] = turn_back(total[:HD], cos_ref[b], sin_ref[b]).astype(BF)
        out_ref[b, 2 * HD :] = total[HD:].astype(BF)


def combine(dq, terms, cosine, sine):
    blocks, unused, width = dq.shape
    return staged(
        functools.partial(combine_kernel, len(terms)),
        [dq, *terms, cosine, sine],
        [shaped((blocks, 3 * HD, width), BF)],
        "combine",
        cost=work(dq.size, 20 * dq.size),
    )[0]


def standardise(values):
    centred = values - jnp.mean(values, axis=-1, keepdims=True)
    spread = jnp.mean(centred * centred, axis=-1, keepdims=True)
    scale = lax.rsqrt(spread + NORM_EPS)
    return centred * scale, scale


def standardise_back(gradient, gain, normed, scale):
    y = gradient * gain
    along = jnp.mean(y * normed, axis=-1, keepdims=True)
    return scale * (y - jnp.mean(y, axis=-1, keepdims=True) - normed * along)


def project_kernel(hidden_ref, gain_ref, cos_ref, sin_ref, *refs):
    weights, (packed_ref, input_ref), waits = refs[:3], refs[3:5], refs[5:]
    normed, unused = standardise(hidden_ref[...].astype(F32))
    attn_input = (normed * gain_ref[...]).astype(BF)
    input_ref[...] = attn_input
    cosine, sine = cos_ref[...], sin_ref[...]
    for c in range(3):
        waits[c]()
        rows = nn(attn_input, weights[c][0]).T
        for h in range(packed_ref.shape[0]):
            block = rows[h * HD : (h + 1) * HD]
            if c < 2:
                first, second = block[:HALF], block[HALF:]
                block = jnp.concatenate(
                    [first * cosine - second * sine, second * cosine + first * sine], axis=0
                )
            if c == 0:
                block = block * (HD**-0.5)
            packed_ref[h, c * HD : (c + 1) * HD] = block.astype(BF)


def project(hidden, gain, cosine, sine, weights):
    width, model = hidden.shape
    heads = weights.shape[2] // HD
    hbm, vmem = pl.BlockSpec(memory_space=pltpu.HBM), pl.BlockSpec(memory_space=pltpu.VMEM)

    def kernel(h_ref, g_ref, c_ref, s_ref, w_ref, packed_ref, input_ref, h_scr, w_scr, sems):
        copies = [pltpu.make_async_copy(h_ref, h_scr, sems.at[3])]
        copies += [pltpu.make_async_copy(w_ref.at[c], w_scr.at[c], sems.at[c]) for c in range(3)]
        for copy in copies:
            copy.start()
        copies[0].wait()
        blocks = [w_scr.at[pl.ds(c, 1)] for c in range(3)]
        waits = [copy.wait for copy in copies[1:]]
        project_kernel(h_scr, g_ref, c_ref, s_ref, *blocks, packed_ref, input_ref, *waits)

    return pl.pallas_call(
        kernel,
        in_specs=[hbm, vmem, vmem, vmem, hbm],
        out_specs=(vmem, vmem),
        out_shape=(shaped((heads, 3 * HD, width), BF), shaped((width, model), BF)),
        scratch_shapes=[
            pltpu.VMEM(hidden.shape, BF),
            pltpu.VMEM(weights.shape, BF),
            pltpu.SemaphoreType.DMA((4,)),
        ],
        compiler_params=pltpu.CompilerParams(vmem_limit_bytes=GRANT),
        name="project",
    )(hidden, gain, cosine, sine, weights)


def unit_back_kernel(cot_ref, w_ref, out_ref):
    out_ref[...] = nt(cot_ref[...], w_ref[...])


def unit_back(cotangent, weights):
    width, units = cotangent.shape[0], weights.shape[0]
    return staged(
        unit_back_kernel,
        [cotangent, weights],
        [shaped((width, units), F32)],
        "unit_back",
        cost=work(2 * width * weights.size, 2 * weights.size),
    )[0]


def middle_kernel(
    tp_ref,
    attn_ref,
    hidden_ref,
    cot_ref,
    gain_ref,
    own_ref,
    other_ref,
    grad_act_ref,
    w_in_ref,
    middle_ref,
    input_ref,
    gated_ref,
    act_ref,
    part_ref,
    heads_ref,
    wait_units,
):
    tp = tp_ref[0]
    branch = nn(attn_ref[tp].T, own_ref[...]) + nn(attn_ref[1 - tp].T, other_ref[...])
    middle = hidden_ref[...].astype(F32) + branch
    middle_ref[...] = middle
    normed, scale = standardise(middle)
    gain = gain_ref[...]
    mlp_input = (normed * gain).astype(BF)
    input_ref[...] = mlp_input
    wait_units()
    gate, up = nt(mlp_input, w_in_ref[0]), nt(mlp_input, w_in_ref[1])
    share = 0.5 * (1.0 + lax.erf(gate * (0.5**0.5)))
    slope = share + gate * jnp.exp(-0.5 * gate * gate) * ((2.0 * math.pi) ** -0.5)
    bent = gate * share
    grad_act = grad_act_ref[...]
    grad_gate = (slope * up * grad_act).astype(BF)
    grad_up = (bent * grad_act).astype(BF)
    units = grad_gate.shape[1]
    gated_ref[:, :units] = grad_gate
    gated_ref[:, units : 2 * units] = grad_up
    activated = (bent * up).astype(BF)
    gated_ref[:, 2 * units :] = activated
    act_ref[...] = activated
    part = nn(grad_gate, w_in_ref[0]) + nn(grad_up, w_in_ref[1])
    part_ref[...] = part.astype(BF)
    grad = 0.5 * cot_ref[...].astype(F32) + standardise_back(part, gain, normed, scale)
    grad = grad.astype(BF)
    shape = heads_ref.shape[1:]
    heads_ref[tp] = nt(own_ref[...], grad).astype(BF).reshape(shape)
    heads_ref[1 - tp] = nt(other_ref[...], grad).astype(BF).reshape(shape)


def middle_part(tp, attn, hidden, cotangent, gain, own, other, grad_act, w_in):
    width, model = hidden.shape
    units = w_in.shape[1]
    inner = own.shape[0]
    return staged(
        middle_kernel,
        [tp, attn, hidden, cotangent, gain, own, other, grad_act, w_in],
        [
            shaped((width, model), F32),
            shaped((width, model), BF),
            shaped((width, 3 * units), BF),
            shaped((width, units), BF),
            shaped((width, model), BF),
            shaped((2, inner // HD, HD, width), BF),
        ],
        "middle_part",
        late=1,
        scalars=1,
        cost=work(8 * width * model * (units + inner), 2 * w_in.size, 2 * width * units),
    )


def project_back_kernel(grad_ref, w_ref, out_ref):
    heads = grad_ref.shape[0]
    total = jnp.zeros(out_ref.shape, F32)
    for c in range(3):
        rows = jnp.concatenate([grad_ref[h, c * HD : (c + 1) * HD, :] for h in range(heads)], axis=0)
        total += nt(rows.T, w_ref[c])
    out_ref[...] = total.astype(BF)


def project_back(grad, weights):
    width = grad.shape[2]
    return staged(
        project_back_kernel,
        [grad, weights],
        [shaped((width, weights.shape[1]), BF)],
        "project_back",
        cost=work(2 * width * weights.size, 2 * weights.size),
    )[0]


def picked(pick_ref, own_ref, other_ref):
    values = jnp.concatenate([own_ref[...], other_ref[...]], axis=0)
    return nt(pick_ref[...], values).astype(BF)


def pick_kernel(pick_ref, own_ref, other_ref, out_ref):
    out_ref[...] = picked(pick_ref, own_ref, other_ref)


def pick_rows(pick, own, other):
    rows, width = pick.shape[0], own.shape[0]
    return staged(
        pick_kernel,
        [pick, own, other],
        [shaped((rows, 2 * width), BF)],
        "pick_rows",
        cost=work(4 * rows * own.size, 6 * own.size),
    )[0]


def head_weight_kernel(ids_ref, own_ref, other_ref, *refs):
    rows, out_ref = refs[:-1], refs[-1]
    width = own_ref.shape[2]
    total = jnp.zeros((rows[0].shape[0], own_ref.shape[1]), F32)
    for b, ref in enumerate(rows):
        at = ids_ref[b]
        total += nt(ref[:, :width], own_ref[at])
        total += nt(ref[:, width:], other_ref[at])
    out_ref[...] = total.astype(BF)


def head_weight(ids, own, other, rows):
    count = len(rows)
    return staged(
        head_weight_kernel,
        [ids, own, other, *rows],
        [shaped((rows[0].shape[0], own.shape[1]), BF)],
        "head_weight",
        scalars=1,
        cost=work(2 * count * rows[0].size * own.shape[1], 2 * count * rows[0].size),
    )[0]


def mlp_weight_kernel(sizes, pick_ref, *refs):
    given, outs = refs[:6], refs[6 : 6 + len(sizes)]
    total_scr, sems, wait_own, wait_other = refs[6 + len(sizes) :]
    in_own, in_other, cot_own, cot_other, own_ref, other_ref = given
    units = own_ref.shape[1] // 3
    rows_in = picked(pick_ref, in_own, in_other)
    rows_out = picked(pick_ref, cot_own, cot_other)
    wait_own()
    wait_other()
    columns = jnp.concatenate([own_ref[...], other_ref[...]], axis=0)
    total_scr[:, : 2 * units] = nn(rows_in, columns[:, : 2 * units]).astype(BF)
    total_scr[:, 2 * units :] = nn(rows_out, columns[:, 2 * units :]).astype(BF)
    copies, first = [], 0
    for r, ref in enumerate(outs):
        copies.append(pltpu.make_async_copy(total_scr.at[pl.ds(first, sizes[r])], ref, sems.at[r]))
        first += sizes[r]
    for copy in copies:
        copy.start()
    for copy in copies:
        copy.wait()


def mlp_weight(sizes, pick, in_own, in_other, cot_own, cot_other, own, other):
    rows, columns = sum(sizes), own.shape[1]
    return staged(
        functools.partial(mlp_weight_kernel, sizes),
        [pick, in_own, in_other, cot_own, cot_other, own, other],
        [shaped((size, columns), BF) for size in sizes],
        "mlp_weight",
        [pltpu.VMEM((rows, columns), BF), pltpu.SemaphoreType.DMA((len(sizes),))],
        late=2,
        cost=work(4 * rows * own.size, 2 * rows * columns + 8 * own.size),
        far=len(sizes),
    )


def out_weight_kernel(pick_ref, own_ref, other_ref, attn_ref, attn_other_ref, *outs):
    rows = picked(pick_ref, own_ref, other_ref)
    columns = jnp.concatenate([attn_ref[...], attn_other_ref[...]], axis=1)
    total = nt(rows, columns).astype(BF)
    first = 0
    for ref in outs:
        ref[...] = total[first : first + ref.shape[0]]
        first += ref.shape[0]


def out_weight(sizes, pick, own, other, attn, attn_other):
    return staged(
        out_weight_kernel,
        [pick, own, other, attn, attn_other],
        [shaped((size, attn.shape[0]), BF) for size in sizes],
        "out_weight",
        cost=work(4 * sum(sizes) * attn.size, 8 * own.size),
    )


def finish_qkv_kernel(first_ref, blocks_ref, w_ref, out_ref, gain_ref, w_scr, sem):
    mine = out_ref.shape[1]
    rows = pl.ds(pl.multiple_of(first_ref[0], mine), mine)
    copy = pltpu.make_async_copy(w_ref.at[:, rows, :], w_scr, sem)
    copy.start()
    for c in range(3):
        for h in range(blocks_ref.shape[0]):
            cut = slice(h * HD, (h + 1) * HD)
            out_ref[c, :, cut] = blocks_ref[h, :, c * HD : (c + 1) * HD].astype(F32)
    copy.wait()
    total = jnp.zeros((mine, 1), F32)
    for c in range(3):
        total += jnp.sum(out_ref[c] * w_scr[c].astype(F32), axis=1, keepdims=True)
    gain_ref[...] = total


def finish_qkv(first, blocks, weights):
    heads, mine, unused = blocks.shape
    inner = weights.shape[2]
    vmem, hbm = pl.BlockSpec(memory_space=pltpu.VMEM), pl.BlockSpec(memory_space=pltpu.HBM)
    return pl.pallas_call(
        finish_qkv_kernel,
        in_specs=[pl.BlockSpec(memory_space=pltpu.SMEM), vmem, hbm],
        out_specs=(vmem, vmem),
        out_shape=(shaped((3, mine, inner), F32), shaped((mine, 1), F32)),
        scratch_shapes=[pltpu.VMEM((3, mine, inner), BF), pltpu.SemaphoreType.DMA],
        compiler_params=pltpu.CompilerParams(vmem_limit_bytes=GRANT),
        name="finish_qkv",
    )(first, blocks, weights)


def finish_mlp_kernel(own_ref, right_ref, left_ref, w_ref, in_ref, out_ref, gain_ref):
    units = out_ref.shape[1]
    total = own_ref[...].astype(F32) + right_ref[...].astype(F32) + left_ref[...].astype(F32)
    out_ref[...] = total[:, 2 * units :]
    in_ref[:, 0, :] = total[:, :units]
    in_ref[:, 1, :] = total[:, units : 2 * units]
    gain_ref[...] = jnp.sum(total[:, : 2 * units] * w_ref[...].astype(F32), axis=1, keepdims=True)


def finish_mlp(own, right, left, rows):
    mine, units = own.shape[0], own.shape[1] // 3
    return staged(
        finish_mlp_kernel,
        [own, right, left, rows],
        [shaped((mine, 2, units), F32), shaped((mine, units), F32), shaped((mine, 1), F32)],
        "finish_mlp",
        cost=work(8 * own.size, 14 * own.size),
    )


def middle_back_kernel(middle_ref, cot_ref, gain_ref, own_ref, other_ref, out_ref, low_ref):
    normed, scale = standardise(middle_ref[...])
    part = own_ref[...].astype(F32) + other_ref[...].astype(F32)
    grad = cot_ref[...].astype(F32) + standardise_back(part, gain_ref[...], normed, scale)
    out_ref[...] = grad
    low_ref[...] = grad.astype(BF)


def middle_back(middle, cotangent, gain, own, other):
    return staged(
        middle_back_kernel,
        [middle, cotangent, gain, own, other],
        [shaped(middle.shape, F32), shaped(middle.shape, BF)],
        "middle_back",
        cost=work(20 * middle.size, 16 * middle.size),
    )


def input_back_kernel(hidden_ref, gain_ref, own_ref, grad_ref, other_ref, out_ref):
    normed, scale = standardise(hidden_ref[...].astype(F32))
    part = own_ref[...].astype(F32) + other_ref[...].astype(F32)
    out_ref[...] = grad_ref[...] + standardise_back(part, gain_ref[...], normed, scale)


def input_back(hidden, gain, own, grad, other):
    return staged(
        input_back_kernel,
        [hidden, gain, own, grad, other],
        [shaped(grad.shape, F32)],
        "input_back",
        cost=work(20 * grad.size, 14 * grad.size),
    )[0]


def layer(ctx_size, tp_size, hidden_in, cotangent, gain_attn, gain_mlp, w_qkv, w_attn_out, w_in, w_mlp_out):
    width = hidden_in.shape[0]
    model = hidden_in.shape[1]
    inner = w_qkv.shape[2]
    heads = inner // HD
    units = w_in.shape[2]
    chips = ctx_size // 2
    copies = chips // heads
    mine = model // ctx_size
    me = lax.axis_index("ctx")
    core = me % 2

    same_core = [[2 * p + k for p in range(chips)] for k in range(2)]
    head_groups = [
        [2 * (heads * g + p) + k for p in range(heads)] for g in range(copies) for k in range(2)
    ]

    wide_groups = [
        [(2 * (heads * g + p) + k) * tp_size + t for t in range(tp_size) for p in range(heads)]
        for g in range(copies)
        for k in range(2)
    ]

    def exchange_wide(values):
        return lax.all_to_all(values, ("ctx", "tp"), 0, 0, axis_index_groups=wide_groups)

    def exchange(values):
        return lax.all_to_all(values, "ctx", 0, 0, axis_index_groups=head_groups)

    def swap_core(values):
        return lax.ppermute(values, "ctx", [(c, c ^ 1) for c in range(ctx_size)])

    def shift_keys(values, step):
        ring = 2 * copies
        pairs = []
        for c in range(ctx_size):
            g, p, k = c // (2 * heads), (c // 2) % heads, c % 2
            t = (2 * g + k + step) % ring
            pairs.append((c, 2 * (heads * (t // 2) + p) + t % 2))
        return lax.ppermute(values, "ctx", pairs)

    def swap_tp(values):
        return lax.ppermute(values, "tp", [(0, 1), (1, 0)])

    def add_tp(low):
        return low.astype(F32) + swap_tp(low).astype(F32)

    def after(values, *earlier):
        return lax.optimization_barrier((values, earlier))[0]

    def ring_chip(position):
        position = position % chips
        up = 2 * position
        return jnp.where(position < chips // 2, up, 2 * chips - 1 - up)

    ring = [2 * q if q < chips // 2 else 2 * chips - 1 - 2 * q for q in range(chips)]
    place = {p: q for q, p in enumerate(ring)}

    def turn(values, step):
        pairs = [
            (2 * p + k, 2 * ring[(place[p] + step) % chips] + k)
            for p in range(chips)
            for k in range(2)
        ]
        return lax.ppermute(values, "ctx", pairs)

    chip = me // 2
    position = jnp.where(chip % 2 == 0, chip // 2, chips - 1 - chip // 2)
    ringed = copies == 1

    def picker(chip_ids):
        wanted = ((2 * chip_ids + core) * mine)[:, None] + jnp.arange(mine)[None, :]
        return (wanted.reshape(-1, 1) == jnp.arange(model)[None, :]).astype(BF)

    class Sum:
        def __init__(self, blocks):
            half = chips // 2
            self.own, self.step = blocks[0], 0
            self.rights = [blocks[half], *blocks[half - 1 : 0 : -1]]
            self.lefts = [blocks[half + 1], *blocks[half + 2 :]]

        def advance(self, *earlier):
            right, left = self.rights[self.step], self.lefts[self.step]
            if self.step == 1:
                cut = self.right.shape[-2]
                first = right[..., :cut, :].astype(F32) + self.right.astype(F32)
                right = jnp.concatenate([first.astype(BF), right[..., cut:, :]], axis=-2)
                last = left[..., cut:, :].astype(F32) + self.left.astype(F32)
                left = jnp.concatenate([left[..., :cut, :], last.astype(BF)], axis=-2)
            elif self.step > 1:
                right = (right.astype(F32) + self.right.astype(F32)).astype(BF)
                left = (left.astype(F32) + self.left.astype(F32)).astype(BF)
            self.step += 1
            right, left = after((right, left), *earlier)
            self.right, self.left = turn(right, 1), turn(left, -1)
            return right, left

        def result(self):
            total = self.own.astype(F32) + self.right.astype(F32)
            return total + self.left.astype(F32)

    def scatter(parts):
        flat = parts.reshape(chips, -1)
        summed = lax.psum_scatter(
            flat, "ctx", scatter_dimension=0, tiled=True, axis_index_groups=same_core
        )
        return summed.reshape((mine,) + parts.shape[1:]).astype(F32)

    group_first = (me // (2 * heads)) * (2 * heads)
    block_ids = group_first + 2 * jnp.arange(heads) + core
    inverse = ROPE_BASE ** (-(jnp.arange(HALF).astype(F32) * 2.0) / HD)

    def tables(ids):
        positions = (ids[:, None] * width + jnp.arange(width)[None, :]).astype(F32)
        angles = positions[:, None, :] * inverse[None, :, None]
        return jnp.cos(angles), jnp.sin(angles)

    tp = lax.axis_index("tp")
    tp_list = tp.astype(jnp.int32).reshape(1)
    cos_one, sin_one = tables(me[None])
    w_three = w_qkv.transpose(1, 0, 2)
    w_pair = w_in.transpose(1, 2, 0)

    packed, attn_input = project(hidden_in, gain_attn[None], cos_one[0], sin_one[0], w_three)
    own = exchange(packed)
    w_out_other = swap_tp(w_attn_out)
    later_cot = after(cotangent, packed)
    cot_other = swap_core(later_cot)
    later_input = after(attn_input, packed)
    rows_in = pick_rows(
        picker(after(jnp.arange(chips), packed)), later_input, swap_core(later_input)
    )
    gathered = [rows_in]
    right = left = rows_in

    def gather_step(step, *earlier):
        nonlocal right, left
        if 2 * step == chips:
            right = turn(after(right, *earlier), 1)
            gathered.append(right)
            return
        right, left = after((right, left), *earlier)
        right, left = turn(right, 1), turn(left, -1)
        gathered.extend([right, left])

    if ringed:
        gather_step(1)
    cos_all, sin_all = tables(after(block_ids, rows_in))
    grad_activated = unit_back(after(later_cot, rows_in), w_mlp_out)
    order = after(jnp.arange(chips), rows_in)
    pick_ring = picker(ring_chip(position + order) if ringed else order)
    own = after(own, grad_activated, cos_all, sin_all, pick_ring)
    others = [shift_keys(own, step) for step in range(1, 2 * copies)]
    attended, attended_low, lse = attend(tp_size, own, others)
    attn_all = exchange_wide(attended_low.reshape(tp_size * heads, HD, width))
    if ringed:
        gather_step(2, attended_low)
    rows_w_in = lax.dynamic_slice_in_dim(after(w_in, attended_low), me * mine, mine, 0)
    rows_w_in = rows_w_in.reshape(mine, 2 * units)
    attn_all = after(attn_all, rows_w_in).reshape(tp_size, inner, width)
    if ringed:
        gather_step(3, attn_all)
    middle, mlp_input, gated, activated_low, part_two, head_terms = middle_part(
        tp_list,
        attn_all,
        hidden_in,
        cotangent,
        gain_mlp[None],
        w_attn_out,
        w_out_other,
        grad_activated,
        w_pair,
    )
    grad_received = exchange_wide(head_terms.reshape(tp_size * heads, HD, width))

    half = chips // 2
    sizes = [mine] * half + [mine // 2, mine // 2] + [mine] * (half - 1) if ringed else [chips * mine]
    parts_mlp = mlp_weight(
        sizes,
        pick_ring,
        mlp_input,
        swap_core(mlp_input),
        cotangent,
        cot_other,
        gated,
        swap_core(gated),
    )
    grad_received = after(grad_received, parts_mlp)
    if ringed:
        sum_mlp = Sum(parts_mlp)
        sum_mlp.advance()
        gather_step(4, grad_received)
    grad_received = grad_received.reshape(tp_size, heads, HD, width)
    dq, *grad_kv = attend_back(own, others, grad_received, attended, lse, cos_all, sin_all)

    part_two = after(part_two, parts_mlp)
    part_two_other = swap_tp(part_two)
    terms = [grad_kv[0]]
    for step in range(1, 2 * copies):
        terms.append(shift_keys(grad_kv[step], -step))
    if ringed:
        sent = sum_mlp.advance(dq)
        terms[0] = after(terms[0], sent)
    grad_own = combine(dq, terms, cos_all, sin_all)
    grad_back = exchange(grad_own)

    later_two = after(part_two_other, grad_own)
    grad_middle, grad_middle_low = middle_back(middle, cotangent, gain_mlp[None], part_two, later_two)
    attn_flat_t = lax.dynamic_index_in_dim(after(attn_all, grad_own), tp, 0, keepdims=False)
    parts_out = out_weight(
        sizes,
        pick_ring,
        grad_middle_low,
        swap_core(grad_middle_low),
        attn_flat_t,
        swap_core(attn_flat_t),
    )
    if ringed:
        sum_out = Sum(parts_out)
        sum_out.advance()
        steps = [0]
        for step in range(1, chips // 2 + 1):
            steps.extend([-step, step])
        ids = ring_chip(position + jnp.array(steps[:chips])).astype(jnp.int32)
        part_qkv = head_weight(ids, grad_own, swap_core(grad_own), gathered)
        grad_back = after(grad_back, part_qkv)
    part_one = project_back(grad_back, w_three)
    part_one_other = swap_tp(part_one)
    first = me * mine
    if ringed:
        blocks_qkv = exchange(after(part_qkv, part_one).reshape(chips, mine, 3 * HD))
        sent = sum_mlp.advance(part_one)
        sum_out.advance(sent)
        mlp_part = nn(after(activated_low, sent), w_mlp_out).astype(BF)
        output = (middle + add_tp(mlp_part)).astype(BF)
        part_one_other = after(part_one_other, mlp_part)
        grad_input = input_back(hidden_in, gain_attn[None], part_one, grad_middle, part_one_other)
        grad_w_qkv, gain_one = finish_qkv(
            first.astype(jnp.int32).reshape(1), after(blocks_qkv, grad_input), w_three
        )
        sum_out.advance(grad_input)
        sum_mlp.advance(gain_one)
        sum_out.advance(gain_one)
        grad_w_qkv = grad_w_qkv.transpose(1, 0, 2)
        grad_w_attn_out = sum_out.result().T
        grad_w_in, grad_w_mlp_out, gain_two = finish_mlp(
            sum_mlp.own, sum_mlp.right, sum_mlp.left, rows_w_in
        )
    else:
        output = (middle + add_tp(nn(activated_low, w_mlp_out).astype(BF))).astype(BF)
        grad_input = input_back(hidden_in, gain_attn[None], part_one, grad_middle, part_one_other)
        grad_back = grad_back.reshape(heads, 3, HD, width)
        grad_back = grad_back.transpose(1, 0, 2, 3).reshape(3, inner, width)
        columns_in = jnp.concatenate([grad_back, swap_core(grad_back)], axis=2)
        part_qkv = jnp.einsum("dt,cft->dcf", rows_in, columns_in, preferred_element_type=F32)
        grad_w_qkv = scatter(part_qkv.astype(BF))
        grad_mlp = scatter(parts_mlp[0])
        grad_w_in = grad_mlp[:, : 2 * units].reshape(mine, 2, units)
        grad_w_mlp_out = grad_mlp[:, 2 * units :]
        grad_w_attn_out = scatter(parts_out[0]).T
        rows_w_qkv = lax.dynamic_slice_in_dim(w_qkv, first, mine, 0)
        gain_one = jnp.sum(rows_w_qkv.astype(F32) * grad_w_qkv, axis=(1, 2))[:, None]
        gain_two = jnp.sum(rows_w_in.astype(F32) * grad_mlp[:, : 2 * units], axis=1)[:, None]

    def scale_gradient(term, gain):
        term = term[:, 0]
        return (term + swap_tp(term)) / lax.dynamic_slice_in_dim(gain, first, mine, 0)

    return (
        output,
        grad_input,
        scale_gradient(gain_one, gain_attn),
        scale_gradient(gain_two, gain_mlp),
        grad_w_qkv,
        grad_w_attn_out,
        grad_w_in,
        grad_w_mlp_out.T,
    )


def solution(mesh):
    in_specs = (
        P("ctx", None),
        P("ctx", None),
        P(),
        P(),
        P(None, None, "tp"),
        P("tp", None),
        P(None, None, "tp"),
        P("tp", None),
    )
    out_specs = (
        P("ctx", None),
        P("ctx", None),
        P("ctx"),
        P("ctx"),
        P("ctx", None, "tp"),
        P("tp", "ctx"),
        P("ctx", None, "tp"),
        P("tp", "ctx"),
    )
    body = functools.partial(layer, mesh.shape["ctx"], mesh.shape["tp"])
    return jax.shard_map(body, mesh=mesh, in_specs=in_specs, out_specs=out_specs, check_vma=False)
```

```python
import functools
import math

import jax
import jax.numpy as jnp
from jax import lax
from jax.experimental import pallas as pl
from jax.experimental.pallas import tpu as pltpu
from jax.sharding import PartitionSpec as P

HD = 64
HALF = HD // 2
ROPE_BASE = 160000.0
NORM_EPS = 1e-05
BF = jnp.bfloat16
F32 = jnp.float32
GRANT = 60 * 1024 * 1024


def dot(a, b, dims):
    return lax.dot_general(a, b, (dims, ((), ())), preferred_element_type=F32)


def nn(a, b):
    return dot(a, b, ((1,), (0,)))


def nt(a, b):
    return dot(a, b, ((1,), (1,)))


def staged(body, ins, outs, name, scratch=(), late=0, scalars=0, cost=None, far=0):
    arrays = ins[scalars:]
    count = len(arrays)

    def kernel(*refs):
        front, refs = refs[:scalars], refs[scalars:]
        given, refs = refs[:count], refs[count:]
        results, refs = refs[: len(outs)], refs[len(outs) :]
        held, sems, rest = refs[:count], refs[count], refs[count + 1 :]
        copies = [pltpu.make_async_copy(g, h, sems.at[i]) for i, (g, h) in enumerate(zip(given, held))]
        for copy in copies:
            copy.start()
        for copy in copies[: count - late]:
            copy.wait()
        body(*front, *held, *results, *rest, *[copy.wait for copy in copies[count - late :]])

    vmem, hbm = pl.BlockSpec(memory_space=pltpu.VMEM), pl.BlockSpec(memory_space=pltpu.HBM)
    specs = [vmem] * (len(outs) - far) + [hbm] * far
    return pl.pallas_call(
        kernel,
        in_specs=[pl.BlockSpec(memory_space=pltpu.SMEM)] * scalars + [hbm] * count,
        out_specs=specs,
        out_shape=outs,
        scratch_shapes=[
            *[pltpu.VMEM(v.shape, v.dtype) for v in arrays],
            pltpu.SemaphoreType.DMA((count,)),
            *scratch,
        ],
        compiler_params=pltpu.CompilerParams(vmem_limit_bytes=GRANT),
        cost_estimate=cost,
        name=name,
    )(*ins)


def whole_lanes(size):
    return -(-size // 128) * 128


def work(flops, byte_count, transcendentals=0):
    return pl.CostEstimate(flops=flops, bytes_accessed=byte_count, transcendentals=transcendentals)


def shaped(shape, dtype):
    return jax.ShapeDtypeStruct(shape, dtype)


def load_rows(parts, row, out_ref):
    for j, (ref, first) in enumerate(parts):
        blocks, width = ref.shape[0], ref.shape[2]
        for b in range(blocks):
            out_ref[j, b * width : (b + 1) * width, :] = ref[b, first + row : first + row + HD, :].T


def load_columns(parts, row, out_ref):
    for j, (ref, first) in enumerate(parts):
        blocks, width = ref.shape[0], ref.shape[2]
        for b in range(blocks):
            out_ref[j, :, b * width : (b + 1) * width] = ref[b, first + row : first + row + HD, :]


def attend_kernel(part_count, own_ref, *refs):
    others = refs[: part_count - 1]
    out_ref, low_ref, lse_ref, k_scr, vt_scr, s_scr = refs[part_count - 1 :]
    blocks, width = own_ref.shape[0], own_ref.shape[2]
    parts = [(r, HD) for r in (own_ref, *others)]
    load_rows(parts, 0, k_scr)
    load_columns(parts, HD, vt_scr)
    pair = s_scr.shape[2] // width

    @pl.loop(0, blocks // pair)
    def query_block(i):
        qt = jnp.concatenate([own_ref[pair * i + b, :HD, :] for b in range(pair)], axis=1)

        def score(j, top):
            s = nn(k_scr[j], qt)
            s_scr[j] = s
            return jnp.maximum(top, jnp.max(s, axis=0, keepdims=True))

        top = jnp.full((1, pair * width), -jnp.inf, F32)
        top = lax.fori_loop(0, part_count, score, top, unroll=part_count <= 2)

        def weigh(j, carry):
            total, acc = carry
            p = jnp.exp(s_scr[j] - top)
            return total + jnp.sum(p, axis=0, keepdims=True), acc + nn(vt_scr[j], p.astype(BF))

        start = (jnp.zeros((1, pair * width), F32), jnp.zeros((HD, pair * width), F32))
        total, acc = lax.fori_loop(0, part_count, weigh, start, unroll=part_count <= 2)
        attended = acc / total
        lse = top + jnp.log(total)
        for b in range(pair):
            cut = slice(b * width, (b + 1) * width)
            out_ref[pair * i + b] = attended[:, cut]
            for t in range(low_ref.shape[0]):
                low_ref[t, pair * i + b] = attended[:, cut].astype(BF)
            lse_ref[pair * i + b] = lse[:, cut]


def attend(tp_size, own, others):
    blocks, unused, width = own.shape
    part_count = 1 + len(others)
    keys = blocks * width
    pair = 2 if blocks % 2 == 0 else 1
    flops = 4 * keys * keys * part_count * HD
    return staged(
        functools.partial(attend_kernel, part_count),
        [own, *others],
        [
            shaped((blocks, HD, width), F32),
            shaped((tp_size, blocks, HD, width), BF),
            shaped((blocks, 1, width), F32),
        ],
        "attend",
        [
            pltpu.VMEM((part_count, keys, HD), BF),
            pltpu.VMEM((part_count, HD, keys), BF),
            pltpu.VMEM((part_count, keys, pair * width), F32),
        ],
        cost=work(flops, 4 * own.size, keys * keys * part_count),
    )


def turn_back(values, cosine, sine):
    first, second = values[:HALF], values[HALF:]
    return jnp.concatenate([first * cosine + second * sine, second * cosine - first * sine], axis=0)


def attend_back_kernel(part_count, own_ref, *refs):
    others = refs[: part_count - 1]
    refs = refs[part_count - 1 :]
    grad_ref, out_ref, lse_ref, cos_ref, sin_ref = refs[:5]
    dq_ref, dkv_ref = refs[5:7]
    dkv_others = refs[7 : 6 + part_count]
    k_scr, v_scr, kt_scr, dk_scr, dv_scr = refs[6 + part_count :]
    blocks, width = own_ref.shape[0], own_ref.shape[2]
    parts = [(r, HD) for r in (own_ref, *others)]
    load_rows(parts, 0, k_scr)
    load_rows(parts, HD, v_scr)
    load_columns(parts, 0, kt_scr)
    dk_scr[...] = jnp.zeros_like(dk_scr)
    dv_scr[...] = jnp.zeros_like(dv_scr)
    pair = 2 if blocks % 2 == 0 else 1

    @pl.loop(0, blocks // pair)
    def query_block(i):
        span = range(pair)
        qt = jnp.concatenate([own_ref[pair * i + b, :HD, :] for b in span], axis=1)
        gt = jnp.concatenate(
            [
                (grad_ref[0, pair * i + b].astype(F32) + grad_ref[1, pair * i + b].astype(F32)).astype(BF)
                for b in span
            ],
            axis=1,
        )
        ot = jnp.concatenate([out_ref[pair * i + b] for b in span], axis=1)
        lse = jnp.concatenate([lse_ref[pair * i + b] for b in span], axis=1)
        q, g = qt.T, gt.T
        delta = jnp.sum(gt.astype(F32) * ot, axis=0, keepdims=True)

        def one(j, dq):
            p = jnp.exp(nn(k_scr[j], qt) - lse)
            ds = (p * (nn(v_scr[j], gt) - delta)).astype(BF)
            dv_scr[j] += nn(p.astype(BF), g)
            dk_scr[j] += nn(ds, q)
            return dq + nn(kt_scr[j], ds)

        start = jnp.zeros((HD, pair * width), F32)
        dq = lax.fori_loop(0, part_count, one, start, unroll=part_count <= 2)
        for b in span:
            at = pair * i + b
            block = dq[:, b * width : (b + 1) * width] * (HD**-0.5)
            dq_ref[at] = turn_back(block, cos_ref[at], sin_ref[at]).astype(BF)

    for j, ref in enumerate((dkv_ref, *dkv_others)):
        for b in range(blocks):
            rows = slice(b * width, (b + 1) * width)
            ref[b, :HD, :] = dk_scr[j, rows, :].T
            ref[b, HD:, :] = dv_scr[j, rows, :].T


def attend_back(own, others, grad, attended, lse, cosine, sine):
    blocks, unused, width = own.shape
    part_count = 1 + len(others)
    keys = blocks * width
    flops = 10 * keys * keys * part_count * HD
    return staged(
        functools.partial(attend_back_kernel, part_count),
        [own, *others, grad, attended, lse, cosine, sine],
        [shaped((blocks, HD, width), BF)] + [shaped((blocks, 2 * HD, width), F32)] * part_count,
        "attend_back",
        [
            pltpu.VMEM((part_count, keys, HD), BF),
            pltpu.VMEM((part_count, keys, HD), BF),
            pltpu.VMEM((part_count, HD, keys), BF),
            pltpu.VMEM((part_count, keys, HD), F32),
            pltpu.VMEM((part_count, keys, HD), F32),
        ],
        cost=work(flops, 8 * own.size, keys * keys * part_count),
    )


def combine_kernel(count, dq_ref, *refs):
    terms, (cos_ref, sin_ref, out_ref) = refs[:count], refs[count:]
    for b in range(dq_ref.shape[0]):
        total = terms[0][b]
        for ref in terms[1:]:
            total = total + ref[b]
        out_ref[b, :HD] = dq_ref[b]
        out_ref[b, HD : 2 * HD] = turn_back(total[:HD], cos_ref[b], sin_ref[b]).astype(BF)
        out_ref[b, 2 * HD :] = total[HD:].astype(BF)


def combine(dq, terms, cosine, sine):
    blocks, unused, width = dq.shape
    return staged(
        functools.partial(combine_kernel, len(terms)),
        [dq, *terms, cosine, sine],
        [shaped((blocks, 3 * HD, width), BF)],
        "combine",
        cost=work(dq.size, 20 * dq.size),
    )[0]


def standardise(values):
    centred = values - jnp.mean(values, axis=-1, keepdims=True)
    spread = jnp.mean(centred * centred, axis=-1, keepdims=True)
    scale = lax.rsqrt(spread + NORM_EPS)
    return centred * scale, scale


def standardise_back(gradient, gain, normed, scale):
    y = gradient * gain
    along = jnp.mean(y * normed, axis=-1, keepdims=True)
    return scale * (y - jnp.mean(y, axis=-1, keepdims=True) - normed * along)


def project_kernel(hidden_ref, gain_ref, cos_ref, sin_ref, *refs):
    weights, (packed_ref, input_ref), waits = refs[:3], refs[3:5], refs[5:]
    normed, unused = standardise(hidden_ref[...].astype(F32))
    attn_input = (normed * gain_ref[...]).astype(BF)
    input_ref[...] = attn_input
    cosine, sine = cos_ref[...], sin_ref[...]
    for c in range(3):
        waits[c]()
        rows = nn(attn_input, weights[c][0]).T
        for h in range(packed_ref.shape[0]):
            block = rows[h * HD : (h + 1) * HD]
            if c < 2:
                first, second = block[:HALF], block[HALF:]
                block = jnp.concatenate(
                    [first * cosine - second * sine, second * cosine + first * sine], axis=0
                )
            if c == 0:
                block = block * (HD**-0.5)
            packed_ref[h, c * HD : (c + 1) * HD] = block.astype(BF)


def project(hidden, gain, cosine, sine, weights):
    width, model = hidden.shape
    heads = weights.shape[2] // HD
    hbm, vmem = pl.BlockSpec(memory_space=pltpu.HBM), pl.BlockSpec(memory_space=pltpu.VMEM)

    def kernel(h_ref, g_ref, c_ref, s_ref, w_ref, packed_ref, input_ref, h_scr, w_scr, sems):
        copies = [pltpu.make_async_copy(h_ref, h_scr, sems.at[3])]
        copies += [pltpu.make_async_copy(w_ref.at[c], w_scr.at[c], sems.at[c]) for c in range(3)]
        for copy in copies:
            copy.start()
        copies[0].wait()
        blocks = [w_scr.at[pl.ds(c, 1)] for c in range(3)]
        waits = [copy.wait for copy in copies[1:]]
        project_kernel(h_scr, g_ref, c_ref, s_ref, *blocks, packed_ref, input_ref, *waits)

    return pl.pallas_call(
        kernel,
        in_specs=[hbm, vmem, vmem, vmem, hbm],
        out_specs=(vmem, vmem),
        out_shape=(shaped((heads, 3 * HD, width), BF), shaped((width, model), BF)),
        scratch_shapes=[
            pltpu.VMEM(hidden.shape, BF),
            pltpu.VMEM(weights.shape, BF),
            pltpu.SemaphoreType.DMA((4,)),
        ],
        compiler_params=pltpu.CompilerParams(vmem_limit_bytes=GRANT),
        cost_estimate=work(2 * width * weights.size, 2 * weights.size),
        name="project",
    )(hidden, gain, cosine, sine, weights)


def unit_back_kernel(cot_ref, w_ref, out_ref):
    out_ref[...] = nt(cot_ref[...], w_ref[...])


def unit_back(cotangent, weights):
    width, units = cotangent.shape[0], weights.shape[0]
    return staged(
        unit_back_kernel,
        [cotangent, weights],
        [shaped((width, units), F32)],
        "unit_back",
        cost=work(2 * width * weights.size, 2 * weights.size),
    )[0]


def middle_kernel(
    tp_ref,
    attn_ref,
    hidden_ref,
    cot_ref,
    gain_ref,
    own_ref,
    other_ref,
    grad_act_ref,
    w_in_ref,
    middle_ref,
    mid_ref,
    act_ref,
    part_ref,
    heads_ref,
    wait_units,
):
    tp = tp_ref[0]
    attn_own = attn_ref[tp].T
    branch = nn(attn_own, own_ref[...]) + nn(attn_ref[1 - tp].T, other_ref[...])
    middle = hidden_ref[...].astype(F32) + branch
    middle_ref[...] = middle
    normed, scale = standardise(middle)
    gain = gain_ref[...]
    mlp_input = (normed * gain).astype(BF)
    model, inner = mlp_input.shape[1], attn_own.shape[1]
    first = model + inner
    mid_ref[:, :model] = mlp_input
    mid_ref[:, model:first] = attn_own
    wait_units()
    gate, up = nt(mlp_input, w_in_ref[0]), nt(mlp_input, w_in_ref[1])
    share = 0.5 * (1.0 + lax.erf(gate * (0.5**0.5)))
    slope = share + gate * jnp.exp(-0.5 * gate * gate) * ((2.0 * math.pi) ** -0.5)
    bent = gate * share
    grad_act = grad_act_ref[...]
    grad_gate = (slope * up * grad_act).astype(BF)
    grad_up = (bent * grad_act).astype(BF)
    units = grad_gate.shape[1]
    mid_ref[:, first : first + units] = grad_gate
    mid_ref[:, first + units : first + 2 * units] = grad_up
    activated = (bent * up).astype(BF)
    mid_ref[:, first + 2 * units : first + 3 * units] = activated
    act_ref[...] = activated
    last = first + 3 * units
    if last < mid_ref.shape[1]:
        mid_ref[:, last:] = jnp.zeros((activated.shape[0], mid_ref.shape[1] - last), BF)
    part = nn(grad_gate, w_in_ref[0]) + nn(grad_up, w_in_ref[1])
    part_ref[...] = part.astype(BF)
    grad = 0.5 * cot_ref[...].astype(F32) + standardise_back(part, gain, normed, scale)
    grad = grad.astype(BF)
    shape = heads_ref.shape[1:]
    heads_ref[tp] = nt(own_ref[...], grad).astype(BF).reshape(shape)
    heads_ref[1 - tp] = nt(other_ref[...], grad).astype(BF).reshape(shape)


def middle_part(tp, attn, hidden, cotangent, gain, own, other, grad_act, w_in):
    width, model = hidden.shape
    units = w_in.shape[1]
    inner = own.shape[0]
    return staged(
        middle_kernel,
        [tp, attn, hidden, cotangent, gain, own, other, grad_act, w_in],
        [
            shaped((width, model), F32),
            shaped((width, whole_lanes(model + inner + 3 * units)), BF),
            shaped((width, units), BF),
            shaped((width, model), BF),
            shaped((2, inner // HD, HD, width), BF),
        ],
        "middle_part",
        late=1,
        scalars=1,
        cost=work(8 * width * model * (units + inner), 2 * w_in.size, 2 * width * units),
    )


def project_back_kernel(grad_ref, w_ref, out_ref):
    heads = grad_ref.shape[0]
    total = jnp.zeros(out_ref.shape, F32)
    for c in range(3):
        rows = jnp.concatenate([grad_ref[h, c * HD : (c + 1) * HD, :] for h in range(heads)], axis=0)
        total += nt(rows.T, w_ref[c])
    out_ref[...] = total.astype(BF)


def project_back(grad, weights):
    width = grad.shape[2]
    return staged(
        project_back_kernel,
        [grad, weights],
        [shaped((width, weights.shape[1]), BF)],
        "project_back",
        cost=work(2 * width * weights.size, 2 * weights.size),
    )[0]


def picked(pick_ref, own_ref, other_ref):
    values = jnp.concatenate([own_ref[...], other_ref[...]], axis=0)
    return nt(pick_ref[...], values).astype(BF)


def head_weight_kernel(mine, ids_ref, grad_ref, *refs):
    rows, keep_ref, give_ref, total_scr = refs[:-3], *refs[-3:]
    count = len(rows)
    core = ids_ref[count]
    grads = jnp.concatenate([grad_ref[ids_ref[b]] for b in range(count)], axis=1)
    inputs = jnp.concatenate([ref[...] for ref in rows], axis=0)
    total_scr[...] = nn(grads, inputs).T
    for b in range(keep_ref.shape[0]):
        keep = pl.multiple_of((2 * b + core) * mine, mine)
        give = pl.multiple_of((2 * b + 1 - core) * mine, mine)
        keep_ref[b] = total_scr[pl.ds(keep, mine), :].astype(BF)
        give_ref[b] = total_scr[pl.ds(give, mine), :].astype(BF)


def head_weight(chips, ids, grad, rows):
    width, model = rows[0].shape
    columns = grad.shape[1]
    mine = model // (2 * chips)
    return staged(
        functools.partial(head_weight_kernel, mine),
        [ids, grad, *rows],
        [shaped((chips, mine, columns), BF)] * 2,
        "head_weight",
        [pltpu.VMEM((model, columns), F32)],
        scalars=1,
        cost=work(2 * len(rows) * rows[0].size * columns, 2 * len(rows) * rows[0].size),
    )


def mlp_weight_kernel(sizes, inner, units, pick_ref, *refs):
    cot_own, cot_other, own_ref, other_ref = refs[:4]
    outs = refs[4 : 4 + len(sizes)]
    total_scr, sems = refs[4 + len(sizes) :]
    model = cot_own.shape[1]
    first = model + inner
    cot_both = jnp.concatenate([cot_own[...], cot_other[...]], axis=0)
    both = jnp.concatenate([own_ref[...], other_ref[...]], axis=0)
    columns = both[:, first : first + 3 * units]
    copies, start, done, rows = [], 0, 0, total_scr.shape[0]
    for r, ref in enumerate(outs):
        while start + sizes[r] > done:
            cut = slice(done, done + rows // 2)
            in_rows = nt(pick_ref[cut], both[:, :model]).astype(BF)
            cot_rows = nt(pick_ref[cut], cot_both).astype(BF)
            total_scr[cut, : 2 * units] = nn(in_rows, columns[:, : 2 * units]).astype(BF)
            total_scr[cut, 2 * units : 3 * units] = nn(cot_rows, columns[:, 2 * units :]).astype(BF)
            if 3 * units < total_scr.shape[1]:
                rest = total_scr.shape[1] - 3 * units
                total_scr[cut, 3 * units :] = jnp.zeros((rows // 2, rest), BF)
            done += rows // 2
        copies.append(pltpu.make_async_copy(total_scr.at[pl.ds(start, sizes[r])], ref, sems.at[r]))
        copies[-1].start()
        start += sizes[r]
    for copy in copies:
        copy.wait()


def mlp_weight(sizes, inner, units, pick, cot_own, cot_other, own, other):
    rows, columns = sum(sizes), whole_lanes(3 * units)
    return staged(
        functools.partial(mlp_weight_kernel, sizes, inner, units),
        [pick, cot_own, cot_other, own, other],
        [shaped((size, columns), BF) for size in sizes],
        "mlp_weight",
        [pltpu.VMEM((rows, columns), BF), pltpu.SemaphoreType.DMA((len(sizes),))],
        cost=work(4 * rows * own.size, 2 * rows * columns + 8 * own.size),
        far=len(sizes),
    )


def out_weight_kernel(mine, pick_ref, own_ref, other_ref, attn_ref, attn_other_ref, *outs):
    both = jnp.concatenate([own_ref[...], other_ref[...]], axis=0)
    rows = nt(pick_ref[...], both).astype(BF)
    total = nn(rows, jnp.concatenate([attn_ref[...], attn_other_ref[...]], axis=0)).astype(BF)
    for r, ref in enumerate(outs):
        ref[...] = total[r * ref.shape[0] : (r + 1) * ref.shape[0]]


def out_weight(count, inner, pick, own, other, mid, mid_other):
    rows, (width, model) = pick.shape[0], own.shape
    vmem, hbm = pl.BlockSpec(memory_space=pltpu.VMEM), pl.BlockSpec(memory_space=pltpu.HBM)

    def kernel(pick_ref, own_ref, other_ref, mid_ref, mid_other_ref, *refs):
        outs, held, sems = refs[:count], refs[count : count + 5], refs[count + 5]
        columns = pl.ds(model, inner)
        given = [pick_ref, own_ref, other_ref, mid_ref.at[:, columns], mid_other_ref.at[:, columns]]
        copies = [pltpu.make_async_copy(g, h, sems.at[i]) for i, (g, h) in enumerate(zip(given, held))]
        for copy in copies:
            copy.start()
        for copy in copies:
            copy.wait()
        out_weight_kernel(rows // count, *held, *outs)

    return pl.pallas_call(
        kernel,
        in_specs=[hbm] * 5,
        out_specs=[vmem] * count,
        out_shape=[shaped((rows // count, inner), BF)] * count,
        scratch_shapes=[
            pltpu.VMEM(pick.shape, BF),
            pltpu.VMEM(own.shape, BF),
            pltpu.VMEM(own.shape, BF),
            pltpu.VMEM((width, inner), BF),
            pltpu.VMEM((width, inner), BF),
            pltpu.SemaphoreType.DMA((5,)),
        ],
        compiler_params=pltpu.CompilerParams(vmem_limit_bytes=GRANT),
        cost_estimate=work(4 * rows * own.size, 8 * own.size),
        name="out_weight",
    )(pick, own, other, mid, mid_other)


def ring_add_kernel(carried, *refs):
    for side in range(2):
        block, got, narrow = refs[3 * side : 3 * side + 3]
        out = refs[6 + side]
        wide, rows = block.shape[1], got.shape[0]
        total = block[...].astype(F32)
        if rows == block.shape[0]:
            out[:, :wide] = (total + got[:, :wide].astype(F32)).astype(BF)
        elif side == 0:
            out[:rows, :wide] = (total[:rows] + got[...].astype(F32)).astype(BF)
            out[rows:, :wide] = block[rows:, :]
        else:
            out[:rows, :wide] = block[:rows, :]
            out[rows:, :wide] = (total[rows:] + got[...].astype(F32)).astype(BF)
        if carried:
            out[:, wide:] = (narrow[...].astype(F32) + got[:, wide:].astype(F32)).astype(BF)
        else:
            out[:, wide:] = narrow[...]


def ring_add(carried, *arrays):
    rows, columns = arrays[0].shape[0], arrays[0].shape[1] + arrays[2].shape[1]
    return staged(
        functools.partial(ring_add_kernel, carried),
        list(arrays),
        [shaped((rows, columns), BF)] * 2,
        "ring_add",
        cost=work(4 * rows * columns, 12 * rows * columns),
    )


def finish_qkv_kernel(first_ref, blocks_ref, w_ref, out_ref, gain_ref, w_scr, sem):
    mine = out_ref.shape[1]
    rows = pl.ds(pl.multiple_of(first_ref[0], mine), mine)
    copy = pltpu.make_async_copy(w_ref.at[:, rows, :], w_scr, sem)
    copy.start()
    for c in range(3):
        for h in range(blocks_ref.shape[0]):
            cut = slice(h * HD, (h + 1) * HD)
            out_ref[c, :, cut] = blocks_ref[h, :, c * HD : (c + 1) * HD].astype(F32)
    copy.wait()
    total = jnp.zeros((mine, 1), F32)
    for c in range(3):
        total += jnp.sum(out_ref[c] * w_scr[c].astype(F32), axis=1, keepdims=True)
    gain_ref[...] = total


def finish_qkv(first, blocks, weights):
    heads, mine, unused = blocks.shape
    inner = weights.shape[2]
    vmem, hbm = pl.BlockSpec(memory_space=pltpu.VMEM), pl.BlockSpec(memory_space=pltpu.HBM)
    return pl.pallas_call(
        finish_qkv_kernel,
        in_specs=[pl.BlockSpec(memory_space=pltpu.SMEM), vmem, hbm],
        out_specs=(vmem, vmem),
        out_shape=(shaped((3, mine, inner), F32), shaped((mine, 1), F32)),
        scratch_shapes=[pltpu.VMEM((3, mine, inner), BF), pltpu.SemaphoreType.DMA],
        compiler_params=pltpu.CompilerParams(vmem_limit_bytes=GRANT),
        cost_estimate=work(2 * blocks.size, 10 * blocks.size),
        name="finish_qkv",
    )(first, blocks, weights)


def finish_mlp_kernel(own_ref, right_ref, left_ref, w_ref, gain_ref, in_ref, out_ref, gains_ref):
    units = out_ref.shape[1]
    wide = own_ref.shape[1]
    total = own_ref[...].astype(F32) + right_ref[:, :wide].astype(F32) + left_ref[:, :wide].astype(F32)
    out_ref[...] = total[:, 2 * units : 3 * units]
    in_ref[:, 0, :] = total[:, :units]
    in_ref[:, 1, :] = total[:, units : 2 * units]
    term = jnp.sum(total[:, : 2 * units] * w_ref[...].astype(F32), axis=1, keepdims=True)
    mine = term.shape[0]
    gains_ref[0:1] = jnp.broadcast_to(gain_ref[...], (mine, 128)).T[0:1]
    gains_ref[1:2] = jnp.broadcast_to(term, (mine, 128)).T[0:1]


def finish_mlp(units, own, right, left, rows, gain):
    mine = own.shape[0]
    return staged(
        finish_mlp_kernel,
        [own, right, left, rows, gain],
        [shaped((mine, 2, units), F32), shaped((mine, units), F32), shaped((2, mine), F32)],
        "finish_mlp",
        cost=work(8 * own.size, 14 * own.size),
    )


def middle_back_kernel(middle_ref, cot_ref, gain_ref, own_ref, other_ref, out_ref, low_ref):
    normed, scale = standardise(middle_ref[...])
    part = own_ref[...].astype(F32) + other_ref[...].astype(F32)
    grad = cot_ref[...].astype(F32) + standardise_back(part, gain_ref[...], normed, scale)
    out_ref[...] = grad
    low_ref[...] = grad.astype(BF)


def middle_back(middle, cotangent, gain, own, other):
    return staged(
        middle_back_kernel,
        [middle, cotangent, gain, own, other],
        [shaped(middle.shape, F32), shaped(middle.shape, BF)],
        "middle_back",
        cost=work(20 * middle.size, 16 * middle.size),
    )


def input_back_kernel(hidden_ref, gain_ref, own_ref, grad_ref, other_ref, out_ref):
    normed, scale = standardise(hidden_ref[...].astype(F32))
    part = own_ref[...].astype(F32) + other_ref[...].astype(F32)
    out_ref[...] = grad_ref[...] + standardise_back(part, gain_ref[...], normed, scale)


def input_back(hidden, gain, own, grad, other):
    return staged(
        input_back_kernel,
        [hidden, gain, own, grad, other],
        [shaped(grad.shape, F32)],
        "input_back",
        cost=work(20 * grad.size, 14 * grad.size),
    )[0]


def layer(ctx_size, tp_size, hidden_in, cotangent, gain_attn, gain_mlp, w_qkv, w_attn_out, w_in, w_mlp_out):
    width = hidden_in.shape[0]
    model = hidden_in.shape[1]
    inner = w_qkv.shape[2]
    heads = inner // HD
    units = w_in.shape[2]
    chips = ctx_size // 2
    copies = chips // heads
    mine = model // ctx_size
    me = lax.axis_index("ctx")
    core = me % 2

    same_core = [[2 * p + k for p in range(chips)] for k in range(2)]
    head_groups = [
        [2 * (heads * g + p) + k for p in range(heads)] for g in range(copies) for k in range(2)
    ]

    wide_groups = [
        [(2 * (heads * g + p) + k) * tp_size + t for t in range(tp_size) for p in range(heads)]
        for g in range(copies)
        for k in range(2)
    ]

    def exchange_wide(values):
        return lax.all_to_all(values, ("ctx", "tp"), 0, 0, axis_index_groups=wide_groups)

    def exchange(values):
        return lax.all_to_all(values, "ctx", 0, 0, axis_index_groups=head_groups)

    def swap_core(values):
        return lax.ppermute(values, "ctx", [(c, c ^ 1) for c in range(ctx_size)])

    def shift_keys(values, step):
        ring = 2 * copies
        pairs = []
        for c in range(ctx_size):
            g, p, k = c // (2 * heads), (c // 2) % heads, c % 2
            t = (2 * g + k + step) % ring
            pairs.append((c, 2 * (heads * (t // 2) + p) + t % 2))
        return lax.ppermute(values, "ctx", pairs)

    def swap_tp(values):
        return lax.ppermute(values, "tp", [(0, 1), (1, 0)])

    def add_tp(low):
        return low.astype(F32) + swap_tp(low).astype(F32)

    def after(values, *earlier):
        return lax.optimization_barrier((values, earlier))[0]

    def ring_chip(position):
        position = position % chips
        up = 2 * position
        return jnp.where(position < chips // 2, up, 2 * chips - 1 - up)

    ring = [2 * q if q < chips // 2 else 2 * chips - 1 - 2 * q for q in range(chips)]
    place = {p: q for q, p in enumerate(ring)}

    def turn(values, step):
        pairs = [
            (2 * p + k, 2 * ring[(place[p] + step) % chips] + k)
            for p in range(chips)
            for k in range(2)
        ]
        return lax.ppermute(values, "ctx", pairs)

    chip = me // 2
    position = jnp.where(chip % 2 == 0, chip // 2, chips - 1 - chip // 2)
    ringed = copies == 1

    def picker(chip_ids):
        wanted = ((2 * chip_ids + core) * mine)[:, None] + jnp.arange(mine)[None, :]
        return (wanted.reshape(-1, 1) == jnp.arange(model)[None, :]).astype(BF)

    def scatter(parts):
        flat = parts.reshape(chips, -1)
        summed = lax.psum_scatter(
            flat, "ctx", scatter_dimension=0, tiled=True, axis_index_groups=same_core
        )
        return summed.reshape((mine,) + parts.shape[1:]).astype(F32)

    group_first = (me // (2 * heads)) * (2 * heads)
    block_ids = group_first + 2 * jnp.arange(heads) + core
    inverse = ROPE_BASE ** (-(jnp.arange(HALF).astype(F32) * 2.0) / HD)

    def tables(ids):
        positions = (ids[:, None] * width + jnp.arange(width)[None, :]).astype(F32)
        angles = positions[:, None, :] * inverse[None, :, None]
        return jnp.cos(angles), jnp.sin(angles)

    tp = lax.axis_index("tp")
    tp_list = tp.astype(jnp.int32).reshape(1)
    cos_one, sin_one = tables(me[None])
    w_three = w_qkv.transpose(1, 0, 2)
    w_pair = w_in.transpose(1, 2, 0)

    packed, attn_input = project(hidden_in, gain_attn[None], cos_one[0], sin_one[0], w_three)
    own = exchange(packed)
    w_out_other = swap_tp(w_attn_out)
    later_cot = after(cotangent, packed)
    cot_other = swap_core(later_cot)
    cos_all, sin_all = tables(after(block_ids, packed))
    order = after(jnp.arange(chips), packed)
    pick = picker(ring_chip(position + order) if ringed else order)
    gathered = [attn_input]
    right = left = after(attn_input, cos_all, sin_all, pick)

    def gather_step(step, *earlier):
        nonlocal right, left
        if 2 * step == chips:
            right = turn(after(right, *earlier), 1)
            gathered.append(right)
            return
        right, left = after((right, left), *earlier)
        right, left = turn(right, 1), turn(left, -1)
        gathered.extend([right, left])

    if ringed:
        gather_step(1)
    own = after(own, cos_all, sin_all, pick)
    others = [shift_keys(own, step) for step in range(1, 2 * copies)]
    attended, attended_low, lse = attend(tp_size, own, others)
    if ringed:
        attended_low = after(attended_low, right, left)
    attn_all = exchange_wide(attended_low.reshape(tp_size * heads, HD, width))
    grad_activated = unit_back(after(cotangent, attended_low), w_mlp_out)
    if ringed:
        gather_step(2, attended_low)
    rows_w_in = lax.dynamic_slice_in_dim(after(w_in, attended_low), me * mine, mine, 0)
    rows_w_in = rows_w_in.reshape(mine, 2 * units)
    attn_all = after(attn_all, rows_w_in, grad_activated, right, left)
    attn_all = attn_all.reshape(tp_size, inner, width)
    if ringed:
        gather_step(3, attn_all)
    middle, mid, activated_low, part_two, head_terms = middle_part(
        tp_list,
        attn_all,
        hidden_in,
        cotangent,
        gain_mlp[None],
        w_attn_out,
        w_out_other,
        grad_activated,
        w_pair,
    )
    grad_received = exchange_wide(head_terms.reshape(tp_size * heads, HD, width))
    if ringed:
        gather_step(4, head_terms)

    half = chips // 2
    sizes = [mine] * half + [mine // 2, mine // 2] + [mine] * (half - 1) if ringed else [chips * mine]
    mid_other = swap_core(mid)
    parts_mlp = mlp_weight(sizes, inner, units, pick, cotangent, cot_other, mid, mid_other)
    if ringed:
        mlp_rights = parts_mlp[half::-1]
        mlp_lefts = parts_mlp[half + 1 :]
        got_right, got_left = turn(mlp_rights[0], 1), turn(mlp_lefts[0], -1)
    part_two_other = swap_tp(part_two)
    later_two = after(part_two_other, parts_mlp)
    grad_middle, grad_middle_low = middle_back(middle, cotangent, gain_mlp[None], part_two, later_two)
    parts_out = out_weight(
        chips if ringed else 1,
        inner,
        pick,
        grad_middle_low,
        swap_core(grad_middle_low),
        mid,
        mid_other,
    )
    grad_received = after(grad_received, parts_mlp, parts_out, right, left)
    grad_received = grad_received.reshape(tp_size, heads, HD, width)
    dq, *grad_kv = attend_back(own, others, grad_received, attended, lse, cos_all, sin_all)

    if ringed:
        grad_kv = after(grad_kv, got_right, got_left)
    terms = [grad_kv[0]]
    for step in range(1, 2 * copies):
        terms.append(shift_keys(grad_kv[step], -step))
    if ringed:

        def ring_step(step, *earlier):
            nonlocal got_right, got_left
            sent = ring_add(
                step > 1,
                mlp_rights[step],
                after(got_right, *earlier),
                parts_out[half + 1 - step],
                mlp_lefts[step],
                got_left,
                parts_out[half + step],
            )
            got_right, got_left = turn(sent[0], 1), turn(sent[1], -1)
            return sent

        sent = ring_step(1, dq)
        terms[0] = after(terms[0], sent)
    grad_own = combine(dq, terms, cos_all, sin_all)
    grad_back = exchange(grad_own)
    if ringed:
        steps = [0]
        for step in range(1, half + 1):
            steps.extend([-step, step])
        ids = ring_chip(position + jnp.array(steps[:chips]))
        ids = jnp.concatenate([ids, core[None]]).astype(jnp.int32)
        keep_qkv, give_qkv = head_weight(chips, ids, grad_own, gathered)
        given_qkv = swap_core(give_qkv)
        sent = ring_step(2, keep_qkv)
        part_qkv = (keep_qkv.astype(F32) + given_qkv.astype(F32)).astype(BF)
        blocks_qkv = exchange(after(part_qkv, sent))
        mlp_part = nn(after(activated_low, sent), w_mlp_out).astype(BF)
        grad_back = after(grad_back, part_qkv, mlp_part, sent)
    part_one = project_back(grad_back, w_three)
    part_one_other = swap_tp(part_one)
    first = me * mine
    if ringed:
        sent = ring_step(3, part_one_other, blocks_qkv)
        output = (middle + add_tp(after(mlp_part, sent))).astype(BF)
        part_one_other = after(part_one_other, sent)
        grad_input = input_back(hidden_in, gain_attn[None], part_one, grad_middle, part_one_other)
        grad_w_qkv, gain_one = finish_qkv(
            first.astype(jnp.int32).reshape(1), blocks_qkv, w_three
        )
        wide = mlp_rights[0].shape[1]
        last = parts_out[1].astype(F32) + got_right[:, wide:].astype(F32)
        last = turn(last.astype(BF), 1)
        grad_w_in, grad_w_mlp_out, gains = finish_mlp(
            units, parts_mlp[0], got_right, got_left, rows_w_in, gain_one
        )
        grad_out = parts_out[0].astype(F32) + got_left[:, wide:].astype(F32)
        grad_w_attn_out = (grad_out + last.astype(F32)).T
        grad_w_qkv = grad_w_qkv.transpose(1, 0, 2)
    else:
        output = (middle + add_tp(nn(activated_low, w_mlp_out).astype(BF))).astype(BF)
        grad_input = input_back(hidden_in, gain_attn[None], part_one, grad_middle, part_one_other)
        grad_back = grad_back.reshape(heads, 3, HD, width)
        grad_back = grad_back.transpose(1, 0, 2, 3).reshape(3, inner, width)
        columns_in = jnp.concatenate([grad_back, swap_core(grad_back)], axis=2)
        rows_in = jnp.concatenate([attn_input, swap_core(attn_input)], axis=0)
        rows_in = nt(pick, rows_in).astype(BF)
        part_qkv = jnp.einsum("dt,cft->dcf", rows_in, columns_in, preferred_element_type=F32)
        grad_w_qkv = scatter(part_qkv.astype(BF))
        grad_mlp = scatter(parts_mlp[0])
        grad_w_in = grad_mlp[:, : 2 * units].reshape(mine, 2, units)
        grad_w_mlp_out = grad_mlp[:, 2 * units : 3 * units]
        grad_w_attn_out = scatter(parts_out[0]).T
        rows_w_qkv = lax.dynamic_slice_in_dim(w_qkv, first, mine, 0)
        gain_one = jnp.sum(rows_w_qkv.astype(F32) * grad_w_qkv, axis=(1, 2))
        gain_two = jnp.sum(rows_w_in.astype(F32) * grad_mlp[:, : 2 * units], axis=1)
        gains = jnp.stack([gain_one, gain_two])

    gains = gains + swap_tp(gains)
    return (
        output,
        grad_input,
        gains[0] / lax.dynamic_slice_in_dim(gain_attn, first, mine, 0),
        gains[1] / lax.dynamic_slice_in_dim(gain_mlp, first, mine, 0),
        grad_w_qkv,
        grad_w_attn_out,
        grad_w_in,
        grad_w_mlp_out.T,
    )


def solution(mesh):
    in_specs = (
        P("ctx", None),
        P("ctx", None),
        P(),
        P(),
        P(None, None, "tp"),
        P("tp", None),
        P(None, None, "tp"),
        P("tp", None),
    )
    out_specs = (
        P("ctx", None),
        P("ctx", None),
        P("ctx"),
        P("ctx"),
        P("ctx", None, "tp"),
        P("tp", "ctx"),
        P("ctx", None, "tp"),
        P("tp", "ctx"),
    )
    body = functools.partial(layer, mesh.shape["ctx"], mesh.shape["tp"])
    return jax.shard_map(body, mesh=mesh, in_specs=in_specs, out_specs=out_specs, check_vma=False)
```

```python
import functools
import math

import jax
import jax.numpy as jnp
from jax import lax
from jax.experimental import pallas as pl
from jax.experimental.pallas import tpu as pltpu
from jax.sharding import PartitionSpec as P

HD = 64
HALF = HD // 2
ROPE_BASE = 160000.0
NORM_EPS = 1e-05
BF = jnp.bfloat16
F32 = jnp.float32
GRANT = 60 * 1024 * 1024


def dot(a, b, dims):
    return lax.dot_general(a, b, (dims, ((), ())), preferred_element_type=F32)


def nn(a, b):
    return dot(a, b, ((1,), (0,)))


def nt(a, b):
    return dot(a, b, ((1,), (1,)))


def staged(body, ins, outs, name, scratch=(), late=0, scalars=0, cost=None, far=0):
    arrays = ins[scalars:]
    count = len(arrays)

    def kernel(*refs):
        front, refs = refs[:scalars], refs[scalars:]
        given, refs = refs[:count], refs[count:]
        results, refs = refs[: len(outs)], refs[len(outs) :]
        held, sems, rest = refs[:count], refs[count], refs[count + 1 :]
        copies = [pltpu.make_async_copy(g, h, sems.at[i]) for i, (g, h) in enumerate(zip(given, held))]
        for copy in copies:
            copy.start()
        for copy in copies[: count - late]:
            copy.wait()
        body(*front, *held, *results, *rest, *[copy.wait for copy in copies[count - late :]])

    vmem, hbm = pl.BlockSpec(memory_space=pltpu.VMEM), pl.BlockSpec(memory_space=pl.ANY)
    specs = [vmem] * (len(outs) - far) + [hbm] * far
    return pl.pallas_call(
        kernel,
        in_specs=[pl.BlockSpec(memory_space=pltpu.SMEM)] * scalars + [hbm] * count,
        out_specs=specs,
        out_shape=outs,
        scratch_shapes=[
            *[pltpu.VMEM(v.shape, v.dtype) for v in arrays],
            pltpu.SemaphoreType.DMA((count,)),
            *scratch,
        ],
        compiler_params=pltpu.CompilerParams(vmem_limit_bytes=GRANT),
        cost_estimate=cost,
        name=name,
    )(*ins)


def whole_lanes(size):
    return -(-size // 128) * 128


def work(flops, byte_count, transcendentals=0):
    return pl.CostEstimate(flops=flops, bytes_accessed=byte_count, transcendentals=transcendentals)


def shaped(shape, dtype):
    return jax.ShapeDtypeStruct(shape, dtype)


def load_rows(parts, row, out_ref):
    for j, (ref, first) in enumerate(parts):
        blocks, width = ref.shape[0], ref.shape[2]
        for b in range(blocks):
            out_ref[j, b * width : (b + 1) * width, :] = ref[b, first + row : first + row + HD, :].T


def load_columns(parts, row, out_ref):
    for j, (ref, first) in enumerate(parts):
        blocks, width = ref.shape[0], ref.shape[2]
        for b in range(blocks):
            out_ref[j, :, b * width : (b + 1) * width] = ref[b, first + row : first + row + HD, :]


def attend_kernel(part_count, own_ref, *refs):
    others = refs[: part_count - 1]
    out_ref, low_ref, lse_ref, k_scr, vt_scr, s_scr = refs[part_count - 1 :]
    blocks, width = own_ref.shape[0], own_ref.shape[2]
    parts = [(r, HD) for r in (own_ref, *others)]
    load_rows(parts, 0, k_scr)
    load_columns(parts, HD, vt_scr)
    pair = s_scr.shape[2] // width

    @pl.loop(0, blocks // pair, unroll=True)
    def query_block(i):
        qt = jnp.concatenate([own_ref[pair * i + b, :HD, :] for b in range(pair)], axis=1)

        def score(j, top):
            s = nn(k_scr[j], qt)
            s_scr[j] = s
            return jnp.maximum(top, jnp.max(s, axis=0, keepdims=True))

        top = jnp.full((1, pair * width), -jnp.inf, F32)
        top = lax.fori_loop(0, part_count, score, top, unroll=part_count <= 2)

        def weigh(j, carry):
            total, acc = carry
            p = jnp.exp(s_scr[j] - top)
            return total + jnp.sum(p, axis=0, keepdims=True), acc + nn(vt_scr[j], p.astype(BF))

        start = (jnp.zeros((1, pair * width), F32), jnp.zeros((HD, pair * width), F32))
        total, acc = lax.fori_loop(0, part_count, weigh, start, unroll=part_count <= 2)
        attended = acc / total
        lse = top + jnp.log(total)
        for b in range(pair):
            cut = slice(b * width, (b + 1) * width)
            out_ref[pair * i + b] = attended[:, cut]
            for t in range(low_ref.shape[0]):
                low_ref[t, pair * i + b] = attended[:, cut].astype(BF)
            lse_ref[pair * i + b] = lse[:, cut]


def attend(tp_size, own, others):
    blocks, unused, width = own.shape
    part_count = 1 + len(others)
    keys = blocks * width
    pair = 2 if blocks % 2 == 0 else 1
    flops = 4 * keys * keys * part_count * HD
    return staged(
        functools.partial(attend_kernel, part_count),
        [own, *others],
        [
            shaped((blocks, HD, width), F32),
            shaped((tp_size, blocks, HD, width), BF),
            shaped((blocks, 1, width), F32),
        ],
        "attend",
        [
            pltpu.VMEM((part_count, keys, HD), BF),
            pltpu.VMEM((part_count, HD, keys), BF),
            pltpu.VMEM((part_count, keys, pair * width), F32),
        ],
        cost=work(flops, 4 * own.size, keys * keys * part_count),
    )


def turn_back(values, cosine, sine):
    first, second = values[:HALF], values[HALF:]
    return jnp.concatenate([first * cosine + second * sine, second * cosine - first * sine], axis=0)


def attend_back_kernel(part_count, own_ref, *refs):
    others = refs[: part_count - 1]
    refs = refs[part_count - 1 :]
    grad_ref, out_ref, lse_ref, cos_ref, sin_ref = refs[:5]
    dq_ref, dkv_ref = refs[5:7]
    dkv_others = refs[7 : 6 + part_count]
    k_scr, v_scr, kt_scr, dk_scr, dv_scr = refs[6 + part_count :]
    blocks, width = own_ref.shape[0], own_ref.shape[2]
    parts = [(r, HD) for r in (own_ref, *others)]
    load_rows(parts, 0, k_scr)
    load_rows(parts, HD, v_scr)
    load_columns(parts, 0, kt_scr)
    dk_scr[...] = jnp.zeros_like(dk_scr)
    dv_scr[...] = jnp.zeros_like(dv_scr)
    pair = 2 if blocks % 2 == 0 else 1

    @pl.loop(0, blocks // pair, unroll=True)
    def query_block(i):
        span = range(pair)
        qt = jnp.concatenate([own_ref[pair * i + b, :HD, :] for b in span], axis=1)
        gt = jnp.concatenate(
            [
                (grad_ref[0, pair * i + b].astype(F32) + grad_ref[1, pair * i + b].astype(F32)).astype(BF)
                for b in span
            ],
            axis=1,
        )
        ot = jnp.concatenate([out_ref[pair * i + b] for b in span], axis=1)
        lse = jnp.concatenate([lse_ref[pair * i + b] for b in span], axis=1)
        q, g = qt.T, gt.T
        delta = jnp.sum(gt.astype(F32) * ot, axis=0, keepdims=True)

        def one(j, dq):
            p = jnp.exp(nn(k_scr[j], qt) - lse)
            ds = (p * (nn(v_scr[j], gt) - delta)).astype(BF)
            dv_scr[j] += nn(p.astype(BF), g)
            dk_scr[j] += nn(ds, q)
            return dq + nn(kt_scr[j], ds)

        start = jnp.zeros((HD, pair * width), F32)
        dq = lax.fori_loop(0, part_count, one, start, unroll=part_count <= 2)
        for b in span:
            at = pair * i + b
            block = dq[:, b * width : (b + 1) * width] * (HD**-0.5)
            dq_ref[at] = turn_back(block, cos_ref[at], sin_ref[at]).astype(BF)

    for j, ref in enumerate((dkv_ref, *dkv_others)):
        for b in range(blocks):
            rows = slice(b * width, (b + 1) * width)
            ref[b, :HD, :] = dk_scr[j, rows, :].T
            ref[b, HD:, :] = dv_scr[j, rows, :].T


def attend_back(own, others, grad, attended, lse, cosine, sine):
    blocks, unused, width = own.shape
    part_count = 1 + len(others)
    keys = blocks * width
    flops = 10 * keys * keys * part_count * HD
    return staged(
        functools.partial(attend_back_kernel, part_count),
        [own, *others, grad, attended, lse, cosine, sine],
        [shaped((blocks, HD, width), BF)] + [shaped((blocks, 2 * HD, width), F32)] * part_count,
        "attend_back",
        [
            pltpu.VMEM((part_count, keys, HD), BF),
            pltpu.VMEM((part_count, keys, HD), BF),
            pltpu.VMEM((part_count, HD, keys), BF),
            pltpu.VMEM((part_count, keys, HD), F32),
            pltpu.VMEM((part_count, keys, HD), F32),
        ],
        cost=work(flops, 8 * own.size, keys * keys * part_count),
    )


def combine_kernel(count, dq_ref, *refs):
    terms, (cos_ref, sin_ref, out_ref) = refs[:count], refs[count:]
    for b in range(dq_ref.shape[0]):
        total = terms[0][b]
        for ref in terms[1:]:
            total = total + ref[b]
        out_ref[b, :HD] = dq_ref[b]
        out_ref[b, HD : 2 * HD] = turn_back(total[:HD], cos_ref[b], sin_ref[b]).astype(BF)
        out_ref[b, 2 * HD :] = total[HD:].astype(BF)


def combine(dq, terms, cosine, sine):
    blocks, unused, width = dq.shape
    return staged(
        functools.partial(combine_kernel, len(terms)),
        [dq, *terms, cosine, sine],
        [shaped((blocks, 3 * HD, width), BF)],
        "combine",
        cost=work(dq.size, 20 * dq.size),
    )[0]


def standardise(values):
    centred = values - jnp.mean(values, axis=-1, keepdims=True)
    spread = jnp.mean(centred * centred, axis=-1, keepdims=True)
    scale = lax.rsqrt(spread + NORM_EPS)
    return centred * scale, scale


def standardise_back(gradient, gain, normed, scale):
    y = gradient * gain
    along = jnp.mean(y * normed, axis=-1, keepdims=True)
    return scale * (y - jnp.mean(y, axis=-1, keepdims=True) - normed * along)


def project_kernel(hidden_ref, gain_ref, cos_ref, sin_ref, *refs):
    weights, (packed_ref, input_ref), waits = refs[:3], refs[3:5], refs[5:]
    normed, unused = standardise(hidden_ref[...].astype(F32))
    attn_input = (normed * gain_ref[...]).astype(BF)
    input_ref[...] = attn_input
    cosine, sine = cos_ref[...], sin_ref[...]
    for c in range(3):
        waits[c]()
        rows = nn(attn_input, weights[c][0]).T
        for h in range(packed_ref.shape[0]):
            block = rows[h * HD : (h + 1) * HD]
            if c < 2:
                first, second = block[:HALF], block[HALF:]
                block = jnp.concatenate(
                    [first * cosine - second * sine, second * cosine + first * sine], axis=0
                )
            if c == 0:
                block = block * (HD**-0.5)
            packed_ref[h, c * HD : (c + 1) * HD] = block.astype(BF)


def project(hidden, gain, cosine, sine, weights):
    width, model = hidden.shape
    heads = weights.shape[2] // HD
    hbm, vmem = pl.BlockSpec(memory_space=pltpu.HBM), pl.BlockSpec(memory_space=pltpu.VMEM)

    def kernel(h_ref, g_ref, c_ref, s_ref, w_ref, packed_ref, input_ref, h_scr, w_scr, sems):
        copies = [pltpu.make_async_copy(h_ref, h_scr, sems.at[3])]
        copies += [pltpu.make_async_copy(w_ref.at[c], w_scr.at[c], sems.at[c]) for c in range(3)]
        for copy in copies:
            copy.start()
        copies[0].wait()
        blocks = [w_scr.at[pl.ds(c, 1)] for c in range(3)]
        waits = [copy.wait for copy in copies[1:]]
        project_kernel(h_scr, g_ref, c_ref, s_ref, *blocks, packed_ref, input_ref, *waits)

    return pl.pallas_call(
        kernel,
        in_specs=[hbm, vmem, vmem, vmem, hbm],
        out_specs=(vmem, vmem),
        out_shape=(shaped((heads, 3 * HD, width), BF), shaped((width, model), BF)),
        scratch_shapes=[
            pltpu.VMEM(hidden.shape, BF),
            pltpu.VMEM(weights.shape, BF),
            pltpu.SemaphoreType.DMA((4,)),
        ],
        compiler_params=pltpu.CompilerParams(vmem_limit_bytes=GRANT),
        cost_estimate=work(2 * width * weights.size, 2 * weights.size),
        name="project",
    )(hidden, gain, cosine, sine, weights)


def unit_back_kernel(cot_ref, w_ref, out_ref):
    out_ref[...] = nt(cot_ref[...], w_ref[...])


def unit_back(cotangent, weights):
    width, units = cotangent.shape[0], weights.shape[0]
    return staged(
        unit_back_kernel,
        [cotangent, weights],
        [shaped((width, units), F32)],
        "unit_back",
        cost=work(2 * width * weights.size, 2 * weights.size),
    )[0]


def middle_kernel(
    tp_ref,
    attn_ref,
    hidden_ref,
    cot_ref,
    gain_ref,
    own_ref,
    other_ref,
    grad_act_ref,
    w_in_ref,
    middle_ref,
    mid_ref,
    act_ref,
    part_ref,
    heads_ref,
    wait_units,
):
    tp = tp_ref[0]
    attn_own = attn_ref[tp].T
    branch = nn(attn_own, own_ref[...]) + nn(attn_ref[1 - tp].T, other_ref[...])
    middle = hidden_ref[...].astype(F32) + branch
    middle_ref[...] = middle
    normed, scale = standardise(middle)
    gain = gain_ref[...]
    mlp_input = (normed * gain).astype(BF)
    model, inner = mlp_input.shape[1], attn_own.shape[1]
    first = model + inner
    mid_ref[:, :model] = mlp_input
    mid_ref[:, model:first] = attn_own
    wait_units()
    turned = mlp_input.T
    gate, up = nn(w_in_ref[0], turned).T, nn(w_in_ref[1], turned).T
    share = 0.5 * (1.0 + lax.erf(gate * (0.5**0.5)))
    slope = share + gate * jnp.exp(-0.5 * gate * gate) * ((2.0 * math.pi) ** -0.5)
    bent = gate * share
    grad_act = grad_act_ref[...]
    grad_gate = (slope * up * grad_act).astype(BF)
    grad_up = (bent * grad_act).astype(BF)
    units = grad_gate.shape[1]
    mid_ref[:, first : first + units] = grad_gate
    mid_ref[:, first + units : first + 2 * units] = grad_up
    activated = (bent * up).astype(BF)
    mid_ref[:, first + 2 * units : first + 3 * units] = activated
    act_ref[...] = activated
    last = first + 3 * units
    if last < mid_ref.shape[1]:
        mid_ref[:, last:] = jnp.zeros((activated.shape[0], mid_ref.shape[1] - last), BF)
    part = nn(grad_gate, w_in_ref[0]) + nn(grad_up, w_in_ref[1])
    part_ref[...] = part.astype(BF)
    grad = 0.5 * cot_ref[...].astype(F32) + standardise_back(part, gain, normed, scale)
    grad = grad.astype(BF)
    shape = heads_ref.shape[1:]
    heads_ref[tp] = nt(own_ref[...], grad).astype(BF).reshape(shape)
    heads_ref[1 - tp] = nt(other_ref[...], grad).astype(BF).reshape(shape)


def middle_part(tp, attn, hidden, cotangent, gain, own, other, grad_act, w_in):
    width, model = hidden.shape
    units = w_in.shape[1]
    inner = own.shape[0]
    return staged(
        middle_kernel,
        [tp, attn, hidden, cotangent, gain, own, other, grad_act, w_in],
        [
            shaped((width, model), F32),
            shaped((width, whole_lanes(model + inner + 3 * units)), BF),
            shaped((width, units), BF),
            shaped((width, model), BF),
            shaped((2, inner // HD, HD, width), BF),
        ],
        "middle_part",
        late=1,
        scalars=1,
        cost=work(8 * width * model * (units + inner), 2 * w_in.size, 2 * width * units),
    )


def project_back_kernel(grad_ref, w_ref, out_ref):
    heads = grad_ref.shape[0]
    total = jnp.zeros(out_ref.shape, F32)
    for c in range(3):
        rows = jnp.concatenate([grad_ref[h, c * HD : (c + 1) * HD, :] for h in range(heads)], axis=0)
        total += nt(rows.T, w_ref[c])
    out_ref[...] = total.astype(BF)


def project_back(grad, weights):
    width = grad.shape[2]
    return staged(
        project_back_kernel,
        [grad, weights],
        [shaped((width, weights.shape[1]), BF)],
        "project_back",
        cost=work(2 * width * weights.size, 2 * weights.size),
    )[0]


def picked(pick_ref, own_ref, other_ref):
    values = jnp.concatenate([own_ref[...], other_ref[...]], axis=0)
    return nt(pick_ref[...], values).astype(BF)


def head_weight_kernel(mine, ids_ref, grad_ref, *refs):
    rows, keep_ref, give_ref, total_scr = refs[:-3], *refs[-3:]
    count = len(rows)
    core = ids_ref[count]
    grads = jnp.concatenate([grad_ref[ids_ref[b]] for b in range(count)], axis=1)
    inputs = jnp.concatenate([ref[...] for ref in rows], axis=0)
    total_scr[...] = nn(grads, inputs).T
    for b in range(keep_ref.shape[0]):
        keep = pl.multiple_of((2 * b + core) * mine, mine)
        give = pl.multiple_of((2 * b + 1 - core) * mine, mine)
        keep_ref[b] = total_scr[pl.ds(keep, mine), :].astype(BF)
        give_ref[b] = total_scr[pl.ds(give, mine), :].astype(BF)


def head_weight(chips, ids, grad, rows):
    width, model = rows[0].shape
    columns = grad.shape[1]
    mine = model // (2 * chips)
    return staged(
        functools.partial(head_weight_kernel, mine),
        [ids, grad, *rows],
        [shaped((chips, mine, columns), BF)] * 2,
        "head_weight",
        [pltpu.VMEM((model, columns), F32)],
        scalars=1,
        cost=work(2 * len(rows) * rows[0].size * columns, 2 * len(rows) * rows[0].size),
    )


def mlp_weight_kernel(sizes, inner, units, pick_ref, *refs):
    cot_own, cot_other, own_ref, other_ref = refs[:4]
    outs = refs[4 : 4 + len(sizes)]
    total_scr, sems = refs[4 + len(sizes) :]
    model = cot_own.shape[1]
    first = model + inner
    cot_both = jnp.concatenate([cot_own[...], cot_other[...]], axis=0)
    both = jnp.concatenate([own_ref[...], other_ref[...]], axis=0)
    columns = both[:, first : first + 3 * units]
    copies, start, done, rows = [], 0, 0, total_scr.shape[0]
    for r, ref in enumerate(outs):
        while start + sizes[r] > done:
            cut = slice(done, done + rows // 2)
            in_rows = nt(pick_ref[cut], both[:, :model]).astype(BF)
            cot_rows = nt(pick_ref[cut], cot_both).astype(BF)
            total_scr[cut, : 2 * units] = nn(in_rows, columns[:, : 2 * units]).astype(BF)
            total_scr[cut, 2 * units : 3 * units] = nn(cot_rows, columns[:, 2 * units :]).astype(BF)
            if 3 * units < total_scr.shape[1]:
                rest = total_scr.shape[1] - 3 * units
                total_scr[cut, 3 * units :] = jnp.zeros((rows // 2, rest), BF)
            done += rows // 2
        copies.append(pltpu.make_async_copy(total_scr.at[pl.ds(start, sizes[r])], ref, sems.at[r]))
        copies[-1].start()
        start += sizes[r]
    for copy in copies:
        copy.wait()


def mlp_weight(sizes, inner, units, pick, cot_own, cot_other, own, other):
    rows, columns = sum(sizes), whole_lanes(3 * units)
    return staged(
        functools.partial(mlp_weight_kernel, sizes, inner, units),
        [pick, cot_own, cot_other, own, other],
        [shaped((size, columns), BF) for size in sizes],
        "mlp_weight",
        [pltpu.VMEM((rows, columns), BF), pltpu.SemaphoreType.DMA((len(sizes),))],
        cost=work(4 * rows * own.size, 2 * rows * columns + 8 * own.size),
        far=len(sizes),
    )


def out_weight_kernel(mine, pick_ref, own_ref, other_ref, attn_ref, attn_other_ref, *outs):
    both = jnp.concatenate([own_ref[...], other_ref[...]], axis=0)
    rows = nt(pick_ref[...], both).astype(BF)
    total = nn(rows, jnp.concatenate([attn_ref[...], attn_other_ref[...]], axis=0)).astype(BF)
    for r, ref in enumerate(outs):
        ref[...] = total[r * ref.shape[0] : (r + 1) * ref.shape[0]]


def out_weight(count, inner, pick, own, other, mid, mid_other):
    rows, (width, model) = pick.shape[0], own.shape
    vmem, hbm = pl.BlockSpec(memory_space=pltpu.VMEM), pl.BlockSpec(memory_space=pl.ANY)

    def kernel(pick_ref, own_ref, other_ref, mid_ref, mid_other_ref, *refs):
        outs, held, sems = refs[:count], refs[count : count + 5], refs[count + 5]
        columns = pl.ds(model, inner)
        given = [pick_ref, own_ref, other_ref, mid_ref.at[:, columns], mid_other_ref.at[:, columns]]
        copies = [pltpu.make_async_copy(g, h, sems.at[i]) for i, (g, h) in enumerate(zip(given, held))]
        for copy in copies:
            copy.start()
        for copy in copies:
            copy.wait()
        out_weight_kernel(rows // count, *held, *outs)

    return pl.pallas_call(
        kernel,
        in_specs=[hbm] * 5,
        out_specs=[vmem] * count,
        out_shape=[shaped((rows // count, inner), BF)] * count,
        scratch_shapes=[
            pltpu.VMEM(pick.shape, BF),
            pltpu.VMEM(own.shape, BF),
            pltpu.VMEM(own.shape, BF),
            pltpu.VMEM((width, inner), BF),
            pltpu.VMEM((width, inner), BF),
            pltpu.SemaphoreType.DMA((5,)),
        ],
        compiler_params=pltpu.CompilerParams(vmem_limit_bytes=GRANT),
        cost_estimate=work(4 * rows * own.size, 8 * own.size),
        name="out_weight",
    )(pick, own, other, mid, mid_other)


def ring_add_kernel(count, *refs):
    outs, scratch, sems = refs[2 * count : 2 * count + 2], refs[2 * count + 2], refs[2 * count + 3]
    waits = refs[2 * count + 4 :]
    copies = []
    for side in range(2):
        given = refs[count * side : count * (side + 1)]
        for wait in waits[count * side : count * (side + 1)]:
            wait()
        block, got = given[:2]
        out = scratch.at[side]
        wide, rows = block.shape[1], got.shape[0]
        total = block[...].astype(F32)
        if rows == block.shape[0]:
            out[:, :wide] = (total + got[:, :wide].astype(F32)).astype(BF)
        elif side == 0:
            out[:rows, :wide] = (total[:rows] + got[...].astype(F32)).astype(BF)
            out[rows:, :wide] = block[rows:, :]
        else:
            out[:rows, :wide] = block[:rows, :]
            out[rows:, :wide] = (total[rows:] + got[...].astype(F32)).astype(BF)
        if count == 3 and got.shape[1] > wide:
            out[:, wide:] = (given[2][...].astype(F32) + got[:, wide:].astype(F32)).astype(BF)
        elif count == 3:
            out[:, wide:] = given[2][...]
        copies.append(pltpu.make_async_copy(out, outs[side], sems.at[side]))
        copies[-1].start()
    for copy in copies:
        copy.wait()


def ring_add(right, left):
    rows = right[0].shape[0]
    columns = right[0].shape[1] + (right[2].shape[1] if len(right) == 3 else 0)
    return staged(
        functools.partial(ring_add_kernel, len(right)),
        [*right, *left],
        [shaped((rows, columns), BF)] * 2,
        "ring_add",
        [pltpu.VMEM((2, rows, columns), BF), pltpu.SemaphoreType.DMA((2,))],
        late=2 * len(right),
        cost=work(4 * rows * columns, 12 * rows * columns),
        far=2,
    )


def finish_qkv_kernel(first_ref, blocks_ref, w_ref, out_ref, gain_ref, w_scr, sem):
    mine = out_ref.shape[1]
    rows = pl.ds(pl.multiple_of(first_ref[0], mine), mine)
    copy = pltpu.make_async_copy(w_ref.at[:, rows, :], w_scr, sem)
    copy.start()
    for c in range(3):
        for h in range(blocks_ref.shape[0]):
            cut = slice(h * HD, (h + 1) * HD)
            out_ref[c, :, cut] = blocks_ref[h, :, c * HD : (c + 1) * HD].astype(F32)
    copy.wait()
    total = jnp.zeros((mine, 1), F32)
    for c in range(3):
        total += jnp.sum(out_ref[c] * w_scr[c].astype(F32), axis=1, keepdims=True)
    gain_ref[...] = total


def finish_qkv(first, blocks, weights):
    heads, mine, unused = blocks.shape
    inner = weights.shape[2]
    vmem, hbm = pl.BlockSpec(memory_space=pltpu.VMEM), pl.BlockSpec(memory_space=pltpu.HBM)
    return pl.pallas_call(
        finish_qkv_kernel,
        in_specs=[pl.BlockSpec(memory_space=pltpu.SMEM), vmem, hbm],
        out_specs=(vmem, vmem),
        out_shape=(shaped((3, mine, inner), F32), shaped((mine, 1), F32)),
        scratch_shapes=[pltpu.VMEM((3, mine, inner), BF), pltpu.SemaphoreType.DMA],
        compiler_params=pltpu.CompilerParams(vmem_limit_bytes=GRANT),
        cost_estimate=work(2 * blocks.size, 10 * blocks.size),
        name="finish_qkv",
    )(first, blocks, weights)


def finish_mlp_kernel(own_ref, right_ref, left_ref, w_ref, gain_ref, inverse_ref, in_ref, out_ref, gains_ref):
    units = out_ref.shape[1]
    wide = own_ref.shape[1]
    total = own_ref[...].astype(F32) + right_ref[:, :wide].astype(F32) + left_ref[:, :wide].astype(F32)
    out_ref[...] = total[:, 2 * units : 3 * units]
    in_ref[:, 0, :] = total[:, :units]
    in_ref[:, 1, :] = total[:, units : 2 * units]
    term = jnp.sum(total[:, : 2 * units] * w_ref[...].astype(F32), axis=1, keepdims=True)
    mine = term.shape[0]
    inverse = inverse_ref[...]
    gains_ref[0:1] = jnp.broadcast_to(gain_ref[...], (mine, 128)).T[0:1] * inverse[0:1]
    gains_ref[1:2] = jnp.broadcast_to(term, (mine, 128)).T[0:1] * inverse[1:2]


def finish_mlp(units, own, right, left, rows, gain, inverse):
    mine = own.shape[0]
    return staged(
        finish_mlp_kernel,
        [own, right, left, rows, gain, inverse],
        [shaped((mine, 2, units), F32), shaped((mine, units), F32), shaped((2, mine), F32)],
        "finish_mlp",
        cost=work(8 * own.size, 14 * own.size),
    )


def middle_back_kernel(middle_ref, cot_ref, gain_ref, own_ref, other_ref, out_ref, low_ref):
    normed, scale = standardise(middle_ref[...])
    part = own_ref[...].astype(F32) + other_ref[...].astype(F32)
    grad = cot_ref[...].astype(F32) + standardise_back(part, gain_ref[...], normed, scale)
    out_ref[...] = grad
    low_ref[...] = grad.astype(BF)


def middle_back(middle, cotangent, gain, own, other):
    return staged(
        middle_back_kernel,
        [middle, cotangent, gain, own, other],
        [shaped(middle.shape, F32), shaped(middle.shape, BF)],
        "middle_back",
        cost=work(20 * middle.size, 16 * middle.size),
    )


def input_back_kernel(hidden_ref, gain_ref, own_ref, grad_ref, other_ref, out_ref):
    normed, scale = standardise(hidden_ref[...].astype(F32))
    part = own_ref[...].astype(F32) + other_ref[...].astype(F32)
    out_ref[...] = grad_ref[...] + standardise_back(part, gain_ref[...], normed, scale)


def input_back(hidden, gain, own, grad, other):
    return staged(
        input_back_kernel,
        [hidden, gain, own, grad, other],
        [shaped(grad.shape, F32)],
        "input_back",
        cost=work(20 * grad.size, 14 * grad.size),
    )[0]


def layer(ctx_size, tp_size, hidden_in, cotangent, gain_attn, gain_mlp, w_qkv, w_attn_out, w_in, w_mlp_out):
    width = hidden_in.shape[0]
    model = hidden_in.shape[1]
    inner = w_qkv.shape[2]
    heads = inner // HD
    units = w_in.shape[2]
    chips = ctx_size // 2
    copies = chips // heads
    mine = model // ctx_size
    me = lax.axis_index("ctx")
    core = me % 2

    same_core = [[2 * p + k for p in range(chips)] for k in range(2)]
    head_groups = [
        [2 * (heads * g + p) + k for p in range(heads)] for g in range(copies) for k in range(2)
    ]

    wide_groups = [
        [(2 * (heads * g + p) + k) * tp_size + t for t in range(tp_size) for p in range(heads)]
        for g in range(copies)
        for k in range(2)
    ]

    def exchange_wide(values):
        return lax.all_to_all(values, ("ctx", "tp"), 0, 0, axis_index_groups=wide_groups)

    def exchange(values):
        return lax.all_to_all(values, "ctx", 0, 0, axis_index_groups=head_groups)

    def swap_core(values):
        return lax.ppermute(values, "ctx", [(c, c ^ 1) for c in range(ctx_size)])

    def shift_keys(values, step):
        ring = 2 * copies
        pairs = []
        for c in range(ctx_size):
            g, p, k = c // (2 * heads), (c // 2) % heads, c % 2
            t = (2 * g + k + step) % ring
            pairs.append((c, 2 * (heads * (t // 2) + p) + t % 2))
        return lax.ppermute(values, "ctx", pairs)

    def swap_tp(values):
        return lax.ppermute(values, "tp", [(0, 1), (1, 0)])

    def add_tp(low):
        return low.astype(F32) + swap_tp(low).astype(F32)

    def after(values, *earlier):
        return lax.optimization_barrier((values, earlier))[0]

    def ring_chip(position):
        position = position % chips
        up = 2 * position
        return jnp.where(position < chips // 2, up, 2 * chips - 1 - up)

    ring = [2 * q if q < chips // 2 else 2 * chips - 1 - 2 * q for q in range(chips)]
    place = {p: q for q, p in enumerate(ring)}

    def turn(values, step):
        pairs = [
            (2 * p + k, 2 * ring[(place[p] + step) % chips] + k)
            for p in range(chips)
            for k in range(2)
        ]
        return lax.ppermute(values, "ctx", pairs)

    chip = me // 2
    position = jnp.where(chip % 2 == 0, chip // 2, chips - 1 - chip // 2)
    ringed = copies == 1

    def picker(chip_ids):
        wanted = ((2 * chip_ids + core) * mine)[:, None] + jnp.arange(mine)[None, :]
        return (wanted.reshape(-1, 1) == jnp.arange(model)[None, :]).astype(BF)

    def scatter(parts):
        flat = parts.reshape(chips, -1)
        summed = lax.psum_scatter(
            flat, "ctx", scatter_dimension=0, tiled=True, axis_index_groups=same_core
        )
        return summed.reshape((mine,) + parts.shape[1:]).astype(F32)

    group_first = (me // (2 * heads)) * (2 * heads)
    block_ids = group_first + 2 * jnp.arange(heads) + core
    inverse = ROPE_BASE ** (-(jnp.arange(HALF).astype(F32) * 2.0) / HD)

    def tables(ids):
        positions = (ids[:, None] * width + jnp.arange(width)[None, :]).astype(F32)
        angles = positions[:, None, :] * inverse[None, :, None]
        return jnp.cos(angles), jnp.sin(angles)

    tp = lax.axis_index("tp")
    tp_list = tp.astype(jnp.int32).reshape(1)
    cos_one, sin_one = tables(me[None])
    w_three = w_qkv.transpose(1, 0, 2)
    w_pair = w_in.transpose(1, 2, 0)

    packed, attn_input = project(hidden_in, gain_attn[None], cos_one[0], sin_one[0], w_three)
    own = exchange(packed)
    first = me * mine
    both_gains = after(jnp.stack([gain_attn, gain_mlp]), packed)
    gain_inverse = 1.0 / lax.dynamic_slice_in_dim(both_gains, first, mine, 1)
    w_out_other = swap_tp(w_attn_out)
    later_cot = after(cotangent, packed)
    cot_other = swap_core(later_cot)
    cos_all, sin_all = tables(after(block_ids, packed))
    order = after(jnp.arange(chips), packed)
    pick = picker(ring_chip(position + order) if ringed else order)
    gathered = [attn_input]
    right = left = after(attn_input, cos_all, sin_all, pick)

    def gather_step(step, *earlier):
        nonlocal right, left
        if 2 * step == chips:
            right = turn(after(right, *earlier), 1)
            gathered.append(right)
            return
        right, left = after((right, left), *earlier)
        right, left = turn(right, 1), turn(left, -1)
        gathered.extend([right, left])

    if ringed:
        gather_step(1)
    own = after(own, cos_all, sin_all, pick)
    others = [shift_keys(own, step) for step in range(1, 2 * copies)]
    attended, attended_low, lse = attend(tp_size, own, others)
    if ringed:
        attended_low = after(attended_low, right, left)
    attn_all = exchange_wide(attended_low.reshape(tp_size * heads, HD, width))
    grad_activated = unit_back(after(cotangent, attended_low), w_mlp_out)
    if ringed:
        gather_step(2, attended_low)
    rows_w_in = lax.dynamic_slice_in_dim(after(w_in, attended_low), me * mine, mine, 0)
    rows_w_in = rows_w_in.reshape(mine, 2 * units)
    attn_all = after(attn_all, rows_w_in, grad_activated, right, left).reshape(tp_size, inner, width)
    if ringed:
        gather_step(3, attn_all)
    middle, mid, activated_low, part_two, head_terms = middle_part(
        tp_list,
        attn_all,
        hidden_in,
        cotangent,
        gain_mlp[None],
        w_attn_out,
        w_out_other,
        grad_activated,
        w_pair,
    )
    if ringed:
        results = (middle, mid, activated_low, part_two, head_terms)
        middle, mid, activated_low, part_two, head_terms = after(results, right, left)
    grad_received = exchange_wide(head_terms.reshape(tp_size * heads, HD, width))

    half = chips // 2
    sizes = [mine] * half + [mine // 2, mine // 2] + [mine] * (half - 1) if ringed else [chips * mine]
    mid_other = swap_core(mid)
    parts_mlp = mlp_weight(sizes, inner, units, pick, cotangent, cot_other, mid, mid_other)
    if ringed:
        mlp_rights = parts_mlp[half::-1]
        mlp_lefts = parts_mlp[half + 1 :]
        got_right, got_left = turn(mlp_rights[0], 1), turn(mlp_lefts[0], -1)
    part_two_other = swap_tp(after(part_two, mid_other))
    later_two = after(part_two_other, parts_mlp)
    grad_middle, grad_middle_low = middle_back(middle, cotangent, gain_mlp[None], part_two, later_two)
    grad_received = after(grad_received, parts_mlp, right, left, grad_middle_low)
    if ringed:
        gather_step(4, parts_mlp)
    grad_received = grad_received.reshape(tp_size, heads, HD, width)
    dq, *grad_kv = attend_back(own, others, grad_received, attended, lse, cos_all, sin_all)

    low_other = swap_core(grad_middle_low)
    if ringed:
        grad_kv = after(grad_kv, got_right, got_left, right, low_other)
    terms = [grad_kv[0]]
    for step in range(1, 2 * copies):
        terms.append(shift_keys(grad_kv[step], -step))
    parts_out = out_weight(
        chips if ringed else 1,
        inner,
        pick,
        after(grad_middle_low, dq),
        low_other,
        mid,
        mid_other,
    )
    if ringed:

        def ring_step(step, narrow, *earlier):
            nonlocal got_right, got_left
            rights = [mlp_rights[step], after(got_right, *earlier)]
            lefts = [mlp_lefts[step], got_left]
            if narrow:
                rights.append(parts_out[half - step])
                lefts.append(parts_out[half + step])
            sent = ring_add(rights, lefts)
            got_right, got_left = turn(sent[0], 1), turn(sent[1], -1)
            return sent

        sent = ring_step(1, True, dq)
        terms[0] = after(terms[0], sent)
    grad_own = combine(dq, terms, cos_all, sin_all)
    grad_back = exchange(grad_own)
    if ringed:
        direct = turn(after(parts_out[half], sent), half)
        steps = [0]
        for step in range(1, half + 1):
            steps.extend([-step, step])
        ids = ring_chip(position + jnp.array(steps[:chips]))
        ids = jnp.concatenate([ids, core[None]]).astype(jnp.int32)
        keep_qkv, give_qkv = head_weight(chips, ids, grad_own, gathered)
        given_qkv = swap_core(give_qkv)
        sent = ring_step(2, True, keep_qkv)
        part_qkv = (keep_qkv.astype(F32) + given_qkv.astype(F32)).astype(BF)
        blocks_qkv = exchange(after(part_qkv, sent))
        grad_back = after(grad_back, part_qkv, sent)
    part_one = project_back(grad_back, w_three)
    part_one_other = swap_tp(part_one)
    if ringed:
        mlp_part = nn(after(activated_low, part_one), w_mlp_out).astype(BF)
        sent = ring_step(3, True, part_one_other, direct, mlp_part)
        output = (middle + add_tp(mlp_part)).astype(BF)
        part_one_other = after(part_one_other, sent)
        grad_input = input_back(hidden_in, gain_attn[None], part_one, grad_middle, part_one_other)
        grad_w_qkv, gain_one = finish_qkv(
            first.astype(jnp.int32).reshape(1), blocks_qkv, w_three
        )
        wide = mlp_rights[0].shape[1]
        grad_w_in, grad_w_mlp_out, gains = finish_mlp(
            units, parts_mlp[0], got_right, got_left, rows_w_in, gain_one, gain_inverse
        )
        grad_out = parts_out[0].astype(F32) + direct.astype(F32)
        grad_out = grad_out + got_right[:, wide:].astype(F32) + got_left[:, wide:].astype(F32)
        grad_w_attn_out = grad_out.T
        grad_w_qkv = grad_w_qkv.transpose(1, 0, 2)
    else:
        output = (middle + add_tp(nn(activated_low, w_mlp_out).astype(BF))).astype(BF)
        grad_input = input_back(hidden_in, gain_attn[None], part_one, grad_middle, part_one_other)
        grad_back = grad_back.reshape(heads, 3, HD, width)
        grad_back = grad_back.transpose(1, 0, 2, 3).reshape(3, inner, width)
        columns_in = jnp.concatenate([grad_back, swap_core(grad_back)], axis=2)
        rows_in = jnp.concatenate([attn_input, swap_core(attn_input)], axis=0)
        rows_in = nt(pick, rows_in).astype(BF)
        part_qkv = jnp.einsum("dt,cft->dcf", rows_in, columns_in, preferred_element_type=F32)
        grad_w_qkv = scatter(part_qkv.astype(BF))
        grad_mlp = scatter(parts_mlp[0])
        grad_w_in = grad_mlp[:, : 2 * units].reshape(mine, 2, units)
        grad_w_mlp_out = grad_mlp[:, 2 * units : 3 * units]
        grad_w_attn_out = scatter(parts_out[0]).T
        rows_w_qkv = lax.dynamic_slice_in_dim(w_qkv, first, mine, 0)
        gain_one = jnp.sum(rows_w_qkv.astype(F32) * grad_w_qkv, axis=(1, 2))
        gain_two = jnp.sum(rows_w_in.astype(F32) * grad_mlp[:, : 2 * units], axis=1)
        gains = jnp.stack([gain_one, gain_two]) * gain_inverse

    gains = gains + swap_tp(gains)
    return (
        output,
        grad_input,
        gains[0],
        gains[1],
        grad_w_qkv,
        grad_w_attn_out,
        grad_w_in,
        grad_w_mlp_out.T,
    )


def solution(mesh):
    in_specs = (
        P("ctx", None),
        P("ctx", None),
        P(),
        P(),
        P(None, None, "tp"),
        P("tp", None),
        P(None, None, "tp"),
        P("tp", None),
    )
    out_specs = (
        P("ctx", None),
        P("ctx", None),
        P("ctx"),
        P("ctx"),
        P("ctx", None, "tp"),
        P("tp", "ctx"),
        P("ctx", None, "tp"),
        P("tp", "ctx"),
    )
    body = functools.partial(layer, mesh.shape["ctx"], mesh.shape["tp"])
    return jax.shard_map(body, mesh=mesh, in_specs=in_specs, out_specs=out_specs, check_vma=False)
```

```python
import functools
import math

import jax
import jax.numpy as jnp
from jax import lax
from jax.experimental import pallas as pl
from jax.experimental.pallas import tpu as pltpu
from jax.sharding import PartitionSpec as P

HD = 64
HALF = HD // 2
ROPE_BASE = 160000.0
NORM_EPS = 1e-05
BF = jnp.bfloat16
F32 = jnp.float32
GRANT = 60 * 1024 * 1024


def dot(a, b, dims):
    return lax.dot_general(a, b, (dims, ((), ())), preferred_element_type=F32)


def nn(a, b):
    return dot(a, b, ((1,), (0,)))


def nt(a, b):
    return dot(a, b, ((1,), (1,)))


def staged(body, ins, outs, name, scratch=(), late=0, scalars=0, cost=None, far=0):
    arrays = ins[scalars:]
    count = len(arrays)

    def kernel(*refs):
        front, refs = refs[:scalars], refs[scalars:]
        given, refs = refs[:count], refs[count:]
        results, refs = refs[: len(outs)], refs[len(outs) :]
        held, sems, rest = refs[:count], refs[count], refs[count + 1 :]
        copies = [pltpu.make_async_copy(g, h, sems.at[i]) for i, (g, h) in enumerate(zip(given, held))]
        for copy in copies:
            copy.start()
        for copy in copies[: count - late]:
            copy.wait()
        body(*front, *held, *results, *rest, *[copy.wait for copy in copies[count - late :]])

    vmem, hbm = pl.BlockSpec(memory_space=pltpu.VMEM), pl.BlockSpec(memory_space=pl.ANY)
    specs = [vmem] * (len(outs) - far) + [hbm] * far
    return pl.pallas_call(
        kernel,
        in_specs=[pl.BlockSpec(memory_space=pltpu.SMEM)] * scalars + [hbm] * count,
        out_specs=specs,
        out_shape=outs,
        scratch_shapes=[
            *[pltpu.VMEM(v.shape, v.dtype) for v in arrays],
            pltpu.SemaphoreType.DMA((count,)),
            *scratch,
        ],
        compiler_params=pltpu.CompilerParams(vmem_limit_bytes=GRANT),
        cost_estimate=cost,
        name=name,
    )(*ins)


def whole_lanes(size):
    return -(-size // 128) * 128


def work(flops, byte_count, transcendentals=0):
    return pl.CostEstimate(flops=flops, bytes_accessed=byte_count, transcendentals=transcendentals)


def shaped(shape, dtype):
    return jax.ShapeDtypeStruct(shape, dtype)


def load_rows(parts, row, out_ref):
    for j, (ref, first) in enumerate(parts):
        blocks, width = ref.shape[0], ref.shape[2]
        for b in range(blocks):
            out_ref[j, b * width : (b + 1) * width, :] = ref[b, first + row : first + row + HD, :].T


def load_columns(parts, row, out_ref):
    for j, (ref, first) in enumerate(parts):
        blocks, width = ref.shape[0], ref.shape[2]
        for b in range(blocks):
            out_ref[j, :, b * width : (b + 1) * width] = ref[b, first + row : first + row + HD, :]


def attend_kernel(part_count, own_ref, *refs):
    others = refs[: part_count - 1]
    out_ref, low_ref, lse_ref, k_scr, vt_scr, s_scr = refs[part_count - 1 :]
    blocks, width = own_ref.shape[0], own_ref.shape[2]
    parts = [(r, HD) for r in (own_ref, *others)]
    load_rows(parts, 0, k_scr)
    load_columns(parts, HD, vt_scr)
    pair = s_scr.shape[2] // width

    @pl.loop(0, blocks // pair, unroll=True)
    def query_block(i):
        qt = jnp.concatenate([own_ref[pair * i + b, :HD, :] for b in range(pair)], axis=1)

        def score(j, top):
            s = nn(k_scr[j], qt)
            s_scr[j] = s
            return jnp.maximum(top, jnp.max(s, axis=0, keepdims=True))

        top = jnp.full((1, pair * width), -jnp.inf, F32)
        top = lax.fori_loop(0, part_count, score, top, unroll=part_count <= 2)

        def weigh(j, carry):
            total, acc = carry
            p = jnp.exp(s_scr[j] - top)
            return total + jnp.sum(p, axis=0, keepdims=True), acc + nn(vt_scr[j], p.astype(BF))

        start = (jnp.zeros((1, pair * width), F32), jnp.zeros((HD, pair * width), F32))
        total, acc = lax.fori_loop(0, part_count, weigh, start, unroll=part_count <= 2)
        attended = acc / total
        lse = top + jnp.log(total)
        for b in range(pair):
            cut = slice(b * width, (b + 1) * width)
            out_ref[pair * i + b] = attended[:, cut]
            for t in range(low_ref.shape[0]):
                low_ref[t, pair * i + b] = attended[:, cut].astype(BF)
            lse_ref[pair * i + b] = lse[:, cut]


def attend(tp_size, own, others):
    blocks, unused, width = own.shape
    part_count = 1 + len(others)
    keys = blocks * width
    pair = 2 if blocks % 2 == 0 else 1
    flops = 4 * keys * keys * part_count * HD
    return staged(
        functools.partial(attend_kernel, part_count),
        [own, *others],
        [
            shaped((blocks, HD, width), F32),
            shaped((tp_size, blocks, HD, width), BF),
            shaped((blocks, 1, width), F32),
        ],
        "attend",
        [
            pltpu.VMEM((part_count, keys, HD), BF),
            pltpu.VMEM((part_count, HD, keys), BF),
            pltpu.VMEM((part_count, keys, pair * width), F32),
        ],
        cost=work(flops, 4 * own.size, keys * keys * part_count),
    )


def turn_back(values, cosine, sine):
    first, second = values[:HALF], values[HALF:]
    return jnp.concatenate([first * cosine + second * sine, second * cosine - first * sine], axis=0)


def attend_back_kernel(part_count, own_ref, *refs):
    others = refs[: part_count - 1]
    refs = refs[part_count - 1 :]
    grad_ref, out_ref, lse_ref, cos_ref, sin_ref = refs[:5]
    dq_ref, dkv_ref = refs[5:7]
    dkv_others = refs[7 : 6 + part_count]
    k_scr, v_scr, kt_scr, dk_scr, dv_scr = refs[6 + part_count :]
    blocks, width = own_ref.shape[0], own_ref.shape[2]
    parts = [(r, HD) for r in (own_ref, *others)]
    load_rows(parts, 0, k_scr)
    load_rows(parts, HD, v_scr)
    load_columns(parts, 0, kt_scr)
    dk_scr[...] = jnp.zeros_like(dk_scr)
    dv_scr[...] = jnp.zeros_like(dv_scr)
    pair = 2 if blocks % 2 == 0 else 1

    @pl.loop(0, blocks // pair, unroll=True)
    def query_block(i):
        span = range(pair)
        qt = jnp.concatenate([own_ref[pair * i + b, :HD, :] for b in span], axis=1)
        gt = jnp.concatenate(
            [
                (grad_ref[0, pair * i + b].astype(F32) + grad_ref[1, pair * i + b].astype(F32)).astype(BF)
                for b in span
            ],
            axis=1,
        )
        ot = jnp.concatenate([out_ref[pair * i + b] for b in span], axis=1)
        lse = jnp.concatenate([lse_ref[pair * i + b] for b in span], axis=1)
        q, g = qt.T, gt.T
        delta = jnp.sum(gt.astype(F32) * ot, axis=0, keepdims=True)

        def one(j, dq):
            p = jnp.exp(nn(k_scr[j], qt) - lse)
            ds = (p * (nn(v_scr[j], gt) - delta)).astype(BF)
            dv_scr[j] += nn(p.astype(BF), g)
            dk_scr[j] += nn(ds, q)
            return dq + nn(kt_scr[j], ds)

        start = jnp.zeros((HD, pair * width), F32)
        dq = lax.fori_loop(0, part_count, one, start, unroll=part_count <= 2)
        for b in span:
            at = pair * i + b
            block = dq[:, b * width : (b + 1) * width] * (HD**-0.5)
            dq_ref[at] = turn_back(block, cos_ref[at], sin_ref[at]).astype(BF)

    for j, ref in enumerate((dkv_ref, *dkv_others)):
        for b in range(blocks):
            rows = slice(b * width, (b + 1) * width)
            ref[b, :HD, :] = dk_scr[j, rows, :].T
            ref[b, HD:, :] = dv_scr[j, rows, :].T


def attend_back(own, others, grad, attended, lse, cosine, sine):
    blocks, unused, width = own.shape
    part_count = 1 + len(others)
    keys = blocks * width
    flops = 10 * keys * keys * part_count * HD
    return staged(
        functools.partial(attend_back_kernel, part_count),
        [own, *others, grad, attended, lse, cosine, sine],
        [shaped((blocks, HD, width), BF)] + [shaped((blocks, 2 * HD, width), F32)] * part_count,
        "attend_back",
        [
            pltpu.VMEM((part_count, keys, HD), BF),
            pltpu.VMEM((part_count, keys, HD), BF),
            pltpu.VMEM((part_count, HD, keys), BF),
            pltpu.VMEM((part_count, keys, HD), F32),
            pltpu.VMEM((part_count, keys, HD), F32),
        ],
        cost=work(flops, 8 * own.size, keys * keys * part_count),
    )


def combine_kernel(count, dq_ref, *refs):
    terms, (cos_ref, sin_ref, out_ref) = refs[:count], refs[count:]
    for b in range(dq_ref.shape[0]):
        total = terms[0][b]
        for ref in terms[1:]:
            total = total + ref[b]
        out_ref[b, :HD] = dq_ref[b]
        out_ref[b, HD : 2 * HD] = turn_back(total[:HD], cos_ref[b], sin_ref[b]).astype(BF)
        out_ref[b, 2 * HD :] = total[HD:].astype(BF)


def combine(dq, terms, cosine, sine):
    blocks, unused, width = dq.shape
    return staged(
        functools.partial(combine_kernel, len(terms)),
        [dq, *terms, cosine, sine],
        [shaped((blocks, 3 * HD, width), BF)],
        "combine",
        cost=work(dq.size, 20 * dq.size),
    )[0]


def standardise(values):
    centred = values - jnp.mean(values, axis=-1, keepdims=True)
    spread = jnp.mean(centred * centred, axis=-1, keepdims=True)
    scale = lax.rsqrt(spread + NORM_EPS)
    return centred * scale, scale


def standardise_back(gradient, gain, normed, scale):
    y = gradient * gain
    along = jnp.mean(y * normed, axis=-1, keepdims=True)
    return scale * (y - jnp.mean(y, axis=-1, keepdims=True) - normed * along)


def project_kernel(hidden_ref, gain_ref, cos_ref, sin_ref, *refs):
    weights, (packed_ref, input_ref), waits = refs[:3], refs[3:5], refs[5:]
    normed, unused = standardise(hidden_ref[...].astype(F32))
    attn_input = (normed * gain_ref[...]).astype(BF)
    input_ref[...] = attn_input
    cosine, sine = cos_ref[...], sin_ref[...]
    for c in range(3):
        waits[c]()
        rows = nn(attn_input, weights[c][0]).T
        for h in range(packed_ref.shape[0]):
            block = rows[h * HD : (h + 1) * HD]
            if c < 2:
                first, second = block[:HALF], block[HALF:]
                block = jnp.concatenate(
                    [first * cosine - second * sine, second * cosine + first * sine], axis=0
                )
            if c == 0:
                block = block * (HD**-0.5)
            packed_ref[h, c * HD : (c + 1) * HD] = block.astype(BF)


def project(hidden, gain, cosine, sine, weights):
    width, model = hidden.shape
    heads = weights.shape[2] // HD
    hbm, vmem = pl.BlockSpec(memory_space=pltpu.HBM), pl.BlockSpec(memory_space=pltpu.VMEM)

    def kernel(h_ref, g_ref, c_ref, s_ref, w_ref, packed_ref, input_ref, h_scr, w_scr, sems):
        copies = [pltpu.make_async_copy(h_ref, h_scr, sems.at[3])]
        copies += [pltpu.make_async_copy(w_ref.at[c], w_scr.at[c], sems.at[c]) for c in range(3)]
        for copy in copies:
            copy.start()
        copies[0].wait()
        blocks = [w_scr.at[pl.ds(c, 1)] for c in range(3)]
        waits = [copy.wait for copy in copies[1:]]
        project_kernel(h_scr, g_ref, c_ref, s_ref, *blocks, packed_ref, input_ref, *waits)

    return pl.pallas_call(
        kernel,
        in_specs=[hbm, vmem, vmem, vmem, hbm],
        out_specs=(vmem, vmem),
        out_shape=(shaped((heads, 3 * HD, width), BF), shaped((width, model), BF)),
        scratch_shapes=[
            pltpu.VMEM(hidden.shape, BF),
            pltpu.VMEM(weights.shape, BF),
            pltpu.SemaphoreType.DMA((4,)),
        ],
        compiler_params=pltpu.CompilerParams(vmem_limit_bytes=GRANT),
        cost_estimate=work(2 * width * weights.size, 2 * weights.size),
        name="project",
    )(hidden, gain, cosine, sine, weights)


def unit_back_kernel(cot_ref, w_ref, out_ref):
    out_ref[...] = nt(cot_ref[...], w_ref[...])


def unit_back(cotangent, weights):
    width, units = cotangent.shape[0], weights.shape[0]
    return staged(
        unit_back_kernel,
        [cotangent, weights],
        [shaped((width, units), F32)],
        "unit_back",
        cost=work(2 * width * weights.size, 2 * weights.size),
    )[0]


def middle_kernel(
    tp_ref,
    attn_ref,
    hidden_ref,
    cot_ref,
    gain_ref,
    own_ref,
    other_ref,
    grad_act_ref,
    w_in_ref,
    middle_ref,
    mid_ref,
    act_ref,
    part_ref,
    heads_ref,
    wait_units,
):
    tp = tp_ref[0]
    attn_own = attn_ref[tp].T
    branch = nn(attn_own, own_ref[...]) + nn(attn_ref[1 - tp].T, other_ref[...])
    middle = hidden_ref[...].astype(F32) + branch
    middle_ref[...] = middle
    normed, scale = standardise(middle)
    gain = gain_ref[...]
    mlp_input = (normed * gain).astype(BF)
    model, inner = mlp_input.shape[1], attn_own.shape[1]
    first = model + inner
    mid_ref[:, :model] = mlp_input
    mid_ref[:, model:first] = attn_own
    wait_units()
    turned = mlp_input.T
    gate, up = nn(w_in_ref[0], turned).T, nn(w_in_ref[1], turned).T
    share = 0.5 * (1.0 + lax.erf(gate * (0.5**0.5)))
    slope = share + gate * jnp.exp(-0.5 * gate * gate) * ((2.0 * math.pi) ** -0.5)
    bent = gate * share
    grad_act = grad_act_ref[...]
    grad_gate = (slope * up * grad_act).astype(BF)
    grad_up = (bent * grad_act).astype(BF)
    units = grad_gate.shape[1]
    mid_ref[:, first : first + units] = grad_gate
    mid_ref[:, first + units : first + 2 * units] = grad_up
    activated = (bent * up).astype(BF)
    mid_ref[:, first + 2 * units : first + 3 * units] = activated
    act_ref[...] = activated
    last = first + 3 * units
    if last < mid_ref.shape[1]:
        mid_ref[:, last:] = jnp.zeros((activated.shape[0], mid_ref.shape[1] - last), BF)
    part = nn(grad_gate, w_in_ref[0]) + nn(grad_up, w_in_ref[1])
    part_ref[...] = part.astype(BF)
    grad = 0.5 * cot_ref[...].astype(F32) + standardise_back(part, gain, normed, scale)
    grad = grad.astype(BF)
    shape = heads_ref.shape[1:]
    heads_ref[tp] = nt(own_ref[...], grad).astype(BF).reshape(shape)
    heads_ref[1 - tp] = nt(other_ref[...], grad).astype(BF).reshape(shape)


def middle_part(tp, attn, hidden, cotangent, gain, own, other, grad_act, w_in):
    width, model = hidden.shape
    units = w_in.shape[1]
    inner = own.shape[0]
    return staged(
        middle_kernel,
        [tp, attn, hidden, cotangent, gain, own, other, grad_act, w_in],
        [
            shaped((width, model), F32),
            shaped((width, whole_lanes(model + inner + 3 * units)), BF),
            shaped((width, units), BF),
            shaped((width, model), BF),
            shaped((2, inner // HD, HD, width), BF),
        ],
        "middle_part",
        late=1,
        scalars=1,
        cost=work(8 * width * model * (units + inner), 2 * w_in.size, 2 * width * units),
    )


def project_back_kernel(grad_ref, w_ref, out_ref):
    heads = grad_ref.shape[0]
    total = jnp.zeros(out_ref.shape, F32)
    for c in range(3):
        rows = jnp.concatenate([grad_ref[h, c * HD : (c + 1) * HD, :] for h in range(heads)], axis=0)
        total += nt(rows.T, w_ref[c])
    out_ref[...] = total.astype(BF)


def project_back(grad, weights):
    width = grad.shape[2]
    return staged(
        project_back_kernel,
        [grad, weights],
        [shaped((width, weights.shape[1]), BF)],
        "project_back",
        cost=work(2 * width * weights.size, 2 * weights.size),
    )[0]


def picked(pick_ref, own_ref, other_ref):
    values = jnp.concatenate([own_ref[...], other_ref[...]], axis=0)
    return nt(pick_ref[...], values).astype(BF)


def head_weight_kernel(mine, ids_ref, grad_ref, *refs):
    rows, keep_ref, give_ref, total_scr = refs[:-3], *refs[-3:]
    count = len(rows)
    core = ids_ref[count]
    grads = jnp.concatenate([grad_ref[ids_ref[b]] for b in range(count)], axis=1)
    inputs = jnp.concatenate([ref[...] for ref in rows], axis=0)
    total_scr[...] = nn(grads, inputs).T
    for b in range(keep_ref.shape[0]):
        keep = pl.multiple_of((2 * b + core) * mine, mine)
        give = pl.multiple_of((2 * b + 1 - core) * mine, mine)
        keep_ref[b] = total_scr[pl.ds(keep, mine), :].astype(BF)
        give_ref[b] = total_scr[pl.ds(give, mine), :].astype(BF)


def head_weight(chips, ids, grad, rows):
    width, model = rows[0].shape
    columns = grad.shape[1]
    mine = model // (2 * chips)
    return staged(
        functools.partial(head_weight_kernel, mine),
        [ids, grad, *rows],
        [shaped((chips, mine, columns), BF)] * 2,
        "head_weight",
        [pltpu.VMEM((model, columns), F32)],
        scalars=1,
        cost=work(2 * len(rows) * rows[0].size * columns, 2 * len(rows) * rows[0].size),
    )


def mlp_weight_kernel(sizes, inner, units, pick_ref, *refs):
    cot_own, cot_other, own_ref, other_ref = refs[:4]
    outs = refs[4 : 4 + len(sizes)]
    total_scr, sems = refs[4 + len(sizes) :]
    model = cot_own.shape[1]
    first = model + inner
    cot_both = jnp.concatenate([cot_own[...], cot_other[...]], axis=0)
    both = jnp.concatenate([own_ref[...], other_ref[...]], axis=0)
    columns = both[:, first : first + 3 * units]
    copies, start, done, rows = [], 0, 0, total_scr.shape[0]
    for r, ref in enumerate(outs):
        while start + sizes[r] > done:
            cut = slice(done, done + rows // 2)
            in_rows = nt(pick_ref[cut], both[:, :model]).astype(BF)
            cot_rows = nt(pick_ref[cut], cot_both).astype(BF)
            total_scr[cut, : 2 * units] = nn(in_rows, columns[:, : 2 * units]).astype(BF)
            total_scr[cut, 2 * units : 3 * units] = nn(cot_rows, columns[:, 2 * units :]).astype(BF)
            if 3 * units < total_scr.shape[1]:
                rest = total_scr.shape[1] - 3 * units
                total_scr[cut, 3 * units :] = jnp.zeros((rows // 2, rest), BF)
            done += rows // 2
        copies.append(pltpu.make_async_copy(total_scr.at[pl.ds(start, sizes[r])], ref, sems.at[r]))
        copies[-1].start()
        start += sizes[r]
    for copy in copies:
        copy.wait()


def mlp_weight(sizes, inner, units, pick, cot_own, cot_other, own, other):
    rows, columns = sum(sizes), whole_lanes(3 * units)
    return staged(
        functools.partial(mlp_weight_kernel, sizes, inner, units),
        [pick, cot_own, cot_other, own, other],
        [shaped((size, columns), BF) for size in sizes],
        "mlp_weight",
        [pltpu.VMEM((rows, columns), BF), pltpu.SemaphoreType.DMA((len(sizes),))],
        cost=work(4 * rows * own.size, 2 * rows * columns + 8 * own.size),
        far=len(sizes),
    )


def out_weight_kernel(mine, pick_ref, own_ref, other_ref, attn_ref, attn_other_ref, *outs):
    both = jnp.concatenate([own_ref[...], other_ref[...]], axis=0)
    rows = nt(pick_ref[...], both).astype(BF)
    total = nn(rows, jnp.concatenate([attn_ref[...], attn_other_ref[...]], axis=0)).astype(BF)
    for r, ref in enumerate(outs):
        ref[...] = total[r * ref.shape[0] : (r + 1) * ref.shape[0]]


def out_weight(count, inner, pick, own, other, mid, mid_other, ring=()):
    rows, (width, model) = pick.shape[0], own.shape
    vmem, hbm = pl.BlockSpec(memory_space=pltpu.VMEM), pl.BlockSpec(memory_space=pl.ANY)

    size = 5 + len(ring)
    sent = len(ring) // 2

    def kernel(pick_ref, own_ref, other_ref, mid_ref, mid_other_ref, *refs):
        ring_refs, refs = refs[: len(ring)], refs[len(ring) :]
        outs, sent_refs, refs = refs[:count], refs[count : count + sent], refs[count + sent :]
        held, sems = refs[:size], refs[size]
        columns = pl.ds(model, inner)
        given = [pick_ref, own_ref, other_ref, mid_ref.at[:, columns], mid_other_ref.at[:, columns]]
        given += ring_refs
        copies = [pltpu.make_async_copy(g, h, sems.at[i]) for i, (g, h) in enumerate(zip(given, held))]
        for copy in copies:
            copy.start()
        for copy in copies[:5]:
            copy.wait()
        out_weight_kernel(rows // count, *held[:5], *outs)
        for copy in copies[5:]:
            copy.wait()
        for side in range(sent):
            block, got, out = held[5 + 2 * side], held[6 + 2 * side], sent_refs[side]
            wide, cut = block.shape[1], got.shape[0]
            part = slice(0, cut) if side == 0 else slice(cut, None)
            rest = slice(cut, None) if side == 0 else slice(0, cut)
            out[part, :wide] = (block[part].astype(F32) + got[...].astype(F32)).astype(BF)
            out[rest, :wide] = block[rest]
            out[:, wide:] = outs[count // 2 - 1 + 2 * side][...]

    return pl.pallas_call(
        kernel,
        in_specs=[hbm] * size,
        out_specs=[vmem] * (count + sent),
        out_shape=[shaped((rows // count, inner), BF)] * count
        + [shaped((b.shape[0], b.shape[1] + inner), BF) for b in ring[::2]],
        scratch_shapes=[
            pltpu.VMEM(pick.shape, BF),
            pltpu.VMEM(own.shape, BF),
            pltpu.VMEM(own.shape, BF),
            pltpu.VMEM((width, inner), BF),
            pltpu.VMEM((width, inner), BF),
            *[pltpu.VMEM(v.shape, BF) for v in ring],
            pltpu.SemaphoreType.DMA((size,)),
        ],
        compiler_params=pltpu.CompilerParams(vmem_limit_bytes=GRANT),
        cost_estimate=work(4 * rows * own.size, 8 * own.size),
        name="out_weight",
    )(pick, own, other, mid, mid_other, *ring)


def ring_add_kernel(count, *refs):
    outs, scratch, sems = refs[2 * count : 2 * count + 2], refs[2 * count + 2], refs[2 * count + 3]
    waits = refs[2 * count + 4 :]
    copies = []
    for side in range(2):
        given = refs[count * side : count * (side + 1)]
        for wait in waits[count * side : count * (side + 1)]:
            wait()
        block, got = given[:2]
        out = scratch.at[side]
        wide, rows = block.shape[1], got.shape[0]
        total = block[...].astype(F32)
        if rows == block.shape[0]:
            out[:, :wide] = (total + got[:, :wide].astype(F32)).astype(BF)
        elif side == 0:
            out[:rows, :wide] = (total[:rows] + got[...].astype(F32)).astype(BF)
            out[rows:, :wide] = block[rows:, :]
        else:
            out[:rows, :wide] = block[:rows, :]
            out[rows:, :wide] = (total[rows:] + got[...].astype(F32)).astype(BF)
        if count == 3 and got.shape[1] > wide:
            out[:, wide:] = (given[2][...].astype(F32) + got[:, wide:].astype(F32)).astype(BF)
        elif count == 3:
            out[:, wide:] = given[2][...]
        copies.append(pltpu.make_async_copy(out, outs[side], sems.at[side]))
        copies[-1].start()
    for copy in copies:
        copy.wait()


def ring_add(right, left):
    rows = right[0].shape[0]
    columns = right[0].shape[1] + (right[2].shape[1] if len(right) == 3 else 0)
    return staged(
        functools.partial(ring_add_kernel, len(right)),
        [*right, *left],
        [shaped((rows, columns), BF)] * 2,
        "ring_add",
        [pltpu.VMEM((2, rows, columns), BF), pltpu.SemaphoreType.DMA((2,))],
        late=2 * len(right),
        cost=work(4 * rows * columns, 12 * rows * columns),
        far=2,
    )


def finish_qkv_kernel(first_ref, blocks_ref, w_ref, out_ref, gain_ref, w_scr, sem):
    mine = out_ref.shape[1]
    rows = pl.ds(pl.multiple_of(first_ref[0], mine), mine)
    copy = pltpu.make_async_copy(w_ref.at[:, rows, :], w_scr, sem)
    copy.start()
    for c in range(3):
        for h in range(blocks_ref.shape[0]):
            cut = slice(h * HD, (h + 1) * HD)
            out_ref[c, :, cut] = blocks_ref[h, :, c * HD : (c + 1) * HD].astype(F32)
    copy.wait()
    total = jnp.zeros((mine, 1), F32)
    for c in range(3):
        total += jnp.sum(out_ref[c] * w_scr[c].astype(F32), axis=1, keepdims=True)
    gain_ref[...] = total


def finish_qkv(first, blocks, weights):
    heads, mine, unused = blocks.shape
    inner = weights.shape[2]
    vmem, hbm = pl.BlockSpec(memory_space=pltpu.VMEM), pl.BlockSpec(memory_space=pltpu.HBM)
    return pl.pallas_call(
        finish_qkv_kernel,
        in_specs=[pl.BlockSpec(memory_space=pltpu.SMEM), vmem, hbm],
        out_specs=(vmem, vmem),
        out_shape=(shaped((3, mine, inner), F32), shaped((mine, 1), F32)),
        scratch_shapes=[pltpu.VMEM((3, mine, inner), BF), pltpu.SemaphoreType.DMA],
        compiler_params=pltpu.CompilerParams(vmem_limit_bytes=GRANT),
        cost_estimate=work(2 * blocks.size, 10 * blocks.size),
        name="finish_qkv",
    )(first, blocks, weights)


def finish_mlp_kernel(own_ref, right_ref, left_ref, w_ref, gain_ref, inverse_ref, in_ref, out_ref, gains_ref):
    units = out_ref.shape[1]
    wide = own_ref.shape[1]
    total = own_ref[...].astype(F32) + right_ref[:, :wide].astype(F32) + left_ref[:, :wide].astype(F32)
    out_ref[...] = total[:, 2 * units : 3 * units]
    in_ref[:, 0, :] = total[:, :units]
    in_ref[:, 1, :] = total[:, units : 2 * units]
    term = jnp.sum(total[:, : 2 * units] * w_ref[...].astype(F32), axis=1, keepdims=True)
    mine = term.shape[0]
    inverse = inverse_ref[...]
    gains_ref[0:1] = jnp.broadcast_to(gain_ref[...], (mine, 128)).T[0:1] * inverse[0:1]
    gains_ref[1:2] = jnp.broadcast_to(term, (mine, 128)).T[0:1] * inverse[1:2]


def finish_mlp(units, own, right, left, rows, gain, inverse):
    mine = own.shape[0]
    return staged(
        finish_mlp_kernel,
        [own, right, left, rows, gain, inverse],
        [shaped((mine, 2, units), F32), shaped((mine, units), F32), shaped((2, mine), F32)],
        "finish_mlp",
        cost=work(8 * own.size, 14 * own.size),
    )


def middle_back_kernel(middle_ref, cot_ref, gain_ref, own_ref, other_ref, out_ref, low_ref):
    normed, scale = standardise(middle_ref[...])
    part = own_ref[...].astype(F32) + other_ref[...].astype(F32)
    grad = cot_ref[...].astype(F32) + standardise_back(part, gain_ref[...], normed, scale)
    out_ref[...] = grad
    low_ref[...] = grad.astype(BF)


def middle_back(middle, cotangent, gain, own, other):
    return staged(
        middle_back_kernel,
        [middle, cotangent, gain, own, other],
        [shaped(middle.shape, F32), shaped(middle.shape, BF)],
        "middle_back",
        cost=work(20 * middle.size, 16 * middle.size),
    )


def input_back_kernel(hidden_ref, gain_ref, own_ref, grad_ref, other_ref, out_ref):
    normed, scale = standardise(hidden_ref[...].astype(F32))
    part = own_ref[...].astype(F32) + other_ref[...].astype(F32)
    out_ref[...] = grad_ref[...] + standardise_back(part, gain_ref[...], normed, scale)


def input_back(hidden, gain, own, grad, other):
    return staged(
        input_back_kernel,
        [hidden, gain, own, grad, other],
        [shaped(grad.shape, F32)],
        "input_back",
        cost=work(20 * grad.size, 14 * grad.size),
    )[0]


def layer(ctx_size, tp_size, hidden_in, cotangent, gain_attn, gain_mlp, w_qkv, w_attn_out, w_in, w_mlp_out):
    width = hidden_in.shape[0]
    model = hidden_in.shape[1]
    inner = w_qkv.shape[2]
    heads = inner // HD
    units = w_in.shape[2]
    chips = ctx_size // 2
    copies = chips // heads
    mine = model // ctx_size
    me = lax.axis_index("ctx")
    core = me % 2

    same_core = [[2 * p + k for p in range(chips)] for k in range(2)]
    head_groups = [
        [2 * (heads * g + p) + k for p in range(heads)] for g in range(copies) for k in range(2)
    ]

    wide_groups = [
        [(2 * (heads * g + p) + k) * tp_size + t for t in range(tp_size) for p in range(heads)]
        for g in range(copies)
        for k in range(2)
    ]

    def exchange_wide(values):
        return lax.all_to_all(values, ("ctx", "tp"), 0, 0, axis_index_groups=wide_groups)

    def exchange(values):
        return lax.all_to_all(values, "ctx", 0, 0, axis_index_groups=head_groups)

    def swap_core(values):
        return lax.ppermute(values, "ctx", [(c, c ^ 1) for c in range(ctx_size)])

    def shift_keys(values, step):
        ring = 2 * copies
        pairs = []
        for c in range(ctx_size):
            g, p, k = c // (2 * heads), (c // 2) % heads, c % 2
            t = (2 * g + k + step) % ring
            pairs.append((c, 2 * (heads * (t // 2) + p) + t % 2))
        return lax.ppermute(values, "ctx", pairs)

    def swap_tp(values):
        return lax.ppermute(values, "tp", [(0, 1), (1, 0)])

    def add_tp(low):
        return low.astype(F32) + swap_tp(low).astype(F32)

    def after(values, *earlier):
        return lax.optimization_barrier((values, earlier))[0]

    def ring_chip(position):
        position = position % chips
        up = 2 * position
        return jnp.where(position < chips // 2, up, 2 * chips - 1 - up)

    ring = [2 * q if q < chips // 2 else 2 * chips - 1 - 2 * q for q in range(chips)]
    place = {p: q for q, p in enumerate(ring)}

    def turn(values, step):
        pairs = [
            (2 * p + k, 2 * ring[(place[p] + step) % chips] + k)
            for p in range(chips)
            for k in range(2)
        ]
        return lax.ppermute(values, "ctx", pairs)

    chip = me // 2
    position = jnp.where(chip % 2 == 0, chip // 2, chips - 1 - chip // 2)
    ringed = copies == 1

    def picker(chip_ids):
        wanted = ((2 * chip_ids + core) * mine)[:, None] + jnp.arange(mine)[None, :]
        return (wanted.reshape(-1, 1) == jnp.arange(model)[None, :]).astype(BF)

    def scatter(parts):
        flat = parts.reshape(chips, -1)
        summed = lax.psum_scatter(
            flat, "ctx", scatter_dimension=0, tiled=True, axis_index_groups=same_core
        )
        return summed.reshape((mine,) + parts.shape[1:]).astype(F32)

    group_first = (me // (2 * heads)) * (2 * heads)
    block_ids = group_first + 2 * jnp.arange(heads) + core
    inverse = ROPE_BASE ** (-(jnp.arange(HALF).astype(F32) * 2.0) / HD)

    def tables(ids):
        positions = (ids[:, None] * width + jnp.arange(width)[None, :]).astype(F32)
        angles = positions[:, None, :] * inverse[None, :, None]
        return jnp.cos(angles), jnp.sin(angles)

    tp = lax.axis_index("tp")
    tp_list = tp.astype(jnp.int32).reshape(1)
    cos_one, sin_one = tables(me[None])
    w_three = w_qkv.transpose(1, 0, 2)
    w_pair = w_in.transpose(1, 2, 0)

    packed, attn_input = project(hidden_in, gain_attn[None], cos_one[0], sin_one[0], w_three)
    own = exchange(packed)
    first = me * mine
    both_gains = after(jnp.stack([gain_attn, gain_mlp]), packed)
    gain_inverse = 1.0 / lax.dynamic_slice_in_dim(both_gains, first, mine, 1)
    w_out_other = swap_tp(w_attn_out)
    later_cot = after(cotangent, packed)
    cot_other = swap_core(later_cot)
    cos_all, sin_all = tables(after(block_ids, packed))
    order = after(jnp.arange(chips), packed)
    pick = picker(ring_chip(position + order) if ringed else order)
    gathered = [attn_input]
    right = left = after(attn_input, cos_all, sin_all, pick)

    def gather_step(step, *earlier):
        nonlocal right, left
        if 2 * step == chips:
            right = turn(after(right, *earlier), 1)
            gathered.append(right)
            return
        right, left = after((right, left), *earlier)
        right, left = turn(right, 1), turn(left, -1)
        gathered.extend([right, left])

    if ringed:
        gather_step(1)
    own = after(own, cos_all, sin_all, pick)
    others = [shift_keys(own, step) for step in range(1, 2 * copies)]
    attended, attended_low, lse = attend(tp_size, own, others)
    if ringed:
        attended_low = after(attended_low, right, left)
    attn_all = exchange_wide(attended_low.reshape(tp_size * heads, HD, width))
    grad_activated = unit_back(after(cotangent, attended_low), w_mlp_out)
    if ringed:
        gather_step(2, attended_low)
    rows_w_in = lax.dynamic_slice_in_dim(after(w_in, attended_low), me * mine, mine, 0)
    rows_w_in = rows_w_in.reshape(mine, 2 * units)
    attn_all = after(attn_all, rows_w_in, grad_activated, right, left).reshape(tp_size, inner, width)
    if ringed:
        gather_step(3, attn_all)
    middle, mid, activated_low, part_two, head_terms = middle_part(
        tp_list,
        attn_all,
        hidden_in,
        cotangent,
        gain_mlp[None],
        w_attn_out,
        w_out_other,
        grad_activated,
        w_pair,
    )
    if ringed:
        results = (middle, mid, activated_low, part_two, head_terms)
        middle, mid, activated_low, part_two, head_terms = after(results, right, left)
    grad_received = exchange_wide(head_terms.reshape(tp_size * heads, HD, width))

    half = chips // 2
    sizes = [mine] * half + [mine // 2, mine // 2] + [mine] * (half - 1) if ringed else [chips * mine]
    mid_other = swap_core(mid)
    parts_mlp = mlp_weight(sizes, inner, units, pick, cotangent, cot_other, mid, mid_other)
    if ringed:
        mlp_rights = parts_mlp[half::-1]
        mlp_lefts = parts_mlp[half + 1 :]
        got_right, got_left = turn(mlp_rights[0], 1), turn(mlp_lefts[0], -1)
    part_two_other = swap_tp(after(part_two, mid_other))
    later_two = after(part_two_other, parts_mlp)
    grad_middle, grad_middle_low = middle_back(middle, cotangent, gain_mlp[None], part_two, later_two)
    grad_received = after(grad_received, parts_mlp, right, left, grad_middle_low)
    if ringed:
        gather_step(4, parts_mlp)
    grad_received = grad_received.reshape(tp_size, heads, HD, width)
    dq, *grad_kv = attend_back(own, others, grad_received, attended, lse, cos_all, sin_all)

    low_other = swap_core(grad_middle_low)
    if ringed:
        grad_kv = after(grad_kv, got_right, got_left, right, low_other)
    terms = [grad_kv[0]]
    for step in range(1, 2 * copies):
        terms.append(shift_keys(grad_kv[step], -step))
    carried = ()
    if ringed:
        carried = (mlp_rights[1], after(got_right, dq), mlp_lefts[1], got_left)
    parts_out = out_weight(
        chips if ringed else 1,
        inner,
        pick,
        after(grad_middle_low, dq),
        low_other,
        mid,
        mid_other,
        carried,
    )
    if ringed:

        def ring_step(step, narrow, *earlier):
            nonlocal got_right, got_left
            rights = [mlp_rights[step], after(got_right, *earlier)]
            lefts = [mlp_lefts[step], got_left]
            if narrow:
                rights.append(parts_out[half - step])
                lefts.append(parts_out[half + step])
            sent = ring_add(rights, lefts)
            got_right, got_left = turn(sent[0], 1), turn(sent[1], -1)
            return sent

        parts_out, sent = parts_out[:chips], parts_out[chips:]
        got_right, got_left = turn(sent[0], 1), turn(sent[1], -1)
        terms[0] = after(terms[0], sent)
    grad_own = combine(dq, terms, cos_all, sin_all)
    grad_back = exchange(grad_own)
    if ringed:
        direct = turn(after(parts_out[half], sent), half)
        steps = [0]
        for step in range(1, half + 1):
            steps.extend([-step, step])
        ids = ring_chip(position + jnp.array(steps[:chips]))
        ids = jnp.concatenate([ids, core[None]]).astype(jnp.int32)
        keep_qkv, give_qkv = head_weight(chips, ids, grad_own, gathered)
        given_qkv = swap_core(give_qkv)
        sent = ring_step(2, True, keep_qkv)
        part_qkv = (keep_qkv.astype(F32) + given_qkv.astype(F32)).astype(BF)
        blocks_qkv = exchange(after(part_qkv, sent))
        grad_back = after(grad_back, part_qkv, sent)
    part_one = project_back(grad_back, w_three)
    part_one_other = swap_tp(part_one)
    if ringed:
        mlp_part = nn(after(activated_low, part_one), w_mlp_out).astype(BF)
        sent = ring_step(3, True, part_one_other, direct, mlp_part)
        output = (middle + add_tp(mlp_part)).astype(BF)
        part_one_other = after(part_one_other, sent)
        grad_input = input_back(hidden_in, gain_attn[None], part_one, grad_middle, part_one_other)
        grad_w_qkv, gain_one = finish_qkv(
            first.astype(jnp.int32).reshape(1), blocks_qkv, w_three
        )
        wide = mlp_rights[0].shape[1]
        grad_w_in, grad_w_mlp_out, gains = finish_mlp(
            units, parts_mlp[0], got_right, got_left, rows_w_in, gain_one, gain_inverse
        )
        grad_out = parts_out[0].astype(F32) + direct.astype(F32)
        grad_out = grad_out + got_right[:, wide:].astype(F32) + got_left[:, wide:].astype(F32)
        grad_w_attn_out = grad_out.T
        grad_w_qkv = grad_w_qkv.transpose(1, 0, 2)
    else:
        output = (middle + add_tp(nn(activated_low, w_mlp_out).astype(BF))).astype(BF)
        grad_input = input_back(hidden_in, gain_attn[None], part_one, grad_middle, part_one_other)
        grad_back = grad_back.reshape(heads, 3, HD, width)
        grad_back = grad_back.transpose(1, 0, 2, 3).reshape(3, inner, width)
        columns_in = jnp.concatenate([grad_back, swap_core(grad_back)], axis=2)
        rows_in = jnp.concatenate([attn_input, swap_core(attn_input)], axis=0)
        rows_in = nt(pick, rows_in).astype(BF)
        part_qkv = jnp.einsum("dt,cft->dcf", rows_in, columns_in, preferred_element_type=F32)
        grad_w_qkv = scatter(part_qkv.astype(BF))
        grad_mlp = scatter(parts_mlp[0])
        grad_w_in = grad_mlp[:, : 2 * units].reshape(mine, 2, units)
        grad_w_mlp_out = grad_mlp[:, 2 * units : 3 * units]
        grad_w_attn_out = scatter(parts_out[0]).T
        rows_w_qkv = lax.dynamic_slice_in_dim(w_qkv, first, mine, 0)
        gain_one = jnp.sum(rows_w_qkv.astype(F32) * grad_w_qkv, axis=(1, 2))
        gain_two = jnp.sum(rows_w_in.astype(F32) * grad_mlp[:, : 2 * units], axis=1)
        gains = jnp.stack([gain_one, gain_two]) * gain_inverse

    gains = gains + swap_tp(gains)
    return (
        output,
        grad_input,
        gains[0],
        gains[1],
        grad_w_qkv,
        grad_w_attn_out,
        grad_w_in,
        grad_w_mlp_out.T,
    )


def solution(mesh):
    in_specs = (
        P("ctx", None),
        P("ctx", None),
        P(),
        P(),
        P(None, None, "tp"),
        P("tp", None),
        P(None, None, "tp"),
        P("tp", None),
    )
    out_specs = (
        P("ctx", None),
        P("ctx", None),
        P("ctx"),
        P("ctx"),
        P("ctx", None, "tp"),
        P("tp", "ctx"),
        P("ctx", None, "tp"),
        P("tp", "ctx"),
    )
    body = functools.partial(layer, mesh.shape["ctx"], mesh.shape["tp"])
    return jax.shard_map(body, mesh=mesh, in_specs=in_specs, out_specs=out_specs, check_vma=False)
```
